32 devices in a mesh: dp: 8 (over y, x, core), tp: 4 (over z).
Axes of the slice: x: 2, y: 2, z: 4, core: 2. Of those that a mesh axis runs over, the one named last changes fastest.
Arguments:
- tokens: bfloat16 [4, 1024, 16, 768], P(None, 'tp', 'dp'), may hold values from -6 to 6
- lengths: int32 [4, 16], P(None, 'dp'), may hold values from 128 to 1024, as said below
- cotangent: bfloat16 [4, 1024, 16, 768], P(None, 'tp', 'dp'), may hold values from -6 to 6
- norm1_gain: bfloat16 [768], P('dp'), may hold values from 0.25 to 1.75
- norm1_bias: bfloat16 [768], P('dp'), may hold values from -1.5 to 1.5
- in_weight: bfloat16 [768, 3, 768], P('dp', None, 'tp'), may hold values from -0.21875 to 0.21875
- in_bias: bfloat16 [3, 768], P(None, 'dp'), may hold values from -4 to 4
- filter_base: bfloat16 [2, 2048, 768], P(None, 'dp', 'tp'), may hold values from -5 to 5
- filter_mod: bfloat16 [2, 2048, 768], P(None, 'dp', 'tp'), may hold values from -5 to 5
- out_weight: bfloat16 [768, 768], P('tp', 'dp'), may hold values from -0.4375 to 0.4375
- out_bias: bfloat16 [768], P('dp'), may hold values from -1.5 to 1.5
- norm2_gain: bfloat16 [768], P('dp'), may hold values from 0.25 to 1.75
- norm2_bias: bfloat16 [768], P('dp'), may hold values from -1.5 to 1.5
- gate_weight: bfloat16 [768, 3072], P(None, 'tp'), may hold values from -0.21875 to 0.21875
- up_weight: bfloat16 [768, 3072], P(None, 'tp'), may hold values from -0.21875 to 0.21875
- down_weight: bfloat16 [3072, 768], P('tp'), may hold values from -0.21875 to 0.21875
- down_bias: bfloat16 [768], P('dp'), may hold values from -1.5 to 1.5
Outputs:
- layer_out: bfloat16 [4, 1024, 16, 768], P(None, 'tp', 'dp')
- input_grad: bfloat16 [4, 1024, 16, 768], P(None, 'tp', 'dp')
- grad_norm1_gain: float32 [768], P(('dp', 'tp'))
- grad_norm1_bias: float32 [768], P(('dp', 'tp'))
- grad_in_weight: float32 [768, 3, 768], P('dp', None, 'tp')
- grad_in_bias: float32 [3, 768], P(None, ('dp', 'tp'))
- grad_filter_base: float32 [2, 2048, 768], P(None, 'dp', 'tp')
- grad_filter_mod: float32 [2, 2048, 768], P(None, 'dp', 'tp')
- grad_out_weight: float32 [768, 768], P('tp', 'dp')
- grad_out_bias: float32 [768], P(('dp', 'tp'))
- grad_norm2_gain: float32 [768], P(('dp', 'tp'))
- grad_norm2_bias: float32 [768], P(('dp', 'tp'))
- grad_gate_weight: float32 [768, 3072], P(None, 'tp')
- grad_up_weight: float32 [768, 3072], P(None, 'tp')
- grad_down_weight: float32 [3072, 768], P('tp')
- grad_down_bias: float32 [768], P(('dp', 'tp'))
The draws below stay inside these ranges and needn't reach their ends.
Inputs may be any that keep to these rules, and one draw needn't show every extreme that they name: `lengths`: in each micro-batch every group of 2 consecutive sequences holds one of exactly 1024 tokens, and one sequence has exactly 128.
All inputs are finite; a program needn't handle non-finite values.
Results may differ from the reference program's by a relative error of at most 0.023.
Values may be sent and summed in bfloat16 or wider, within the bound.
A program may use at most 384 MiB of HBM per device.

```python
import math
import jax
import jax.numpy as jnp
from jax import lax

D = 768
FF = 3072
SLOT = 1024
MIN_LEN = 128
SEQ_GRP = 2
MB = 4
SEQS = 16
N_TP = 4


def draw_lengths(key, part):
    key = jax.random.fold_in(key, 11)
    key_uniform, key_second, key_full, key_offset, key_group = jax.random.split(key, 5)
    groups = SEQS // SEQ_GRP
    spread = SLOT - MIN_LEN + 1
    uniform_part = jax.random.randint(key_uniform, (MB, groups, SEQ_GRP), 0, spread)
    second_draw = jax.random.randint(key_second, (MB, groups, SEQ_GRP), 0, 3 * spread)
    result = MIN_LEN + jnp.minimum(uniform_part, second_draw)
    full_slot = jax.random.randint(key_full, (MB, groups, 1), 0, SEQ_GRP)
    offset = jax.random.randint(key_offset, (MB, groups, 1), 1, SEQ_GRP)
    short_slot = (full_slot + offset) % SEQ_GRP
    short_group = jax.random.randint(key_group, (MB, 1, 1), 0, groups)
    column = jnp.arange(SEQ_GRP, dtype=jnp.int32)[None, None, :]
    group_index = jnp.arange(groups, dtype=jnp.int32)[None, :, None]
    result = jnp.where(column == full_slot, SLOT, result)
    result = jnp.where((column == short_slot) & (group_index == short_group), MIN_LEN, result)
    return result.reshape(MB, SEQS).astype(jnp.int32)


def shard_levels(key, dims, pieces, low, top_value):
    gain, own = 1.0, jax.random.fold_in(key, 6)
    for dim, shards_of in pieces:
        heights = jnp.exp(jax.random.uniform(jax.random.fold_in(own, dim), (shards_of,), jnp.float32, low / len(pieces), top_value / len(pieces)))
        gain = gain * jnp.repeat(heights, dims[dim] // shards_of).reshape([-1 if axis == dim else 1 for axis in range(len(dims))])
    return gain


def gaussian(key, extent, width, most, cuts=(), held_as=jnp.bfloat16):
    factor_of = shard_levels(key, extent, cuts, -0.22, 0.18) if cuts else 1.0
    drawn = jax.random.normal(key, extent, jnp.float32) * width * factor_of
    return jnp.minimum(jnp.maximum(drawn, -most), most).astype(held_as)


def setup_inputs(seed: int = 0) -> dict:
    key_list = jax.random.split(jax.random.key(seed), 18)
    return {
        "tokens": gaussian(key_list[0], (MB, SLOT, SEQS, D), 1.0, 6.0, ((1, 4), (2, 8))),
        "lengths": draw_lengths(jax.random.fold_in(key_list[17], 71), 0),
        "cotangent": gaussian(key_list[2], (MB, SLOT, SEQS, D), 1.0, 6.0, ((1, 4), (2, 8))),
        "norm1_gain": jnp.clip(1.0 + 0.15 * jax.random.normal(key_list[3], (D,), jnp.float32), 0.25, 1.75).astype(jnp.bfloat16),
        "norm1_bias": gaussian(key_list[4], (D,), 0.3, 1.5, ((0, 8),)),
        "in_weight": gaussian(key_list[5], (D, 3, D), D ** -0.5, 0.21875, ((0, 8), (2, 4))),
        "in_bias": gaussian(key_list[6], (3, D), 1.0, 4.0, ((1, 8),)),
        "filter_base": gaussian(key_list[7], (2, 2 * SLOT, D), 1.0, 5.0, ((1, 8), (2, 4))),
        "filter_mod": gaussian(key_list[8], (2, 2 * SLOT, D), 1.0, 5.0, ((1, 8), (2, 4))),
        "out_weight": gaussian(key_list[9], (D, D), (D // 4) ** -0.5, 0.4375, ((0, 4), (1, 8))),
        "out_bias": gaussian(key_list[10], (D,), 0.3, 1.5, ((0, 8),)),
        "norm2_gain": jnp.clip(1.0 + 0.15 * jax.random.normal(key_list[11], (D,), jnp.float32), 0.25, 1.75).astype(jnp.bfloat16),
        "norm2_bias": gaussian(key_list[12], (D,), 0.3, 1.5, ((0, 8),)),
        "gate_weight": gaussian(key_list[13], (D, FF), D ** -0.5, 0.21875, ((1, 4),)),
        "up_weight": gaussian(key_list[14], (D, FF), D ** -0.5, 0.21875, ((1, 4),)),
        "down_weight": gaussian(key_list[15], (FF, D), (FF // 4) ** -0.5, 0.21875, ((0, 4),)),
        "down_bias": gaussian(key_list[16], (D,), 0.3, 1.5, ((0, 8),)),
    }


@jax.custom_vjp
def low(v):
    return lax.optimization_barrier(v.astype(jnp.bfloat16)).astype(jnp.float32)

@jax.custom_vjp
def low_back(v):
    return v

def low_keep(v):
    return (low(v), None)

def low_pass(kept, grad):
    return (grad,)

def back_keep(v):
    return (v, None)

def back_low(kept, grad):
    return (low(grad),)
low.defvjp(low_keep, low_pass)
low_back.defvjp(back_keep, back_low)
EPSILON = 1e-05
HIGHEST = lax.Precision.HIGHEST

def layer_norm(inputs, weight_gain, weight_shift):
    centre = lax.optimization_barrier(jnp.mean(inputs, axis=-1, keepdims=True))
    centred = inputs - centre
    spread = lax.optimization_barrier(jnp.mean(centred * centred, axis=-1, keepdims=True))
    return centred * lax.rsqrt(spread + EPSILON) * weight_gain + weight_shift

def transform_table(slot_len):
    frequency = jnp.arange(2 * slot_len, dtype=jnp.int32)[:, None]
    position = jnp.arange(slot_len, dtype=jnp.int32)[None, :]
    angles = (frequency * position % (2 * slot_len)).astype(jnp.float32) * (math.pi / slot_len)
    return jnp.stack([jnp.cos(angles), -jnp.sin(angles)])

def forward(inputs, seq_lengths, transform_rows, norm1_gain, norm1_bias, in_weight, in_bias, filter_base, filter_mod, out_weight, out_bias, norm2_gain, norm2_bias, gate_weight, up_weight, down_weight, down_bias):
    seq_count = inputs.shape[0]
    slot_len = inputs.shape[1]
    model_width = inputs.shape[2]
    channels = model_width // N_TP
    validity = (jnp.arange(slot_len, dtype=jnp.int32)[None, :] < seq_lengths[:, None]).astype(jnp.float32)[:, :, None]
    normed = low(layer_norm(inputs, norm1_gain, norm1_bias))
    projected = low_back(jnp.einsum('btd,dge->btge', normed, in_weight, precision=HIGHEST) + in_bias)
    values = projected[:, :, 0]
    gating = projected[:, :, 1]
    condition = projected[:, :, 2]
    masked_values = low(values * validity)
    spectrum = low_back(jnp.einsum('rkt,btd->brkd', transform_rows, masked_values, precision=HIGHEST))
    mixing = jnp.tanh(lax.optimization_barrier(jnp.sum(condition * validity, axis=1)) / seq_lengths[:, None].astype(jnp.float32))
    filter_real = filter_base[0][None] + mixing[:, None, :] * filter_mod[0][None]
    filter_imag = filter_base[1][None] + mixing[:, None, :] * filter_mod[1][None]
    prod_real = filter_real * spectrum[:, 0] - filter_imag * spectrum[:, 1]
    prod_imag = filter_real * spectrum[:, 1] + filter_imag * spectrum[:, 0]
    product = low(jnp.stack([prod_real, prod_imag], axis=1))
    conv_out = low_back(jnp.einsum('rkt,brkd->btd', transform_rows, product, precision=HIGHEST) * (0.5 / slot_len))
    gated_values = low(conv_out * gating)
    mix_parts = low(jnp.einsum('btpc,pce->pbte', gated_values.reshape(seq_count, slot_len, N_TP, channels), out_weight.reshape(N_TP, channels, model_width), precision=HIGHEST))
    branch = low_back(lax.optimization_barrier(jnp.sum(mix_parts, axis=0)) + out_bias)
    middle = inputs + validity * branch
    normed_two = low(layer_norm(middle, norm2_gain, norm2_bias))
    gate_pre = low_back(jnp.einsum('btd,df->btf', normed_two, gate_weight, precision=HIGHEST))
    up_pre = low_back(jnp.einsum('btd,df->btf', normed_two, up_weight, precision=HIGHEST))
    hidden = low(jax.nn.gelu(gate_pre) * up_pre)
    hidden_blocks = hidden.reshape(seq_count, slot_len, N_TP, -1)
    down_blocks = down_weight.reshape(N_TP, -1, model_width)
    partial_sums = low(jnp.einsum('btpf,pfd->pbtd', hidden_blocks, down_blocks, precision=HIGHEST))
    feed_out = low_back(lax.optimization_barrier(jnp.sum(partial_sums, axis=0)) + down_bias)
    return middle + validity * feed_out

def reference(tokens, lengths, cotangent, norm1_gain, norm1_bias, in_weight, in_bias, filter_base, filter_mod, out_weight, out_bias, norm2_gain, norm2_bias, gate_weight, up_weight, down_weight, down_bias):
    transform_rows = low(transform_table(SLOT))
    weights = tuple((weight_arg.astype(jnp.float32) for weight_arg in (norm1_gain, norm1_bias, in_weight, in_bias, filter_base, filter_mod, out_weight, out_bias, norm2_gain, norm2_bias, gate_weight, up_weight, down_weight, down_bias)))
    per_block = math.gcd(SEQS, max(1, 4096 // SLOT))
    block_count = MB * SEQS // per_block
    seq_major = jnp.transpose(tokens.astype(jnp.float32), (0, 2, 1, 3))
    upstream_major = jnp.transpose(cotangent.astype(jnp.float32), (0, 2, 1, 3))
    token_blocks = seq_major.reshape(block_count, per_block, SLOT, D)
    length_blocks = lengths.reshape(block_count, per_block).astype(jnp.int32)
    upstream_blocks = upstream_major.reshape(block_count, per_block, SLOT, D)

    def one_block(totals, block):
        block_tokens, block_lengths, block_upstream = block

        def forward_block(inputs, *params):
            return forward(inputs, block_lengths, transform_rows, *params)
        result, pull_back = jax.vjp(forward_block, block_tokens, *weights)
        gradients = pull_back(block_upstream)
        totals = tuple((running + fresh for running, fresh in zip(totals, gradients[1:])))
        return (totals, (result.astype(jnp.bfloat16), gradients[0].astype(jnp.bfloat16)))
    zero_totals = tuple((jnp.zeros_like(weight_arg) for weight_arg in weights))
    totals, (results, input_grads) = lax.scan(one_block, zero_totals, (token_blocks, length_blocks, upstream_blocks))
    layer_out = jnp.transpose(results.reshape(MB, SEQS, SLOT, D), (0, 2, 1, 3))
    input_grad = jnp.transpose(input_grads.reshape(MB, SEQS, SLOT, D), (0, 2, 1, 3))
    return (layer_out, input_grad, totals[0], totals[1], totals[2], totals[3], totals[4], totals[5], totals[6], totals[7], totals[8], totals[9], totals[10], totals[11], totals[12], totals[13])
```

```python
import functools
import math

import jax
import jax.numpy as jnp
import numpy as np
from jax import lax
from jax.experimental import pallas as pl
from jax.experimental.pallas import tpu as pltpu
from jax.sharding import PartitionSpec as P

EPSILON = 1e-05
BF = jnp.bfloat16
F32 = jnp.float32
GELU_A = math.sqrt(2.0 / math.pi)
GELU_B = 0.044715


def packed_table(slot_len):
    frequency = np.arange(slot_len, dtype=np.int64)[:, None]
    position = np.arange(slot_len, dtype=np.int64)[None, :]
    angles = (frequency * position % (2 * slot_len)).astype(np.float32) * np.float32(math.pi / slot_len)
    top = np.cos(angles)
    low = -np.sin(angles)
    low[0] = 1.0 - 2.0 * (np.arange(slot_len) % 2)
    return np.concatenate([top, low]).astype(np.float32).astype(jnp.bfloat16)


def shift(x, axis, step):
    n = lax.axis_size(axis)
    return lax.ppermute(x, axis, [(i, (i + step) % n) for i in range(n)])


def exchange(pieces, place, n):
    out = [(place, lax.dynamic_index_in_dim(pieces, place, 0, keepdims=False))]
    for step in range(1, n):
        block = lax.dynamic_index_in_dim(pieces, (place + step) % n, 0, keepdims=False)
        out.append(((place + n - step) % n, shift(block, "tp", step)))
    return out


def mm(a, b):
    return lax.dot_general(a, b, (((1,), (0,)), ((), ())), preferred_element_type=F32)


def mm_nt(a, b):
    return lax.dot_general(a, b, (((1,), (1,)), ((), ())), preferred_element_type=F32)


def mm_tn(a, b):
    return lax.dot_general(a, b, (((0,), (0,)), ((), ())), preferred_element_type=F32)


def mean_of(v):
    return jnp.sum(v, axis=-1, keepdims=True) * (1.0 / v.shape[-1])


def standardize(v):
    centred = v - mean_of(v)
    inverse = lax.rsqrt(mean_of(centred * centred) + EPSILON)
    return centred * inverse, inverse


def norm_back(e, gain, s, q):
    eg = e * gain
    return q * (eg - mean_of(eg) - s * mean_of(eg * s))


def gelu_parts(v):
    square = v * v
    th = jnp.tanh(v * (GELU_A + (GELU_A * GELU_B) * square))
    rise = 0.5 + 0.5 * th
    act = v * rise
    slope = rise + act * (1.0 - th) * (GELU_A + (3.0 * GELU_A * GELU_B) * square)
    return act, slope


def live(rows, first, count):
    at = lax.broadcasted_iota(jnp.int32, (rows, 1), 0) + first
    return jnp.where(at < count, 1.0, 0.0)


def joined(ref):
    v = ref[...]
    return v.reshape(-1, v.shape[-1])


def two_part_dot(a, b, dims):
    high = a.astype(BF)
    low = (a - high.astype(F32)).astype(BF)
    return lax.dot_general(high, b, (dims, ((), ())), preferred_element_type=F32) + lax.dot_general(
        low, b, (dims, ((), ())), preferred_element_type=F32
    )


def top_row(v, rows=8):
    r = lax.broadcasted_iota(jnp.int32, (rows, v.shape[1]), 0)
    return jnp.where(r == 0, jnp.broadcast_to(v, (rows, v.shape[1])), 0.0)


def project_kernel(tile, lens, x, wv, wg, wc, vec, n1, values, gating, nsum, mixing):
    s, t = pl.program_id(0), pl.program_id(1)
    count = lens[s]
    valid = live(tile, t * tile, count)
    std, _ = standardize(x[0].astype(F32))
    normed = (std * vec[0:1] + vec[1:2]).astype(BF)
    n1[0] = normed
    values[0] = ((mm(normed, joined(wv)) + vec[6:7]) * valid).astype(BF)
    gating[0] = (mm(normed, joined(wg)) + vec[7:8]).astype(BF)
    part = top_row(jnp.sum(normed.astype(F32) * valid, axis=0, keepdims=True))

    @pl.when(t == 0)
    def _():
        nsum[0] = part

    @pl.when(t > 0)
    def _():
        nsum[0] += part

    @pl.when(t == pl.num_programs(1) - 1)
    def _():
        length = count.astype(F32)
        cond = two_part_dot(nsum[0], joined(wc), ((1,), (0,))) + length * vec[8:9]
        mixing[0] = jnp.tanh(cond / length)


def filters_of(refs, slots, mix):
    base_r, base_i, mod_r, mod_i = [jnp.concatenate([ref[j] for j in slots]).astype(F32) for ref in refs]
    return base_r + mix * mod_r, base_i + mix * mod_i, mod_r, mod_i


def spectral_kernel(slots, scale, values, gating, mixing, table, table_t, f0, f1, f2, f3, spec, conv, gated):
    v = mm(table[...], values[0])
    n = v.shape[0] // 2
    spec[0] = v.astype(BF)
    sr, si = v[:n], v[n:]
    fr, fi, _, _ = filters_of((f0, f1, f2, f3), slots, mixing[0, 0:1])
    edge = lax.broadcasted_iota(jnp.int32, (n, 1), 0) == 0
    fr2 = jnp.where(edge, fi, fr)
    fi = jnp.where(edge, 0.0, fi)
    prod = jnp.concatenate([(fr * sr - fi * si).astype(BF), (fr2 * si + fi * sr).astype(BF)])
    out = mm(table_t[...], prod) * scale
    conv[0] = out.astype(BF)
    gated[0] = (out * gating[0].astype(F32)).astype(BF)


def feed_kernel(tile, n_tp, lens, x, gated, w_out, wg, wu, wd, vec, middle, n2, act, side, hidden, out):
    s, t = pl.program_id(0), pl.program_id(1)
    valid = live(tile, t * tile, lens[s])
    mid = x[0].astype(F32) + valid * (mm_nt(gated[0], joined(w_out)) + vec[4:5])
    middle[0] = mid
    std, _ = standardize(mid)
    normed = (std * vec[2:3] + vec[3:4]).astype(BF)
    n2[0] = normed
    feed = jnp.zeros(mid.shape, F32)
    for p in range(n_tp):
        gate = mm(normed, joined(wg.at[:, p]))
        up = mm(normed, joined(wu.at[:, p]))
        a, slope = gelu_parts(gate)
        act[0, p] = a.astype(BF)
        side[0, p] = (up * slope).astype(BF)
        h = (a * up).astype(BF)
        hidden[0, p] = h
        feed += mm(h, joined(wd.at[:, p]))
    out[0] = (mid + valid * (feed + vec[5:6])).astype(BF)


def feed_back_kernel(tile, tiles, lens, cot, n2, act, side, hidden, wg, wu, wd, e_out, d_gate, d_up, d_down, e_acc, acc_g, acc_u, acc_d):
    p, u = pl.program_id(0), pl.program_id(1)
    last = pl.num_programs(1) - 1
    valid = live(tile, lax.rem(u, tiles) * tile, lens[u // tiles])
    fg = (cot[0].astype(F32) * valid).astype(BF)
    hg = mm_nt(fg, joined(wd.at[:, 0]))
    gg = (hg * side[0, 0].astype(F32)).astype(BF)
    ug = (hg * act[0, 0].astype(F32)).astype(BF)
    part = mm_nt(gg, joined(wg.at[:, 0])) + mm_nt(ug, joined(wu.at[:, 0]))

    @pl.when(p == 0)
    def _():
        e_acc[u] = part

    @pl.when(p > 0)
    def _():
        e_acc[u] += part

    e_out[0] = e_acc[u]
    normed = n2[0]
    parts = (mm_tn(normed, gg), mm_tn(normed, ug), mm_tn(hidden[0, 0], fg))

    @pl.when(u == 0)
    def _():
        for acc, v in zip((acc_g, acc_u, acc_d), parts):
            acc[...] = v

    @pl.when(u > 0)
    def _():
        for acc, v in zip((acc_g, acc_u, acc_d), parts):
            acc[...] += v

    @pl.when(u == last)
    def _():
        for acc, out in zip((acc_g, acc_u, acc_d), (d_gate, d_up, d_down)):
            out[:, 0] = acc[...].astype(BF).reshape(out.shape[0], out.shape[2], out.shape[3])


def branch_back_kernel(tile, lens, e, middle, cot, gated, gating, conv, w_out, vec, mg_out, cg, gtg, d_out, sums, acc):
    s, t = pl.program_id(0), pl.program_id(1)
    begin = (s == 0) & (t == 0)
    end = (s == pl.num_programs(0) - 1) & (t == pl.num_programs(1) - 1)
    valid = live(tile, t * tile, lens[s])
    up = cot[0].astype(F32)
    fg = (up * valid).astype(BF).astype(F32)
    std, inverse = standardize(middle[0])
    grad = e[0]
    mg = up + norm_back(grad, vec[2:3], std, inverse)
    mg_out[0] = mg
    bgr = (mg * valid).astype(BF)
    ggr = mm(bgr, joined(w_out))
    cg[0] = (ggr * gating[0].astype(F32)).astype(BF)
    gtg[0] = (ggr * conv[0].astype(F32)).astype(BF)
    part = mm_tn(bgr, gated[0])
    rows = [grad * std, grad, bgr.astype(F32), fg]
    rows = [jnp.sum(r, axis=0, keepdims=True) for r in rows]

    @pl.when(begin)
    def _():
        acc[...] = part
        sums[...] = jnp.zeros(sums.shape, F32)

    @pl.when(jnp.logical_not(begin))
    def _():
        acc[...] += part

    for i, r in enumerate(rows):
        sums[i : i + 1] += r

    @pl.when(end)
    def _():
        d_out[...] = acc[...].astype(BF).reshape(d_out.shape)


def spectral_back_kernel(slots, scale, lens, cg, spec, mixing, table, table_t, f0, f1, f2, f3, vg, fgrad, cgv, acc):
    s = pl.program_id(1)
    count = lens[s]
    v = mm(table[...], cg[0]) * scale
    n = v.shape[0] // 2
    pr, pi = v[:n], v[n:]
    mix = mixing[0, 0:1]
    fr, fi, mod_r, mod_i = filters_of((f0, f1, f2, f3), slots, mix)
    edge = lax.broadcasted_iota(jnp.int32, (n, 1), 0) == 0
    fr2 = jnp.where(edge, fi, fr)
    fi = jnp.where(edge, 0.0, fi)
    sg = jnp.concatenate([(fr * pr + fi * pi).astype(BF), (fr2 * pi - fi * pr).astype(BF)])
    sr, si = spec[0, :n].astype(F32), spec[0, n:].astype(F32)
    both = pi * si
    dr = pr * sr + jnp.where(edge, 0.0, both)
    di = jnp.where(edge, both, pi * sr - pr * si)
    mixg = jnp.sum(mod_r * dr + mod_i * di, axis=0, keepdims=True)
    step = mixg * (1.0 - mix * mix) / count.astype(F32)
    cgv[0] = top_row(step.astype(BF).astype(F32))
    vg[0] = (mm(table_t[...], sg) * live(n, 0, count)).astype(BF)
    parts = (dr, di, mix * dr, mix * di)

    @pl.when(s == 0)
    def _():
        for i, part in enumerate(parts):
            acc[i] = part

    @pl.when(s > 0)
    def _():
        for i, part in enumerate(parts):
            acc[i] += part

    @pl.when(s == pl.num_programs(1) - 1)
    def _():
        size = n // len(slots)
        for j in range(len(slots)):
            k = slots.index(j)
            for i in range(4):
                fgrad[j, pl.ds(i * size, size)] = acc[i, pl.ds(k * size, size)].astype(BF)


def input_back_kernel(tile, lens, vg, gtg, n1, x, mg, nsum, cgv, wv, wg, wc, d_out, sums_in, vec, ig, d_in, sums, acc_v, acc_g, acc_c):
    s, t = pl.program_id(0), pl.program_id(1)
    begin = (s == 0) & (t == 0)
    end = (s == pl.num_programs(0) - 1) & (t == pl.num_programs(1) - 1)
    count = lens[s]
    valid = live(tile, t * tile, count)
    cvec = mm_nt(cgv[0].astype(BF), joined(wc))[0:1]
    vgb, gtb = vg[0], gtg[0]
    e = mm_nt(vgb, joined(wv)) + mm_nt(gtb, joined(wg)) + valid * cvec
    std, inverse = standardize(x[0].astype(F32))
    ig[0] = (mg[0] + norm_back(e, vec[0:1], std, inverse)).astype(BF)
    normed = n1[0]
    part_v, part_g = mm_tn(normed, vgb), mm_tn(normed, gtb)
    rows = [e * std, e, vgb.astype(F32), gtb.astype(F32)]
    rows = [jnp.sum(r, axis=0, keepdims=True) for r in rows]

    @pl.when(begin)
    def _():
        acc_v[...] = part_v
        acc_g[...] = part_g
        acc_c[...] = jnp.zeros(acc_c.shape, F32)
        sums[...] = jnp.zeros(sums.shape, F32)
        sums[2:6] = sums_in[0:4]

    @pl.when(jnp.logical_not(begin))
    def _():
        acc_v[...] += part_v
        acc_g[...] += part_g

    for i, r in zip((0, 1, 6, 7), rows):
        sums[i : i + 1] += r

    @pl.when(t == 0)
    def _():
        acc_c[...] += two_part_dot(nsum[0], cgv[0].astype(BF), ((0,), (0,)))
        sums[8:9] += cgv[0, 0:1] * count.astype(F32)

    @pl.when(end)
    def _():
        r = d_out.shape[1]
        shape = (d_in.shape[0], r, d_in.shape[2])
        for i, acc in enumerate((acc_v, acc_g, acc_c)):
            d_in[:, i * r : (i + 1) * r] = acc[...].astype(BF).reshape(shape)
        d_in[:, 3 * r :] = d_out[...]


def call(kernel, grid, lens, ins, in_specs, outs, out_specs, scratch, flops, name, limit=56):
    spec = pltpu.PrefetchScalarGridSpec(
        num_scalar_prefetch=1, grid=grid, in_specs=in_specs, out_specs=out_specs, scratch_shapes=scratch
    )
    moved = sum(math.prod(v.shape) * v.dtype.itemsize for v in list(ins) + list(outs))
    return pl.pallas_call(
        kernel,
        grid_spec=spec,
        out_shape=tuple(outs),
        compiler_params=pltpu.CompilerParams(
            dimension_semantics=("arbitrary",) * len(grid), vmem_limit_bytes=limit * 1024 * 1024
        ),
        cost_estimate=pl.CostEstimate(flops=int(flops), bytes_accessed=int(moved), transcendentals=0),
        name=name,
    )(lens, *ins)


def once(block, index):
    return pl.BlockSpec(block, lambda *_: index, pipeline_mode=pl.Buffered(1))


def shape_of(shape, dtype):
    return jax.ShapeDtypeStruct(shape, dtype)


def project(x, lens, aw, vec):
    own, n, width = x.shape
    tile = min(512, n)
    nd, r = aw.shape[0], width // aw.shape[0]
    tok = pl.BlockSpec((1, tile, width), lambda s, t, *_: (s, t, 0))
    one = pl.BlockSpec((1, 8, width), lambda s, t, *_: (s, 0, 0))
    weights = [once((nd, r, width), (0, g, 0)) for g in range(3)]
    sd = shape_of(x.shape, BF)
    row = shape_of((own, 8, width), F32)
    return call(
        functools.partial(project_kernel, tile),
        (own, n // tile),
        lens,
        [x, aw, aw, aw, vec],
        [tok] + weights + [once(vec.shape, (0, 0))],
        [sd, sd, sd, row, row],
        (tok, tok, tok, one, one),
        [],
        4 * own * n * width * width,
        "project",
    )


def filter_specs(fw, n_dp, rows, cb, first):
    return [
        pl.BlockSpec((n_dp, rows, cb), lambda *g, i=i: (0, first + i, g[0])) for i in range(4)
    ]


def spectral(values, gating, mixing, lens, table, table_t, fw, first, rows, slots, scale):
    own, n, width = values.shape
    cb = min(256, width)
    n_dp = fw.shape[0]
    tok = pl.BlockSpec((1, n, cb), lambda c, s, *_: (s, 0, c))
    both = pl.BlockSpec((1, 2 * n, cb), lambda c, s, *_: (s, 0, c))
    one = pl.BlockSpec((1, 8, cb), lambda c, s, *_: (s, 0, c))

    def kernel(lens, *refs):
        spectral_kernel(slots, scale, *refs)

    return call(
        kernel,
        (width // cb, own),
        lens,
        [values, gating, mixing, table, table_t] + [fw] * 4,
        [tok, tok, one, once(table.shape, (0, 0)), once(table_t.shape, (0, 0))] + filter_specs(fw, n_dp, rows, cb, first),
        [shape_of((own, 2 * n, width), BF), shape_of(values.shape, BF), shape_of(values.shape, BF)],
        (both, tok, tok),
        [],
        8 * own * n * n * width,
        "spectral",
    )


def feed(x, gated, lens, aw, ffw, vec):
    own, n, width = x.shape
    tile = min(512, n)
    nd, n_tp, _, hid = ffw[0].shape
    r = width // aw.shape[0]
    tok = pl.BlockSpec((1, tile, width), lambda s, t, *_: (s, t, 0))
    wide = pl.BlockSpec((1, n_tp, tile, hid), lambda s, t, *_: (s, 0, t, 0))
    ws = [once(shape, (0, 0, at, 0)) for _, shape, at in ffw[1]]
    big = shape_of((own, n_tp, n, hid), BF)
    return call(
        functools.partial(feed_kernel, tile, n_tp),
        (own, n // tile),
        lens,
        [x, gated, aw] + [w for w, _, _ in ffw[1]] + [vec],
        [tok, tok, once((aw.shape[0], r, width), (0, 3, 0))] + ws + [once(vec.shape, (0, 0))],
        [shape_of(x.shape, F32), shape_of(x.shape, BF), big, big, big, shape_of(x.shape, BF)],
        (tok, tok, wide, wide, wide, tok),
        [],
        2 * own * n * width * (width + 3 * n_tp * hid),
        "feed",
        limit=60,
    )


def feed_back(cot, n2, act, side, hidden, lens, ffw):
    own, n, width = cot.shape
    n_tp, hid = act.shape[1], act.shape[3]
    tile = min(512, n)
    tiles = n // tile
    tok = pl.BlockSpec((1, tile, width), lambda p, u, *_: (u // tiles, lax.rem(u, tiles), 0))
    wide = pl.BlockSpec((1, 1, tile, hid), lambda p, u, *_: (u // tiles, p, lax.rem(u, tiles), 0))
    ws = [
        pl.BlockSpec((shape[0], 1) + shape[2:], lambda p, u, *_, at=at: (0, p, at, 0)) for _, shape, at in ffw[1]
    ]
    d_specs = [pl.BlockSpec((shape[0], 1) + shape[2:], lambda p, u, *_: (0, p, 0, 0)) for _, shape, _ in ffw[1]]
    d_shapes = [shape_of(shape, BF) for _, shape, _ in ffw[1]]
    final = n_tp - 1
    e_spec = pl.BlockSpec(
        (1, tile, width),
        lambda p, u, *_: (jnp.where(p == final, u // tiles, 0), jnp.where(p == final, lax.rem(u, tiles), 0), 0),
    )
    return call(
        functools.partial(feed_back_kernel, tile, tiles),
        (n_tp, own * tiles),
        lens,
        [cot, n2, act, side, hidden] + [w for w, _, _ in ffw[1]],
        [tok, tok, wide, wide, wide] + ws,
        [shape_of(cot.shape, F32)] + d_shapes,
        (e_spec, *d_specs),
        [
            pltpu.VMEM((own * tiles, tile, width), F32),
            pltpu.VMEM((width, hid), F32),
            pltpu.VMEM((width, hid), F32),
            pltpu.VMEM((hid, width), F32),
        ],
        12 * own * n * width * n_tp * hid,
        "feed_back",
        limit=60,
    )


def branch_back(e, middle, cot, gated, gating, conv, lens, aw, vec):
    own, n, width = cot.shape
    tile = min(512, n)
    nd, r = aw.shape[0], width // aw.shape[0]
    tok = pl.BlockSpec((1, tile, width), lambda s, t, *_: (s, t, 0))
    return call(
        functools.partial(branch_back_kernel, tile),
        (own, n // tile),
        lens,
        [e, middle, cot, gated, gating, conv, aw, vec],
        [tok] * 6 + [once((nd, r, width), (0, 3, 0)), once(vec.shape, (0, 0))],
        [
            shape_of(cot.shape, F32),
            shape_of(cot.shape, BF),
            shape_of(cot.shape, BF),
            shape_of((nd, r, width), BF),
            shape_of((8, width), F32),
        ],
        (tok, tok, tok, pl.BlockSpec((nd, r, width), lambda *_: (0, 0, 0)), pl.BlockSpec((8, width), lambda *_: (0, 0))),
        [pltpu.VMEM((width, width), F32)],
        4 * own * n * width * width,
        "branch_back",
    )


def spectral_back(cg, spec, mixing, lens, table, table_t, fw, first, rows, slots, scale):
    own, n, width = cg.shape
    cb = min(256, width)
    n_dp = fw.shape[0]
    tok = pl.BlockSpec((1, n, cb), lambda c, s, *_: (s, 0, c))
    both = pl.BlockSpec((1, 2 * n, cb), lambda c, s, *_: (s, 0, c))
    one = pl.BlockSpec((1, 8, cb), lambda c, s, *_: (s, 0, c))
    return call(
        functools.partial(spectral_back_kernel, slots, scale),
        (width // cb, own),
        lens,
        [cg, spec, mixing, table, table_t] + [fw] * 4,
        [tok, both, one, once(table.shape, (0, 0)), once(table_t.shape, (0, 0))] + filter_specs(fw, n_dp, rows, cb, first),
        [shape_of(cg.shape, BF), shape_of((n_dp, 4 * rows, width), BF), shape_of((own, 8, width), F32)],
        (tok, pl.BlockSpec((n_dp, 4 * rows, cb), lambda c, s, *_: (0, 0, c)), one),
        [pltpu.VMEM((4, n, cb), F32)],
        8 * own * n * n * width,
        "spectral_back",
    )


def input_back(vg, gtg, n1, x, mg, nsum, cgv, lens, aw, d_out, sums, vec):
    own, n, width = x.shape
    tile = min(512, n)
    nd, r = aw.shape[0], width // aw.shape[0]
    tok = pl.BlockSpec((1, tile, width), lambda s, t, *_: (s, t, 0))
    one = pl.BlockSpec((1, 8, width), lambda s, t, *_: (s, 0, 0))
    weights = [once((nd, r, width), (0, g, 0)) for g in range(3)]
    return call(
        functools.partial(input_back_kernel, tile),
        (own, n // tile),
        lens,
        [vg, gtg, n1, x, mg, nsum, cgv, aw, aw, aw, d_out, sums, vec],
        [tok] * 5 + [one] * 2 + weights + [once((nd, r, width), (0, 0, 0)), once((8, width), (0, 0)), once(vec.shape, (0, 0))],
        [shape_of(x.shape, BF), shape_of((nd, 4 * r, width), BF), shape_of((16, width), F32)],
        (tok, pl.BlockSpec((nd, 4 * r, width), lambda *_: (0, 0, 0)), pl.BlockSpec((16, width), lambda *_: (0, 0))),
        [pltpu.VMEM((width, width), F32)] * 3,
        8 * own * n * width * width,
        "input_back",
    )


MESH = pl.DeviceIdType.MESH


def flip(index, step):
    return index + step - 2 * step * ((index // step) % 2)


def bit_orders(n_dp):
    bits = [1 << b for b in range(1, (n_dp - 1).bit_length())]
    return bits, bits[::-1]


def greet(d, z, n_dp, n_tp):
    barrier = pltpu.get_barrier_semaphore()
    count = 0
    step = 1
    while step < n_dp:
        pl.semaphore_signal(barrier, inc=1, device_id=(flip(d, step), z), device_id_type=MESH)
        step *= 2
        count += 1
    for k in range(1, n_tp):
        pl.semaphore_signal(barrier, inc=1, device_id=(d, lax.rem(z + k, n_tp)), device_id_type=MESH)
        count += 1
    pl.semaphore_wait(barrier, count)


def remote(src, dst, send, recv, target):
    copy = pltpu.make_async_remote_copy(
        src_ref=src, dst_ref=dst, send_sem=send, recv_sem=recv, device_id=target, device_id_type=MESH
    )
    copy.start()
    return copy


class Spread:
    def __init__(self, part, order, d, z, send, recv):
        self.part, self.order, self.d, self.z = part, order, d, z
        self.send, self.recv = send, recv
        self.held, self.used, self.flying, self.stage = [d], 0, [], 0
        self.all = []

    def start(self):
        step = self.order[self.stage]
        target = (flip(self.d, step), self.z)
        self.flying = []
        for slot in self.held:
            ref = self.part(slot)
            self.flying.append(remote(ref, ref, self.send.at[self.used], self.recv.at[self.used], target))
            self.used += 1
        self.all += self.flying

    def wait(self):
        step = self.order[self.stage]
        for copy in self.flying:
            copy.wait_recv()
        self.held = self.held + [flip(slot, step) for slot in self.held]
        self.stage += 1

    def drain(self):
        for copy in self.all:
            copy.wait_send()


def chunk_of(rows):
    return next((c for c in (128, 96, 64, 48, 32, 16) if rows % c == 0), rows)


def add_rows(dst, src):
    rows = dst.shape[0]
    size = chunk_of(rows)

    @pl.loop(0, rows // size)
    def _(i):
        at = pl.ds(i * size, size)
        dst[at] = (dst[at].astype(F32) + src[at].astype(F32)).astype(BF)


def lane_place(rows, cols, offset):
    r = lax.broadcasted_iota(jnp.int32, (rows, cols), 0)
    c = lax.broadcasted_iota(jnp.int32, (rows, cols), 1)
    return jnp.where(c - r == offset, 1.0, 0.0).astype(BF)


def gather_kernel(
    n_dp, n_tp, cut, ff_in, a_in, vec_in, x_in, ff_out, a_out, x_out, a_z, a_nat, z_send, z_recv, s_send, s_recv, local
):
    d, z = lax.axis_index("dp"), lax.axis_index("tp")
    rows, ch = a_in.shape
    width = a_nat.shape[1]
    greet(d, z, n_dp, n_tp)
    own_ff = pltpu.make_async_copy(ff_in, ff_out.at[d, z], local.at[0])
    own_ff.start()
    own_a = pltpu.make_async_copy(a_in, a_z.at[z], local.at[1])
    own_a.start()
    za, zf = [], []
    for k in range(1, n_tp):
        target = (d, lax.rem(z + k, n_tp))
        za.append(remote(a_in, a_z.at[z], z_send.at[0, k - 1], z_recv.at[0, k - 1], target))
    for k in range(1, n_tp):
        target = (d, lax.rem(z + k, n_tp))
        zf.append(remote(ff_in, ff_out.at[d, z], z_send.at[1, k - 1], z_recv.at[1, k - 1], target))
    size = x_in.shape[2]
    here = pl.ds(z * size, size)
    own_x = pltpu.make_async_copy(x_in.at[z], x_out.at[:, here], local.at[3])
    own_x.start()
    zx = []
    for k in range(1, n_tp):
        peer = lax.rem(z + k, n_tp)
        zx.append(remote(x_in.at[peer], x_out.at[:, here], z_send.at[2, k - 1], z_recv.at[2, k - 1], (d, peer)))
    own_a.wait()
    for copy in za:
        copy.wait_recv()
    size = chunk_of(rows)

    @pl.loop(0, rows // size)
    def _(i):
        at = pl.ds(i * size, size)
        total = jnp.zeros((size, width), F32)
        for s in range(n_tp):
            total += jnp.dot(a_z[s, at], lane_place(ch, width, s * ch), preferred_element_type=F32)
        a_nat[at] = total.astype(BF)

    a_nat[rows:] = vec_in[...]
    put = pltpu.make_async_copy(a_nat, a_out.at[d], local.at[2])
    put.start()
    put.wait()
    first, second = bit_orders(n_dp)
    half_z = n_tp // 2
    total_rows = a_nat.shape[0]
    sa = [
        Spread(lambda s: a_out.at[s, pl.ds(0, cut)], first + [1], d, z, s_send.at[0], s_recv.at[0]),
        Spread(lambda s: a_out.at[s, pl.ds(cut, total_rows - cut)], second + [1], d, z, s_send.at[1], s_recv.at[1]),
    ]
    sf = [
        Spread(lambda s: ff_out.at[s, pl.ds(0, half_z)], first + [1], d, z, s_send.at[2], s_recv.at[2]),
        Spread(lambda s: ff_out.at[s, pl.ds(half_z, n_tp - half_z)], second + [1], d, z, s_send.at[3], s_recv.at[3]),
    ]
    for p in sa:
        p.start()
    own_ff.wait()
    for copy in zf:
        copy.wait_recv()
    for p in sf:
        p.start()
    for stage in range(len(first) + 1):
        for group in (sa, sf):
            for p in group:
                p.wait()
            if stage < len(first):
                for p in group:
                    p.start()
    for p in sa + sf:
        p.drain()
    own_x.wait()
    for copy in zx:
        copy.wait_recv()
    for copy in za + zf + zx:
        copy.wait_send()


def gather_weights(ff_in, a_in, vec_in, x_in, n_dp, n_tp):
    rows, ch = a_in.shape
    width = vec_in.shape[1]
    total = rows + vec_in.shape[0]
    cut = total // 2 // 16 * 16
    anyspace = pl.BlockSpec(memory_space=pl.ANY)
    vmem = pl.BlockSpec(memory_space=pltpu.VMEM)
    return pl.pallas_call(
        functools.partial(gather_kernel, n_dp, n_tp, cut),
        out_shape=(
            jax.ShapeDtypeStruct((n_dp, n_tp) + ff_in.shape, BF),
            jax.ShapeDtypeStruct((n_dp, total, width), BF),
            jax.ShapeDtypeStruct((x_in.shape[1], n_tp * x_in.shape[2], width), BF),
        ),
        in_specs=[anyspace, anyspace, vmem, anyspace],
        out_specs=(anyspace, anyspace, anyspace),
        scratch_shapes=[
            pltpu.VMEM((n_tp, rows, ch), BF),
            pltpu.VMEM((total, width), BF),
            pltpu.SemaphoreType.DMA((3, n_tp - 1)),
            pltpu.SemaphoreType.DMA((3, n_tp - 1)),
            pltpu.SemaphoreType.DMA((4, n_dp - 1)),
            pltpu.SemaphoreType.DMA((4, n_dp - 1)),
            pltpu.SemaphoreType.DMA((4,)),
        ],
        compiler_params=pltpu.CompilerParams(
            collective_id=0, has_side_effects=True, vmem_limit_bytes=48 * 1024 * 1024
        ),
        name="gather_weights",
    )(ff_in, a_in, vec_in, x_in)


def scatter_kernel(
    n_dp, n_tp, cut, g0, g1, g2, a0, a1, v_in, x_in, ff_out, a_out, v_out, x_out,
    ff_mine, a_mine, ff_core, a_core, ff_two, a_two, a_cols, ff_z, a_zbuf, ff_sum, v_got,
    load, core_send, core_recv, x_send, x_recv, z_send, z_recv, s_send, s_recv, v_send, v_recv, local,
):
    d, z = lax.axis_index("dp"), lax.axis_index("tp")
    width = a0.shape[2]
    rows = a0.shape[1] + a1.shape[1]
    ch = a_out.shape[1]
    vec = g0.shape[2]
    half = n_dp // 2
    half_z = n_tp // 2
    side = d % 2
    own = d // 2
    greet(d, z, n_dp, n_tp)
    v_out[...] = v_in[...]
    vs = []

    def v_start(i, target, sem):
        vs.append(remote(v_out, v_got.at[i], v_send.at[sem], v_recv.at[sem], target))

    def v_finish(i):
        vs[-1].wait()
        v_out[...] += v_got[i]

    other = (flip(d, 1), z)
    f_core, a_core_copies, f_load, a_load = [], [], [], []
    for i in range(half):
        for g, src in enumerate((g0, g1, g2)):
            f_core.append(
                remote(src.at[2 * i + 1 - side], ff_core.at[i, g], core_send.at[g, i], core_recv.at[g, i], other)
            )
            copy = pltpu.make_async_copy(src.at[2 * i + side], ff_mine.at[i, g], load.at[g, i])
            copy.start()
            f_load.append(copy)
    for i in range(half):
        at = 0
        for g, src in enumerate((a0, a1)):
            part = pl.ds(at, src.shape[1])
            at += src.shape[1]
            a_core_copies.append(
                remote(src.at[2 * i + 1 - side], a_core.at[i, part], core_send.at[3 + g, i], core_recv.at[3 + g, i], other)
            )
            copy = pltpu.make_async_copy(src.at[2 * i + side], a_mine.at[i, part], load.at[3 + g, i])
            copy.start()
            a_load.append(copy)
    v_start(0, other, 0)
    slot = x_out.shape[2]
    own_x = pltpu.make_async_copy(x_in.at[:, pl.ds(z * slot, slot)], x_out.at[z], local.at[1])
    own_x.start()
    zx = []
    for k in range(1, n_tp):
        peer = lax.rem(z + k, n_tp)
        zx.append(
            remote(x_in.at[:, pl.ds(peer * slot, slot)], x_out.at[z], z_send.at[3, k - 1], z_recv.at[3, k - 1], (d, peer))
        )

    first, second = bit_orders(n_dp)
    orders = ([s // 2 for s in first[::-1]], [s // 2 for s in second[::-1]])
    n_stage = len(orders[0])

    def entries(order, t):
        masks = [0]
        for step in order[t:]:
            masks = masks + [m + step for m in masks]
        return masks

    def at(mask):
        index = own
        step = 1
        while step < half:
            if mask & step:
                index = flip(index, step)
            step *= 2
        return index

    flying = {}
    base = {}
    all_x = []

    def begin(name, h, t, mine, two, part):
        step = orders[h][t]
        target = (flip(d, 2 * step), z)
        first_slot = base.get((name, h), 0)
        copies = []
        for j, m in enumerate(entries(orders[h], t + 1)):
            k = first_slot + j
            copies.append(
                (
                    m,
                    k,
                    remote(part(mine, at(m + step)), part(two, k), x_send.at[name, h, k], x_recv.at[name, h, k], target),
                )
            )
        base[name, h] = first_slot + len(copies)
        flying[name, h] = copies

    def finish(name, h, mine, two, part, add):
        for m, k, copy in flying[name, h]:
            copy.wait()
            add(part(mine, at(m)), part(two, k))

    def ff_part(h):
        lo, size = (0, half_z) if h == 0 else (half_z, n_tp - half_z)
        return lambda ref, e: ref.at[e, :, pl.ds(lo, size)]

    def a_part(h):
        lo, size = (0, cut) if h == 0 else (cut, rows - cut)
        return lambda ref, e: ref.at[e, pl.ds(lo, size)]

    def add_deep(dst, src):
        for g in range(dst.shape[0]):
            for s in range(dst.shape[1]):
                add_rows(dst.at[g, s], src.at[g, s])

    for i in range(half):
        for g in range(3):
            f_load[3 * i + g].wait()
            f_core[3 * i + g].wait_recv()
        add_deep(ff_mine.at[i], ff_core.at[i])
    for h in range(2):
        begin(0, h, 0, ff_mine, ff_two, ff_part(h))
    v_finish(0)
    for copy in a_load:
        copy.wait()
    for copy in a_core_copies:
        copy.wait_recv()
    for i in range(half):
        add_rows(a_mine.at[i], a_core.at[i])
    for i, step in enumerate(first):
        v_start(i + 1, (flip(d, step), z), i + 1)
        v_finish(i + 1)
    for t in range(n_stage):
        for h in range(2):
            finish(0, h, ff_mine, ff_two, ff_part(h), add_deep)
            if t + 1 < n_stage:
                begin(0, h, t + 1, ff_mine, ff_two, ff_part(h))
        if t == 0:
            for h in range(2):
                begin(1, h, 0, a_mine, a_two, a_part(h))
    zf, za, zv = [], [], []
    for k in range(1, n_tp):
        peer = lax.rem(z + k, n_tp)
        zf.append(remote(ff_mine.at[own, :, peer], ff_z.at[k - 1], z_send.at[0, k - 1], z_recv.at[0, k - 1], (d, peer)))
        zv.append(
            remote(v_out, v_got.at[n_stage + k], z_send.at[2, k - 1], z_recv.at[2, k - 1], (d, peer))
        )
    for t in range(n_stage):
        for h in range(2):
            finish(1, h, a_mine, a_two, a_part(h), add_rows)
            if t + 1 < n_stage:
                begin(1, h, t + 1, a_mine, a_two, a_part(h))
    size = chunk_of(rows)

    @pl.loop(0, rows // size)
    def _(i):
        here = pl.ds(i * size, size)
        block = a_mine[own, here]
        for s in range(n_tp):
            a_cols[s, here] = mm_nt(block, lane_place(ch, width, s * ch)).astype(BF)

    for k in range(1, n_tp):
        peer = lax.rem(z + k, n_tp)
        za.append(remote(a_cols.at[peer], a_zbuf.at[k - 1], z_send.at[1, k - 1], z_recv.at[1, k - 1], (d, peer)))
    for copy in zf:
        copy.wait_recv()
    f_size = chunk_of(vec)
    for g in range(3):

        @pl.loop(0, vec // f_size)
        def _(i):
            here = pl.ds(i * f_size, f_size)
            total = ff_mine[own, g, z, here].astype(F32)
            for k in range(1, n_tp):
                total += ff_z[k - 1, g, here].astype(F32)
            ff_sum[g, here] = total.astype(BF)

    put = pltpu.make_async_copy(ff_sum, ff_out.at[d], local.at[0])
    put.start()
    put.wait()
    one, two = bit_orders(n_dp)
    pieces = [(0, 0, vec, one), (1, 0, vec, two)]
    if vec % 32 == 0:
        pieces += [(2, 0, vec // 2, one), (2, vec // 2, vec // 2, two)]
    else:
        pieces += [(2, 0, vec, one)]
    sf = [
        Spread(lambda s, g=g, lo=lo, n=n: ff_out.at[s, g, pl.ds(lo, n)], order + [1], d, z, s_send.at[i], s_recv.at[i])
        for i, (g, lo, n, order) in enumerate(pieces)
    ]
    for p in sf:
        p.start()
    for stage in range(len(one) + 1):
        for p in sf:
            p.wait()
            if stage < len(one):
                p.start()
    for copy in zv:
        copy.wait()
    for k in range(1, n_tp):
        v_out[...] += v_got[n_stage + k]
    for copy in za:
        copy.wait_recv()

    @pl.loop(0, rows // size)
    def _(i):
        here = pl.ds(i * size, size)
        total = a_cols[z, here].astype(F32)
        for k in range(1, n_tp):
            total += a_zbuf[k - 1, here].astype(F32)
        a_out[here] = total

    own_x.wait()
    for copy in zx:
        copy.wait_recv()
    for copy in f_core + a_core_copies + zf + za + zx:
        copy.wait_send()
    for p in sf:
        p.drain()


def scatter_grads(ff, a0, a1, vectors, x_in, n_dp, n_tp):
    width = a0.shape[2]
    rows = a0.shape[1] + a1.shape[1]
    vec, hid = ff[0].shape[2:]
    ch = width // n_tp
    cut = rows // 2 // 16 * 16
    half = n_dp // 2
    stages = half.bit_length() - 1
    anyspace = pl.BlockSpec(memory_space=pl.ANY)
    vmem = pl.BlockSpec(memory_space=pltpu.VMEM)
    dma = pltpu.SemaphoreType.DMA
    return pl.pallas_call(
        functools.partial(scatter_kernel, n_dp, n_tp, cut),
        out_shape=(
            jax.ShapeDtypeStruct((n_dp, 3, vec, hid), BF),
            jax.ShapeDtypeStruct((rows, ch), F32),
            jax.ShapeDtypeStruct(vectors.shape, F32),
            jax.ShapeDtypeStruct((n_tp, x_in.shape[0], x_in.shape[1] // n_tp, width), BF),
        ),
        in_specs=[anyspace] * 5 + [vmem, anyspace],
        out_specs=(anyspace, vmem, vmem, anyspace),
        scratch_shapes=[
            pltpu.VMEM((half, 3, n_tp, vec, hid), BF),
            pltpu.VMEM((half, rows, width), BF),
            pltpu.VMEM((half, 3, n_tp, vec, hid), BF),
            pltpu.VMEM((half, rows, width), BF),
            pltpu.VMEM((half - 1, 3, n_tp, vec, hid), BF),
            pltpu.VMEM((half - 1, rows, width), BF),
            pltpu.VMEM((n_tp, rows, ch), BF),
            pltpu.VMEM((n_tp - 1, 3, vec, hid), BF),
            pltpu.VMEM((n_tp - 1, rows, ch), BF),
            pltpu.VMEM((3, vec, hid), BF),
            pltpu.VMEM((stages + n_tp,) + vectors.shape, F32),
            dma((5, half)),
            dma((5, half)),
            dma((5, half)),
            dma((2, 2, half)),
            dma((2, 2, half)),
            dma((4, n_tp - 1)),
            dma((4, n_tp - 1)),
            dma((4, n_dp - 1)),
            dma((4, n_dp - 1)),
            dma((stages + 1,)),
            dma((stages + 1,)),
            dma((2,)),
        ],
        compiler_params=pltpu.CompilerParams(
            collective_id=1, has_side_effects=True, vmem_limit_bytes=60 * 1024 * 1024
        ),
        name="scatter_grads",
    )(*ff, a0, a1, vectors, x_in)


def body(
    tokens,
    lengths,
    cotangent,
    norm1_gain,
    norm1_bias,
    in_weight,
    in_bias,
    filter_base,
    filter_mod,
    out_weight,
    out_bias,
    norm2_gain,
    norm2_bias,
    gate_weight,
    up_weight,
    down_weight,
    down_bias,
):
    micro, local, group, width = tokens.shape
    n_tp = lax.axis_size("tp")
    n_dp = lax.axis_size("dp")
    z = lax.axis_index("tp")
    d = lax.axis_index("dp")
    slot_len = local * n_tp
    own = micro * group // n_tp
    per_micro = min(group, own)
    ch = in_weight.shape[2]
    vec = width // n_dp
    hid = gate_weight.shape[1]
    table = jnp.asarray(packed_table(slot_len))
    table_t = jnp.asarray(np.ascontiguousarray(packed_table(slot_len).T))
    scale = 0.5 / slot_len

    rows = slot_len // n_dp
    last = n_dp - 1
    upper = d > last - d
    filters = jnp.stack([filter_base, filter_mod])
    across = [(i, (n_dp - i) % n_dp) for i in range(n_dp) if i % (n_dp // 2)] + [(0, n_dp // 2), (n_dp // 2, 0)]
    got = lax.ppermute(filters[:, :, rows:], "dp", [(i, last - i) for i in range(n_dp)])
    got_edge = lax.ppermute(filters[:, :, :1], "dp", across)
    direct = jnp.where(upper, got, filters[:, :, :rows]).astype(F32)
    mirror_lower = jnp.concatenate([got[:, :, 1:], got_edge], axis=2)
    mirror_upper = filters[:, :, 1 : rows + 1]
    mirror = jnp.flip(jnp.where(upper, mirror_upper, mirror_lower), 2).astype(F32)
    nyquist = got_edge[:, 0, 0].astype(F32)
    edge = ((jnp.arange(rows) == 0) & (d == 0))[None, :, None]
    half_real = jnp.where(edge, direct[:, 0], direct[:, 0] + mirror[:, 0])
    half_imag = jnp.where(edge, nyquist[:, None], direct[:, 1] - mirror[:, 1])
    half = jnp.stack([half_real, half_imag], 1).astype(BF).reshape(4 * rows, ch)
    slice_of = [2 * i if 2 * i < n_dp else 2 * (last - i) + 1 for i in range(n_dp)]

    a_in = jnp.concatenate([in_weight.transpose(1, 0, 2).reshape(3 * vec, ch), out_weight.T, half])
    vectors = jnp.stack([norm1_gain, norm1_bias, norm2_gain, norm2_bias, out_bias, down_bias])
    vectors = jnp.concatenate([vectors, in_bias])
    vectors = jnp.pad(vectors, ((0, 16 - 9), (0, width - vec)))
    share = hid // n_dp
    ff_in = jnp.concatenate(
        [
            lax.dynamic_slice_in_dim(gate_weight, d * vec, vec, 0),
            lax.dynamic_slice_in_dim(up_weight, d * vec, vec, 0),
            lax.dynamic_slice_in_dim(down_weight, d * share, share, 0).reshape(vec, hid),
        ]
    )
    x_in = tokens.transpose(0, 2, 1, 3).reshape(n_tp, own, local, width)
    ffw, aw, x_own = gather_weights(ff_in, a_in, vectors, x_in, n_dp, n_tp)
    cotangent, _ = lax.optimization_barrier((cotangent, aw))
    vectors = aw[:, 4 * vec + 4 * rows :, :vec].astype(F32).transpose(1, 0, 2).reshape(16, width)
    slots = [slice_of.index(k) for k in range(n_dp)]
    direct = vec % 16 == 0 and hid == width
    if direct:
        ws = [(ffw, (n_dp, n_tp, vec, hid), g) for g in range(3)]
        a_view = aw
    else:
        natural = [
            ffw[:, :, g * vec : (g + 1) * vec].transpose(1, 0, 2, 3).reshape(n_tp, width, hid) for g in range(2)
        ]
        natural.append(
            ffw[:, :, 2 * vec :].reshape(n_dp, n_tp, share, width).transpose(1, 0, 2, 3).reshape(n_tp, hid, width)
        )
        ws = [(w[None], (1,) + w.shape, 0) for w in natural]
        a_view = aw[:, : 4 * vec].reshape(n_dp, 4, vec, width).transpose(1, 0, 2, 3).reshape(1, 4 * width, width)
    feed_weights = (ws[0][0], ws)

    def to_owner(x):
        pieces = x.transpose(0, 2, 1, 3).reshape(n_tp, own, local, width)
        whole = jnp.zeros((own, slot_len, width), x.dtype)
        for source, block in exchange(pieces, z, n_tp):
            whole = lax.dynamic_update_slice(whole, block, (0, source * local, 0))
        return whole

    def to_slots(x):
        pieces = x.reshape(own, n_tp, local, width).transpose(1, 0, 2, 3)
        whole = jnp.zeros((n_tp, own, local, width), x.dtype)
        for source, block in exchange(pieces, z, n_tp):
            whole = lax.dynamic_update_slice(whole, block[None], (source, 0, 0, 0))
        return whole.reshape(micro, group, local, width).transpose(0, 2, 1, 3)

    c_own = to_owner(cotangent)
    flat_len = lax.dynamic_slice_in_dim(lengths.reshape(-1), z * own, own, 0)
    first = 4 * vec // rows
    n1, values, gating, nsum, mixing = project(x_own, flat_len, a_view, vectors)
    spec, conv, gated = spectral(values, gating, mixing, flat_len, table, table_t, aw, first, rows, slots, scale)
    middle, n2, act, side, hidden, out = feed(x_own, gated, flat_len, a_view, feed_weights, vectors)
    layer_out = to_slots(out)
    e, *d_ff = feed_back(c_own, n2, act, side, hidden, flat_len, feed_weights)
    mg, cg, gtg, d_out, sums = branch_back(e, middle, c_own, gated, gating, conv, flat_len, a_view, vectors)
    layer_out, cg = lax.optimization_barrier((layer_out, cg))
    vg, d_filter, cgv = spectral_back(cg, spec, mixing, flat_len, table, table_t, aw, first, rows, slots, scale)
    ig, d_first, sums = input_back(vg, gtg, n1, x_own, mg, nsum, cgv, flat_len, a_view, d_out, sums, vectors)
    if not direct:
        d_ff = [
            g[0].reshape(n_tp, n_dp, vec, hid).transpose(1, 0, 2, 3) for g in d_ff[:2]
        ] + [d_ff[2][0].reshape(n_tp, n_dp, vec, hid).transpose(1, 0, 2, 3)]
        d_first = d_first.reshape(4, n_dp, vec, width).transpose(1, 0, 2, 3).reshape(n_dp, 4 * vec, width)
    ffg, ag, vecs, input_grad = scatter_grads(d_ff, d_first, d_filter, sums, ig, n_dp, n_tp)
    input_grad = input_grad.reshape(micro, group, local, width).transpose(0, 2, 1, 3)
    gate_grad = ffg[:, 0].reshape(width, hid).astype(F32)
    up_grad = ffg[:, 1].reshape(width, hid).astype(F32)
    down_grad = ffg[:, 2].reshape(hid, width).astype(F32)
    in_grad = ag[: 3 * vec].reshape(3, vec, ch).transpose(1, 0, 2)
    out_grad = ag[3 * vec : 4 * vec].T
    fgrad = ag[4 * vec :].astype(BF).reshape(2, 2, rows, ch)
    other = lax.ppermute(fgrad, "dp", [(i, last - i) for i in range(n_dp)])
    low_slice = jnp.where(upper, other, fgrad)
    high_slice = jnp.where(upper, fgrad, other)
    both = jnp.concatenate([low_slice, high_slice], axis=2)
    follow = lax.ppermute(fgrad[:, :, :1], "dp", across)
    zero = jnp.zeros_like(follow[:, 0])
    follow = jnp.where(d == n_dp // 2, jnp.stack([follow[:, 1], zero], 1), follow)
    mirrored = jnp.flip(jnp.concatenate([both[:, :, 1:], follow], axis=2), 2)
    mirrored = jnp.stack([mirrored[:, 0], -mirrored[:, 1]], 1)
    plain = jnp.stack(
        [both[:, 0], jnp.where((d == 0) & (jnp.arange(2 * rows) == 0)[None, :, None], 0.0, both[:, 1].astype(F32)).astype(BF)], 1
    )
    full = jnp.where(upper, mirrored, plain).astype(F32)

    piece = width // (n_dp * n_tp)
    vecs = lax.dynamic_slice_in_dim(vecs, (d * n_tp + z) * piece, piece, 1)
    return (
        layer_out,
        input_grad,
        vecs[0],
        vecs[1],
        in_grad,
        vecs[6:9],
        full[0],
        full[1],
        out_grad,
        vecs[4],
        vecs[2],
        vecs[3],
        gate_grad,
        up_grad,
        down_grad,
        vecs[5],
    )


def solution(mesh):
    in_specs = (
        P(None, "tp", "dp", None),
        P(None, "dp"),
        P(None, "tp", "dp", None),
        P("dp"),
        P("dp"),
        P("dp", None, "tp"),
        P(None, "dp"),
        P(None, "dp", "tp"),
        P(None, "dp", "tp"),
        P("tp", "dp"),
        P("dp"),
        P("dp"),
        P("dp"),
        P(None, "tp"),
        P(None, "tp"),
        P("tp", None),
        P("dp"),
    )
    out_specs = (
        P(None, "tp", "dp", None),
        P(None, "tp", "dp", None),
        P(("dp", "tp")),
        P(("dp", "tp")),
        P("dp", None, "tp"),
        P(None, ("dp", "tp")),
        P(None, "dp", "tp"),
        P(None, "dp", "tp"),
        P("tp", "dp"),
        P(("dp", "tp")),
        P(("dp", "tp")),
        P(("dp", "tp")),
        P(None, "tp"),
        P(None, "tp"),
        P("tp", None),
        P(("dp", "tp")),
    )
    return jax.shard_map(body, mesh=mesh, in_specs=in_specs, out_specs=out_specs, check_vma=False)
```

```python
import functools
import math

import jax
import jax.numpy as jnp
import numpy as np
from jax import lax
from jax.experimental import pallas as pl
from jax.experimental.pallas import tpu as pltpu
from jax.sharding import PartitionSpec as P

EPSILON = 1e-05
ONE_TABLE = True
BF = jnp.bfloat16
F32 = jnp.float32
GELU_A = math.sqrt(2.0 / math.pi)
GELU_B = 0.044715


def packed_table(slot_len):
    frequency = np.arange(slot_len, dtype=np.int64)[:, None]
    position = np.arange(slot_len, dtype=np.int64)[None, :]
    angles = (frequency * position % (2 * slot_len)).astype(np.float32) * np.float32(math.pi / slot_len)
    top = np.cos(angles)
    low = -np.sin(angles)
    low[0] = 1.0 - 2.0 * (np.arange(slot_len) % 2)
    return np.concatenate([top, low]).astype(np.float32).astype(jnp.bfloat16)


def shift(x, axis, step):
    n = lax.axis_size(axis)
    return lax.ppermute(x, axis, [(i, (i + step) % n) for i in range(n)])


def exchange(pieces, place, n):
    out = [(place, lax.dynamic_index_in_dim(pieces, place, 0, keepdims=False))]
    for step in range(1, n):
        block = lax.dynamic_index_in_dim(pieces, (place + step) % n, 0, keepdims=False)
        out.append(((place + n - step) % n, shift(block, "tp", step)))
    return out


def mm(a, b):
    return lax.dot_general(a, b, (((1,), (0,)), ((), ())), preferred_element_type=F32)


def mm_nt(a, b):
    return lax.dot_general(a, b, (((1,), (1,)), ((), ())), preferred_element_type=F32)


def mm_tn(a, b):
    return lax.dot_general(a, b, (((0,), (0,)), ((), ())), preferred_element_type=F32)


def mean_of(v):
    return jnp.sum(v, axis=-1, keepdims=True) * (1.0 / v.shape[-1])


def standardize(v):
    centred = v - mean_of(v)
    inverse = lax.rsqrt(mean_of(centred * centred) + EPSILON)
    return centred * inverse, inverse


def norm_back(e, gain, s, q):
    eg = e * gain
    return q * (eg - mean_of(eg) - s * mean_of(eg * s))


def gelu_parts(v):
    square = v * v
    th = jnp.tanh(v * (GELU_A + (GELU_A * GELU_B) * square))
    rise = 0.5 + 0.5 * th
    act = v * rise
    slope = rise + act * (1.0 - th) * (GELU_A + (3.0 * GELU_A * GELU_B) * square)
    return act, slope


def live(rows, first, count):
    at = lax.broadcasted_iota(jnp.int32, (rows, 1), 0) + first
    return jnp.where(at < count, 1.0, 0.0)


def joined(ref):
    v = ref[...]
    return v.reshape(-1, v.shape[-1])


def two_part_dot(a, b, dims):
    high = a.astype(BF)
    low = (a - high.astype(F32)).astype(BF)
    return lax.dot_general(high, b, (dims, ((), ())), preferred_element_type=F32) + lax.dot_general(
        low, b, (dims, ((), ())), preferred_element_type=F32
    )


def top_row(v, rows=8):
    r = lax.broadcasted_iota(jnp.int32, (rows, v.shape[1]), 0)
    return jnp.where(r == 0, jnp.broadcast_to(v, (rows, v.shape[1])), 0.0)


def project_kernel(tile, lens, x, wv, wg, wc, vec, n1, values, gating, nsum, mixing):
    s, t = pl.program_id(0), pl.program_id(1)
    count = lens[s]
    valid = live(tile, t * tile, count)
    std, _ = standardize(x[0].astype(F32))
    normed = (std * vec[0:1] + vec[1:2]).astype(BF)
    n1[0] = normed
    values[0] = ((mm(normed, joined(wv)) + vec[6:7]) * valid).astype(BF)
    gating[0] = (mm(normed, joined(wg)) + vec[7:8]).astype(BF)
    part = top_row(jnp.sum(normed.astype(F32) * valid, axis=0, keepdims=True))

    @pl.when(t == 0)
    def _():
        nsum[0] = part

    @pl.when(t > 0)
    def _():
        nsum[0] += part

    @pl.when(t == pl.num_programs(1) - 1)
    def _():
        length = count.astype(F32)
        cond = two_part_dot(nsum[0], joined(wc), ((1,), (0,))) + length * vec[8:9]
        mixing[0] = jnp.tanh(cond / length)


def filters_of(refs, slots, mix):
    base_r, base_i, mod_r, mod_i = [jnp.concatenate([ref[j] for j in slots]).astype(F32) for ref in refs]
    return base_r + mix * mod_r, base_i + mix * mod_i, mod_r, mod_i


def spectral_kernel(slots, scale, values, gating, mixing, table, f0, f1, f2, f3, spec, conv, gated):
    own = values.shape[0]
    n = values.shape[1]
    raw = [mm(table[...], values[s]) for s in range(own)]
    edge = lax.broadcasted_iota(jnp.int32, (n, 1), 0) == 0
    outs = []
    for s in range(own):
        v = raw[s]
        spec[s] = v.astype(BF)
        sr, si = v[:n], v[n:]
        fr, fi, _, _ = filters_of((f0, f1, f2, f3), slots, mixing[s, 0:1])
        fr2 = jnp.where(edge, fi, fr)
        fi = jnp.where(edge, 0.0, fi)
        prod = jnp.concatenate([(fr * sr - fi * si).astype(BF), (fr2 * si + fi * sr).astype(BF)])
        outs.append(mm_tn(table[...], prod))
    for s in range(own):
        out = outs[s] * scale
        conv[s] = out.astype(BF)
        gated[s] = (out * gating[s].astype(F32)).astype(BF)


def feed_kernel(tile, n_tp, lens, x, gated, w_out, wg, wu, wd, vec, middle, n2, act, side, hidden, out):
    s, t = pl.program_id(0), pl.program_id(1)
    valid = live(tile, t * tile, lens[s])
    mid = x[0].astype(F32) + valid * (mm_nt(gated[0], joined(w_out)) + vec[4:5])
    middle[0] = mid
    std, _ = standardize(mid)
    normed = (std * vec[2:3] + vec[3:4]).astype(BF)
    n2[0] = normed
    feed = jnp.zeros(mid.shape, F32)
    for p in range(n_tp):
        gate = mm(normed, joined(wg.at[:, p]))
        up = mm(normed, joined(wu.at[:, p]))
        a, slope = gelu_parts(gate)
        act[0, p] = a.astype(BF)
        side[0, p] = (up * slope).astype(BF)
        h = (a * up).astype(BF)
        hidden[0, p] = h
        feed += mm(h, joined(wd.at[:, p]))
    out[0] = (mid + valid * (feed + vec[5:6])).astype(BF)


def feed_back_kernel(tile, lens, cot, n2, act, side, hidden, wg, wu, wd, e_out, d_gate, d_up, d_down, acc_g, acc_u, acc_d, fgs, ggs, ugs):
    p, s = pl.program_id(0), pl.program_id(1)
    n = cot.shape[1]

    @pl.when(p == 0)
    def _():
        e_out[s] = jnp.zeros(e_out.shape[1:], F32)

    @pl.when(s == 0)
    def _():
        for acc in (acc_g, acc_u, acc_d):
            acc[...] = jnp.zeros(acc.shape, F32)

    down, gate, up = joined(wd.at[:, 0]), joined(wg.at[:, 0]), joined(wu.at[:, 0])
    for i in range(n // tile):
        here = pl.ds(i * tile, tile)
        fg = (cot[0, here].astype(F32) * live(tile, i * tile, lens[s])).astype(BF)
        fgs[here] = fg
        hg = mm_nt(fg, down)
        ggs[here] = (hg * side[0, 0, here].astype(F32)).astype(BF)
        ugs[here] = (hg * act[0, 0, here].astype(F32)).astype(BF)
    for i in range(n // tile):
        here = pl.ds(i * tile, tile)
        e_out[s, here] += mm_nt(ggs[here], gate) + mm_nt(ugs[here], up)
    normed = n2[0]
    acc_g[...] += mm_tn(normed, ggs[...])
    acc_u[...] += mm_tn(normed, ugs[...])
    acc_d[...] += mm_tn(hidden[0, 0], fgs[...])

    @pl.when(s == pl.num_programs(1) - 1)
    def _():
        for acc, out in zip((acc_g, acc_u, acc_d), (d_gate, d_up, d_down)):
            out[:, 0] = acc[...].astype(BF).reshape(out.shape[0], out.shape[2], out.shape[3])


def branch_back_kernel(tile, lens, e, middle, cot, gated, gating, conv, w_out, vec, mg_out, cg, gtg, d_out, sums, acc):
    s, t = pl.program_id(0), pl.program_id(1)
    begin = (s == 0) & (t == 0)
    end = (s == pl.num_programs(0) - 1) & (t == pl.num_programs(1) - 1)

    @pl.when(begin)
    def _():
        acc[...] = jnp.zeros(acc.shape, F32)
        sums[...] = jnp.zeros(sums.shape, F32)

    valid = live(tile, t * tile, lens[s])
    up = cot[0].astype(F32)
    fg = (up * valid).astype(BF).astype(F32)
    std, inverse = standardize(middle[0])
    grad = e[0]
    mg = up + norm_back(grad, vec[2:3], std, inverse)
    mg_out[0] = mg
    bgr = (mg * valid).astype(BF)
    ggr = mm(bgr, joined(w_out))
    cg[0] = (ggr * gating[0].astype(F32)).astype(BF)
    gtg[0] = (ggr * conv[0].astype(F32)).astype(BF)
    part = mm_tn(bgr, gated[0])
    rows = [grad * std, grad, bgr.astype(F32), fg]
    rows = [jnp.sum(r, axis=0, keepdims=True) for r in rows]

    acc[...] += part
    for i, r in enumerate(rows):
        sums[i : i + 1] += r

    @pl.when(end)
    def _():
        d_out[...] = acc[...].astype(BF).reshape(d_out.shape)


def spectral_back_kernel(slots, scale, lens, cg, spec, mixing, table, f0, f1, f2, f3, vg, fgrad, cgv):
    own = cg.shape[0]
    n = cg.shape[1]
    size = n // len(slots)
    raw = [mm(table[...], cg[s]) for s in range(own)]
    edge = lax.broadcasted_iota(jnp.int32, (n, 1), 0) == 0
    outs, total = [], None
    for s in range(own):
        v = raw[s] * scale
        pr, pi = v[:n], v[n:]
        mix = mixing[s, 0:1]
        fr, fi, mod_r, mod_i = filters_of((f0, f1, f2, f3), slots, mix)
        fr2 = jnp.where(edge, fi, fr)
        fi = jnp.where(edge, 0.0, fi)
        sg = jnp.concatenate([(fr * pr + fi * pi).astype(BF), (fr2 * pi - fi * pr).astype(BF)])
        outs.append(mm_tn(table[...], sg))
        sr, si = spec[s, :n].astype(F32), spec[s, n:].astype(F32)
        both = pi * si
        dr = pr * sr + jnp.where(edge, 0.0, both)
        di = jnp.where(edge, both, pi * sr - pr * si)
        mixg = jnp.sum(mod_r * dr + mod_i * di, axis=0, keepdims=True)
        step = mixg * (1.0 - mix * mix) / lens[s].astype(F32)
        cgv[s] = top_row(step.astype(BF).astype(F32))
        parts = (dr, di, mix * dr, mix * di)
        total = parts if total is None else tuple(t + p for t, p in zip(total, parts))
    for s in range(own):
        vg[s] = (outs[s] * live(n, 0, lens[s])).astype(BF)
    for j in range(len(slots)):
        k = slots.index(j)
        for i in range(4):
            fgrad[j, pl.ds(i * size, size)] = total[i][k * size : (k + 1) * size].astype(BF)


def input_back_kernel(tile, lens, vg, gtg, n1, x, mg, nsum, cgv, wv, wg, wc, d_out, sums_in, vec, ig, d_in, sums, acc_v, acc_g, acc_c):
    s, t = pl.program_id(0), pl.program_id(1)
    begin = (s == 0) & (t == 0)
    end = (s == pl.num_programs(0) - 1) & (t == pl.num_programs(1) - 1)
    count = lens[s]

    @pl.when(begin)
    def _():
        for acc in (acc_v, acc_g, acc_c):
            acc[...] = jnp.zeros(acc.shape, F32)
        sums[...] = jnp.zeros(sums.shape, F32)
        sums[2:6] = sums_in[0:4]

    valid = live(tile, t * tile, count)
    cvec = mm_nt(cgv[0].astype(BF), joined(wc))[0:1]
    vgb, gtb = vg[0], gtg[0]
    e = mm_nt(vgb, joined(wv)) + mm_nt(gtb, joined(wg)) + valid * cvec
    std, inverse = standardize(x[0].astype(F32))
    ig[0] = (mg[0] + norm_back(e, vec[0:1], std, inverse)).astype(BF)
    normed = n1[0]
    part_v, part_g = mm_tn(normed, vgb), mm_tn(normed, gtb)
    rows = [e * std, e, vgb.astype(F32), gtb.astype(F32)]
    rows = [jnp.sum(r, axis=0, keepdims=True) for r in rows]

    acc_v[...] += part_v
    acc_g[...] += part_g
    for i, r in zip((0, 1, 6, 7), rows):
        sums[i : i + 1] += r

    @pl.when(t == 0)
    def _():
        acc_c[...] += two_part_dot(nsum[0], cgv[0].astype(BF), ((0,), (0,)))
        sums[8:9] += cgv[0, 0:1] * count.astype(F32)

    @pl.when(end)
    def _():
        r = d_out.shape[1]
        shape = (d_in.shape[0], r, d_in.shape[2])
        for i, acc in enumerate((acc_v, acc_g, acc_c)):
            d_in[:, i * r : (i + 1) * r] = acc[...].astype(BF).reshape(shape)
        d_in[:, 3 * r :] = d_out[...]


def call(kernel, grid, lens, ins, in_specs, outs, out_specs, scratch, flops, name, limit=56):
    spec = pltpu.PrefetchScalarGridSpec(
        num_scalar_prefetch=1, grid=grid, in_specs=in_specs, out_specs=out_specs, scratch_shapes=scratch
    )
    moved = sum(math.prod(v.shape) * v.dtype.itemsize for v in list(ins) + list(outs))
    return pl.pallas_call(
        kernel,
        grid_spec=spec,
        out_shape=tuple(outs),
        compiler_params=pltpu.CompilerParams(
            dimension_semantics=("arbitrary",) * len(grid), vmem_limit_bytes=limit * 1024 * 1024
        ),
        cost_estimate=pl.CostEstimate(flops=int(flops), bytes_accessed=int(moved), transcendentals=0),
        name=name,
    )(lens, *ins)


def once(block, index):
    return pl.BlockSpec(block, lambda *_: index, pipeline_mode=pl.Buffered(1))


def shape_of(shape, dtype):
    return jax.ShapeDtypeStruct(shape, dtype)


def project(x, lens, aw, vec):
    own, n, width = x.shape
    tile = min(512, n)
    nd, r = aw.shape[0], width // aw.shape[0]
    tok = pl.BlockSpec((1, tile, width), lambda s, t, *_: (s, t, 0))
    one = pl.BlockSpec((1, 8, width), lambda s, t, *_: (s, 0, 0))
    weights = [once((nd, r, width), (0, g, 0)) for g in range(3)]
    sd = shape_of(x.shape, BF)
    row = shape_of((own, 8, width), F32)
    return call(
        functools.partial(project_kernel, tile),
        (own, n // tile),
        lens,
        [x, aw, aw, aw, vec],
        [tok] + weights + [once(vec.shape, (0, 0))],
        [sd, sd, sd, row, row],
        (tok, tok, tok, one, one),
        [],
        4 * own * n * width * width,
        "project",
    )


def filter_specs(fw, n_dp, rows, cb, first):
    return [
        pl.BlockSpec((n_dp, rows, cb), lambda *g, i=i: (0, first + i, g[0])) for i in range(4)
    ]


def spectral(values, gating, mixing, lens, table, fw, first, rows, slots, scale):
    own, n, width = values.shape
    cb = min(256, width)
    n_dp = fw.shape[0]
    tok = pl.BlockSpec((own, n, cb), lambda c, *_: (0, 0, c))
    both = pl.BlockSpec((own, 2 * n, cb), lambda c, *_: (0, 0, c))
    one = pl.BlockSpec((own, 8, cb), lambda c, *_: (0, 0, c))

    def kernel(lens, *refs):
        spectral_kernel(slots, scale, *refs)

    return call(
        kernel,
        (width // cb,),
        lens,
        [values, gating, mixing, table] + [fw] * 4,
        [tok, tok, one, once(table.shape, (0, 0))] + filter_specs(fw, n_dp, rows, cb, first),
        [shape_of((own, 2 * n, width), BF), shape_of(values.shape, BF), shape_of(values.shape, BF)],
        (both, tok, tok),
        [],
        8 * own * n * n * width,
        "spectral",
    )


def feed(x, gated, lens, aw, ffw, vec):
    own, n, width = x.shape
    tile = min(512, n)
    nd, n_tp, _, hid = ffw[0].shape
    r = width // aw.shape[0]
    tok = pl.BlockSpec((1, tile, width), lambda s, t, *_: (s, t, 0))
    wide = pl.BlockSpec((1, n_tp, tile, hid), lambda s, t, *_: (s, 0, t, 0))
    ws = [once(shape, (0, 0, at, 0)) for _, shape, at in ffw[1]]
    big = shape_of((own, n_tp, n, hid), BF)
    return call(
        functools.partial(feed_kernel, tile, n_tp),
        (own, n // tile),
        lens,
        [x, gated, aw] + [w for w, _, _ in ffw[1]] + [vec],
        [tok, tok, once((aw.shape[0], r, width), (0, 3, 0))] + ws + [once(vec.shape, (0, 0))],
        [shape_of(x.shape, F32), shape_of(x.shape, BF), big, big, big, shape_of(x.shape, BF)],
        (tok, tok, wide, wide, wide, tok),
        [],
        2 * own * n * width * (width + 3 * n_tp * hid),
        "feed",
        limit=60,
    )


def feed_back(cot, n2, act, side, hidden, lens, ffw):
    own, n, width = cot.shape
    n_tp, hid = act.shape[1], act.shape[3]
    tile = min(512, n)
    tok = pl.BlockSpec((1, n, width), lambda p, s, *_: (s, 0, 0))
    wide = pl.BlockSpec((1, 1, n, hid), lambda p, s, *_: (s, p, 0, 0))
    ws = [
        pl.BlockSpec((shape[0], 1) + shape[2:], lambda p, s, *_, at=at: (0, p, at, 0)) for _, shape, at in ffw[1]
    ]
    d_specs = [pl.BlockSpec((shape[0], 1) + shape[2:], lambda p, s, *_: (0, p, 0, 0)) for _, shape, _ in ffw[1]]
    d_shapes = [shape_of(shape, BF) for _, shape, _ in ffw[1]]
    return call(
        functools.partial(feed_back_kernel, tile),
        (n_tp, own),
        lens,
        [cot, n2, act, side, hidden] + [w for w, _, _ in ffw[1]],
        [tok, tok, wide, wide, wide] + ws,
        [shape_of(cot.shape, F32)] + d_shapes,
        (pl.BlockSpec(cot.shape, lambda *_: (0, 0, 0), pipeline_mode=pl.Buffered(1)), *d_specs),
        [
            pltpu.VMEM((width, hid), F32),
            pltpu.VMEM((width, hid), F32),
            pltpu.VMEM((hid, width), F32),
            pltpu.VMEM((n, width), BF),
            pltpu.VMEM((n, hid), BF),
            pltpu.VMEM((n, hid), BF),
        ],
        12 * own * n * width * n_tp * hid,
        "feed_back",
        limit=60,
    )


def branch_back(e, middle, cot, gated, gating, conv, lens, aw, vec):
    own, n, width = cot.shape
    tile = min(512, n)
    nd, r = aw.shape[0], width // aw.shape[0]
    tok = pl.BlockSpec((1, tile, width), lambda s, t, *_: (s, t, 0))
    return call(
        functools.partial(branch_back_kernel, tile),
        (own, n // tile),
        lens,
        [e, middle, cot, gated, gating, conv, aw, vec],
        [tok] * 6 + [once((nd, r, width), (0, 3, 0)), once(vec.shape, (0, 0))],
        [
            shape_of(cot.shape, F32),
            shape_of(cot.shape, BF),
            shape_of(cot.shape, BF),
            shape_of((nd, r, width), BF),
            shape_of((8, width), F32),
        ],
        (tok, tok, tok, pl.BlockSpec((nd, r, width), lambda *_: (0, 0, 0)), pl.BlockSpec((8, width), lambda *_: (0, 0))),
        [pltpu.VMEM((width, width), F32)],
        4 * own * n * width * width,
        "branch_back",
    )


def spectral_back(cg, spec, mixing, lens, table, fw, first, rows, slots, scale):
    own, n, width = cg.shape
    cb = min(256, width)
    n_dp = fw.shape[0]
    tok = pl.BlockSpec((own, n, cb), lambda c, *_: (0, 0, c))
    both = pl.BlockSpec((own, 2 * n, cb), lambda c, *_: (0, 0, c))
    one = pl.BlockSpec((own, 8, cb), lambda c, *_: (0, 0, c))
    return call(
        functools.partial(spectral_back_kernel, slots, scale),
        (width // cb,),
        lens,
        [cg, spec, mixing, table] + [fw] * 4,
        [tok, both, one, once(table.shape, (0, 0))] + filter_specs(fw, n_dp, rows, cb, first),
        [shape_of(cg.shape, BF), shape_of((n_dp, 4 * rows, width), BF), shape_of((own, 8, width), F32)],
        (tok, pl.BlockSpec((n_dp, 4 * rows, cb), lambda c, *_: (0, 0, c)), one),
        [],
        8 * own * n * n * width,
        "spectral_back",
    )


def input_back(vg, gtg, n1, x, mg, nsum, cgv, lens, aw, d_out, sums, vec):
    own, n, width = x.shape
    tile = min(512, n)
    nd, r = aw.shape[0], width // aw.shape[0]
    tok = pl.BlockSpec((1, tile, width), lambda s, t, *_: (s, t, 0))
    one = pl.BlockSpec((1, 8, width), lambda s, t, *_: (s, 0, 0))
    weights = [once((nd, r, width), (0, g, 0)) for g in range(3)]
    return call(
        functools.partial(input_back_kernel, tile),
        (own, n // tile),
        lens,
        [vg, gtg, n1, x, mg, nsum, cgv, aw, aw, aw, d_out, sums, vec],
        [tok] * 5 + [one] * 2 + weights + [once((nd, r, width), (0, 0, 0)), once((8, width), (0, 0)), once(vec.shape, (0, 0))],
        [shape_of(x.shape, BF), shape_of((nd, 4 * r, width), BF), shape_of((16, width), F32)],
        (tok, pl.BlockSpec((nd, 4 * r, width), lambda *_: (0, 0, 0)), pl.BlockSpec((16, width), lambda *_: (0, 0))),
        [pltpu.VMEM((width, width), F32)] * 3,
        8 * own * n * width * width,
        "input_back",
    )


MESH = pl.DeviceIdType.MESH


def flip(index, step):
    return index + step - 2 * step * ((index // step) % 2)


def bit_orders(n_dp):
    bits = [1 << b for b in range(1, (n_dp - 1).bit_length())]
    return bits, bits[::-1]


def greet(d, z, n_dp, n_tp):
    barrier = pltpu.get_barrier_semaphore()
    count = 0
    step = 1
    while step < n_dp:
        pl.semaphore_signal(barrier, inc=1, device_id=(flip(d, step), z), device_id_type=MESH)
        step *= 2
        count += 1
    for k in range(1, n_tp):
        pl.semaphore_signal(barrier, inc=1, device_id=(d, lax.rem(z + k, n_tp)), device_id_type=MESH)
        count += 1
    pl.semaphore_wait(barrier, count)


def remote(src, dst, send, recv, target):
    copy = pltpu.make_async_remote_copy(
        src_ref=src, dst_ref=dst, send_sem=send, recv_sem=recv, device_id=target, device_id_type=MESH
    )
    copy.start()
    return copy


class Pack:
    def __init__(self, rows, ch):
        self.rows, self.ch = rows, ch
        self.main = ch // 128
        self.rest = ch % 128
        self.dense = self.rest == 64 and rows % 32 == 0
        self.tail = 0 if not self.rest else rows // 2 if self.dense else rows
        self.total = self.main * rows + self.tail

    def pack(self, v):
        parts = [v[:, i * 128 : (i + 1) * 128] for i in range(self.main)]
        if self.rest:
            left = v[:, self.main * 128 :]
            if self.dense:
                parts.append(jnp.concatenate([left[: self.tail], left[self.tail :]], axis=1))
            else:
                parts.append(jnp.pad(left, ((0, 0), (0, 128 - self.rest))))
        return jnp.concatenate(parts)

    def unpack(self, v):
        parts = [v[i * self.rows : (i + 1) * self.rows] for i in range(self.main)]
        if self.rest:
            left = v[self.main * self.rows :]
            if self.dense:
                parts.append(jnp.concatenate([left[:, :64], left[:, 64:]]))
            else:
                parts.append(left[:, : self.rest])
        return jnp.concatenate(parts, axis=1)

    def pieces(self):
        out = [(i * self.rows, 0, self.rows, 0, 128, i * 128) for i in range(self.main)]
        at = self.main * self.rows
        if self.dense:
            out += [(at, 0, self.tail, 0, 64, self.main * 128), (at, self.tail, self.tail, 64, 64, self.main * 128)]
        elif self.rest:
            out += [(at, 0, self.rows, 0, self.rest, self.main * 128)]
        return out


def lanes_to(width, lane, lanes, column):
    r = lax.broadcasted_iota(jnp.int32, (128, width), 0)
    c = lax.broadcasted_iota(jnp.int32, (128, width), 1)
    inside = (r >= lane) & (r < lane + lanes)
    return jnp.where(inside & (c - r == column - lane), 1.0, 0.0).astype(BF)


def fill_places(ones, layout, width, n_tp):
    pieces = layout.pieces()
    for s in range(n_tp):
        for i, (_, _, _, lane, lanes, column) in enumerate(pieces):
            ones[s * len(pieces) + i] = lanes_to(width, lane, lanes, s * layout.ch + column)


class Line:
    def __init__(self, part, d, z, n, send, recv):
        self.part, self.d, self.z, self.n, self.send, self.recv = part, d, z, n, send, recv

    def _copy(self, way, t, block):
        target = (self.d, self.z + 1 if way == 0 else self.z - 1)
        return pltpu.make_async_remote_copy(
            src_ref=self.part(block),
            dst_ref=self.part(block),
            send_sem=self.send.at[way, t],
            recv_sem=self.recv.at[way, t],
            device_id=target,
            device_id_type=MESH,
        )

    def start(self, t):
        z, n = self.z, self.n

        @pl.when((z >= t) & (z < n - 1))
        def _():
            self._copy(0, t, z - t).start()

        @pl.when((z + t < n) & (z > 0))
        def _():
            self._copy(1, t, z + t).start()

    def wait(self, t):
        z, n = self.z, self.n

        @pl.when(z >= t + 1)
        def _():
            self._copy(0, t, z - 1 - t).wait_recv()

        @pl.when(z + t + 1 < n)
        def _():
            self._copy(1, t, z + 1 + t).wait_recv()

    def drain(self):
        z, n = self.z, self.n
        for t in range(n - 1):

            @pl.when((z >= t) & (z < n - 1))
            def _(t=t):
                self._copy(0, t, z - t).wait_send()

            @pl.when((z + t < n) & (z > 0))
            def _(t=t):
                self._copy(1, t, z + t).wait_send()


class Spread:
    def __init__(self, part, order, d, z, send, recv):
        self.part, self.z, self.send, self.recv = part, z, send, recv
        held, self.steps, used = [d], [], 0
        for step in order:
            self.steps.append((flip(d, step), [(slot, used + i) for i, slot in enumerate(held)]))
            used += len(held)
            held = held + [flip(slot, step) for slot in held]
        self.stage = 0

    def copies(self, stage):
        target, sent = self.steps[stage]
        return [
            pltpu.make_async_remote_copy(
                src_ref=self.part(slot),
                dst_ref=self.part(slot),
                send_sem=self.send.at[i],
                recv_sem=self.recv.at[i],
                device_id=(target, self.z),
                device_id_type=MESH,
            )
            for slot, i in sent
        ]

    def start(self):
        for copy in self.copies(self.stage):
            copy.start()

    def wait(self):
        for copy in self.copies(self.stage):
            copy.wait_recv()
        self.stage += 1

    def drain(self):
        for stage in range(len(self.steps)):
            for copy in self.copies(stage):
                copy.wait_send()


def chunk_of(rows):
    return next((c for c in (128, 96, 64, 48, 32, 16) if rows % c == 0), rows)


def add_rows(dst, src):
    rows = dst.shape[0]
    size = chunk_of(rows)

    @pl.loop(0, rows // size)
    def _(i):
        at = pl.ds(i * size, size)
        dst[at] = (dst[at].astype(F32) + src[at].astype(F32)).astype(BF)


def lane_place(rows, cols, offset):
    r = lax.broadcasted_iota(jnp.int32, (rows, cols), 0)
    c = lax.broadcasted_iota(jnp.int32, (rows, cols), 1)
    return jnp.where(c - r == offset, 1.0, 0.0).astype(BF)


def gather_kernel(
    n_dp, n_tp, cut, ff_in, a_in, vec_in, x_in, ff_out, a_out, x_out, a_z, a_nat, ones,
    la_send, la_recv, lf_send, lf_recv, x_send, x_recv, s_send, s_recv, local,
):
    d, z = lax.axis_index("dp"), lax.axis_index("tp")
    width = a_nat.shape[1]
    ch = width // n_tp
    rows = a_nat.shape[0] - vec_in.shape[0]
    layout = Pack(rows, ch)
    own_ff = pltpu.make_async_copy(ff_in, ff_out.at[d, z], local.at[0])
    own_ff.start()
    own_a = pltpu.make_async_copy(a_in, a_z.at[z], local.at[1])
    own_a.start()
    greet(d, z, n_dp, n_tp)
    line_a = Line(lambda s: a_z.at[s], d, z, n_tp, la_send, la_recv)
    line_f = Line(lambda s: ff_out.at[d, s], d, z, n_tp, lf_send, lf_recv)
    first, second = bit_orders(n_dp)
    ff_rows = ff_in.shape[0]
    ff_cut = ff_rows // 2 // 16 * 16

    def block_spreads(block):
        out = []
        for h, (lo, count, order) in enumerate(((0, ff_cut, first), (ff_cut, ff_rows - ff_cut, second))):
            at = 2 + 2 * block + h
            out.append(
                Spread(
                    lambda s, lo=lo, count=count: ff_out.at[s, block, pl.ds(lo, count)],
                    order + [1], d, z, s_send.at[at], s_recv.at[at],
                )
            )
        return out

    own_a.wait()
    line_a.start(0)
    own_ff.wait()
    f_own = block_spreads(z)
    for p in f_own:
        p.start()
    fill_places(ones, layout, width, n_tp)
    for t in range(n_tp - 1):
        line_a.wait(t)
        if t + 1 < n_tp - 1:
            line_a.start(t + 1)
    line_f.start(0)
    half_rows = rows // 2
    n_pieces = len(layout.pieces())
    size = chunk_of(half_rows)
    for side in range(2):
        found = []
        for j, (packed, low, count, _, _, _) in enumerate(layout.pieces()):
            if low <= side * half_rows < low + count:
                found.append((packed + side * half_rows - low, j))

        @pl.loop(0, half_rows // size)
        def _(i, found=found, side=side):
            total = jnp.zeros((size, width), F32)
            for s in range(n_tp):
                for packed, j in found:
                    total += mm(a_z[s, pl.ds(packed + i * size, size)], ones[s * n_pieces + j])
            a_nat[pl.ds(side * half_rows + i * size, size)] = total.astype(BF)

    a_nat[rows:] = vec_in[...]
    put = pltpu.make_async_copy(a_nat, a_out.at[d], local.at[2])
    put.start()
    put.wait()
    total_rows = a_nat.shape[0]
    sa = [
        Spread(lambda s: a_out.at[s, pl.ds(0, cut)], first + [1], d, z, s_send.at[0], s_recv.at[0]),
        Spread(lambda s: a_out.at[s, pl.ds(cut, total_rows - cut)], second + [1], d, z, s_send.at[1], s_recv.at[1]),
    ]
    for p in sa:
        p.start()
    stages = len(first) + 1

    def advance(group):
        for p in group:
            p.wait()
            if p.stage < stages:
                p.start()

    advance(f_own)
    blocks = []
    for t in range(n_tp - 1):
        line_f.wait(t)
        if t + 1 < n_tp - 1:
            line_f.start(t + 1)
        for exists, block in ((z >= t + 1, z - 1 - t), (z + t + 1 < n_tp, z + 1 + t)):
            group = block_spreads(block)
            blocks.append((exists, group))

            @pl.when(exists)
            def _(group=group):
                for p in group:
                    p.start()

        if t == 0:
            advance(sa)
            advance(f_own)
    size = x_in.shape[2]
    here = pl.ds(z * size, size)
    own_x = pltpu.make_async_copy(x_in.at[z], x_out.at[:, here], local.at[3])
    own_x.start()
    zx = []
    for k in range(1, n_tp):
        peer = lax.rem(z + k, n_tp)
        zx.append(remote(x_in.at[peer], x_out.at[:, here], x_send.at[k - 1], x_recv.at[k - 1], (d, peer)))
    for stage in range(stages):
        for exists, group in blocks:

            @pl.when(exists)
            def _(group=group):
                advance(group)

        if stage + 1 < stages:
            advance(sa)
        if stage == 0:
            for p in f_own:
                p.wait()
    for p in sa + f_own:
        p.drain()
    for exists, group in blocks:

        @pl.when(exists)
        def _(group=group):
            for p in group:
                p.drain()

    own_x.wait()
    for copy in zx:
        copy.wait_recv()
    for copy in zx:
        copy.wait_send()
    line_a.drain()
    line_f.drain()


def gather_weights(ff_in, a_in, a_rows, vec_in, x_in, n_dp, n_tp):
    width = vec_in.shape[1]
    rows = a_rows
    total = rows + vec_in.shape[0]
    cut = total // 2 // 16 * 16
    anyspace = pl.BlockSpec(memory_space=pl.ANY)
    vmem = pl.BlockSpec(memory_space=pltpu.VMEM)
    return pl.pallas_call(
        functools.partial(gather_kernel, n_dp, n_tp, cut),
        out_shape=(
            jax.ShapeDtypeStruct((n_dp, n_tp) + ff_in.shape, BF),
            jax.ShapeDtypeStruct((n_dp, total, width), BF),
            jax.ShapeDtypeStruct((x_in.shape[1], n_tp * x_in.shape[2], width), BF),
        ),
        in_specs=[anyspace, anyspace, vmem, anyspace],
        out_specs=(anyspace, anyspace, anyspace),
        scratch_shapes=[
            pltpu.VMEM((n_tp,) + a_in.shape, BF),
            pltpu.VMEM((total, width), BF),
            pltpu.VMEM((n_tp * len(Pack(rows, width // n_tp).pieces()), 128, width), BF),
            pltpu.SemaphoreType.DMA((2, n_tp - 1)),
            pltpu.SemaphoreType.DMA((2, n_tp - 1)),
            pltpu.SemaphoreType.DMA((2, n_tp - 1)),
            pltpu.SemaphoreType.DMA((2, n_tp - 1)),
            pltpu.SemaphoreType.DMA((n_tp - 1,)),
            pltpu.SemaphoreType.DMA((n_tp - 1,)),
            pltpu.SemaphoreType.DMA((2 + 2 * n_tp, n_dp - 1)),
            pltpu.SemaphoreType.DMA((2 + 2 * n_tp, n_dp - 1)),
            pltpu.SemaphoreType.DMA((4,)),
        ],
        compiler_params=pltpu.CompilerParams(
            collective_id=0, has_side_effects=True, vmem_limit_bytes=48 * 1024 * 1024
        ),
        name="gather_weights",
    )(ff_in, a_in, vec_in, x_in)


class Fold:
    def __init__(self, part, mine, two, order, own, d, z, send, recv):
        self.part, self.mine, self.two, self.z, self.send, self.recv = part, mine, two, z, send, recv
        self.steps, used = [], 0

        def at(mask):
            index, step = own, 1
            while step <= mask:
                if mask & step:
                    index = flip(index, step)
                step *= 2
            return index

        for t, step in enumerate(order):
            masks = [0]
            for later in order[t + 1 :]:
                masks = masks + [m + later for m in masks]
            moves = [(at(m + step), at(m), used + j) for j, m in enumerate(masks)]
            used += len(moves)
            self.steps.append((flip(d, 2 * step), moves))
        self.stage = 0

    def copies(self, stage):
        target, moves = self.steps[stage]
        return [
            pltpu.make_async_remote_copy(
                src_ref=self.part(self.mine, away),
                dst_ref=self.part(self.two, k),
                send_sem=self.send.at[k],
                recv_sem=self.recv.at[k],
                device_id=(target, self.z),
                device_id_type=MESH,
            )
            for away, _, k in moves
        ]

    def start(self):
        for copy in self.copies(self.stage):
            copy.start()

    def finish(self, add):
        for copy, (_, keep, k) in zip(self.copies(self.stage), self.steps[self.stage][1]):
            copy.wait()
            add(self.part(self.mine, keep), self.part(self.two, k))
        self.stage += 1


class LineSum:
    def __init__(self, mine, got, d, z, n, send, recv):
        self.mine, self.got, self.d, self.z, self.n, self.send, self.recv = mine, got, d, z, n, send, recv

    def _copy(self, way, block):
        return pltpu.make_async_remote_copy(
            src_ref=self.mine(block),
            dst_ref=self.got.at[way, block],
            send_sem=self.send.at[way, block],
            recv_sem=self.recv.at[way, block],
            device_id=(self.d, self.z - 1 if way == 0 else self.z + 1),
            device_id_type=MESH,
        )

    def take(self, block, add):
        z, n = self.z, self.n

        @pl.when((block <= z) & (z < n - 1))
        def _():
            self._copy(0, block).wait_recv()
            add(self.mine(block), self.got.at[0, block])

        @pl.when((block >= z) & (z > 0))
        def _():
            self._copy(1, block).wait_recv()
            add(self.mine(block), self.got.at[1, block])

    def give(self, block):
        @pl.when(block < self.z)
        def _():
            self._copy(0, block).start()

        @pl.when(block > self.z)
        def _():
            self._copy(1, block).start()

    def drain(self, block):
        @pl.when(block < self.z)
        def _():
            self._copy(0, block).wait_send()

        @pl.when(block > self.z)
        def _():
            self._copy(1, block).wait_send()


def scatter_kernel(
    n_dp, n_tp, cut, g0, g1, g2, a0, a1, v_in, x_in, ff_out, a_out, v_out, x_out,
    ff_mine, a_mine, ff_core, a_core, ff_two, a_two, a_cols, ff_got, a_got, v_got, ones,
    load, core_send, core_recv, f_send, f_recv, h_send, h_recv, lf_send, lf_recv, la_send, la_recv,
    z_send, z_recv, s_send, s_recv, v_send, v_recv, local,
):
    d, z = lax.axis_index("dp"), lax.axis_index("tp")
    width = a0.shape[3]
    rows = a0.shape[2] + a1.shape[2]
    layout = Pack(rows, width // n_tp)
    vec = g0.shape[3]
    half = n_dp // 2
    side = d % 2
    own = d // 2
    other = (flip(d, 1), z)
    late = z // (n_tp // 2)
    order = [n_tp - 1 - j + late * (2 * j - n_tp + 1) for j in range(n_tp)]
    greet(d, z, n_dp, n_tp)
    f_core, f_load = [], []
    for j, b in enumerate(order):
        for g, src in enumerate((g0, g1, g2)):
            f_core.append(
                remote(src.at[:, 1 - side, b], ff_core.at[b, :, g], core_send.at[g, j], core_recv.at[g, j], other)
            )
            copy = pltpu.make_async_copy(src.at[:, side, b], ff_mine.at[b, :, g], load.at[g, j])
            copy.start()
            f_load.append(copy)
    a_swap, a_load = [], []
    at = 0
    for g, src in enumerate((a0, a1)):
        part = pl.ds(at, src.shape[2])
        at += src.shape[2]
        a_swap.append(remote(src.at[:, 1 - side], a_core.at[:, part], core_send.at[3, g], core_recv.at[3, g], other))
        copy = pltpu.make_async_copy(src.at[:, side], a_mine.at[:, part], load.at[3, g])
        copy.start()
        a_load.append(copy)
    slot = x_out.shape[2]
    own_x = pltpu.make_async_copy(x_in.at[:, pl.ds(z * slot, slot)], x_out.at[z], local.at[1])
    own_x.start()
    zx = []
    for k in range(1, n_tp):
        peer = lax.rem(z + k, n_tp)
        zx.append(
            remote(x_in.at[:, pl.ds(peer * slot, slot)], x_out.at[z], z_send.at[1, k - 1], z_recv.at[1, k - 1], (d, peer))
        )
    v_out[...] = v_in[...]
    first, second = bit_orders(n_dp)
    for i, step in enumerate([1] + first):
        copy = remote(v_out, v_got.at[i], v_send.at[i], v_recv.at[i], (flip(d, step), z))
        copy.wait()
        v_out[...] += v_got[i]
    v_base = len(first) + 1
    zv = []
    for k in range(1, n_tp):
        peer = lax.rem(z + k, n_tp)
        zv.append(remote(v_out, v_got.at[v_base + k - 1], z_send.at[0, k - 1], z_recv.at[0, k - 1], (d, peer)))
    fill_places(ones, layout, width, n_tp)

    def add_three(dst, src):
        for g in range(3):
            add_rows(dst.at[g], src.at[g])

    ways = ([s // 2 for s in first[::-1]], [s // 2 for s in second[::-1]])
    folds = []
    for j, b in enumerate(order):
        for g in range(3):
            f_load[3 * j + g].wait()
            f_core[3 * j + g].wait_recv()
        for i in range(half):
            add_three(ff_mine.at[b, i], ff_core.at[b, i])
        fold = Fold(
            lambda ref, e, b=b: ref.at[b, e], ff_mine, ff_two, ways[j % 2], own, d, z, f_send.at[j], f_recv.at[j]
        )
        fold.start()
        folds.append(fold)
    for copy in a_load:
        copy.wait()
    for copy in a_swap:
        copy.wait_recv()
    for i in range(half):
        add_rows(a_mine.at[i], a_core.at[i])
    a_folds = [
        Fold(
            lambda ref, e, lo=lo, count=count: ref.at[e, pl.ds(lo, count)],
            a_mine, a_two, ways[h], own, d, z, h_send.at[h], h_recv.at[h],
        )
        for h, (lo, count) in enumerate(((0, cut), (cut, rows - cut)))
    ]
    n_stage = len(ways[0])
    line_f = LineSum(lambda b: ff_mine.at[b, own], ff_got, d, z, n_tp, lf_send, lf_recv)
    line_a = LineSum(lambda b: a_cols.at[b], a_got, d, z, n_tp, la_send, la_recv)
    for t in range(n_stage - 1):
        for fold in folds:
            fold.finish(add_three)
            fold.start()
        if t == 0:
            for fold in a_folds:
                fold.start()
    for j, (fold, b) in enumerate(zip(folds, order)):
        fold.finish(add_three)

        @pl.when(b != z)
        def _(b=b):
            line_f.take(b, add_three)
            line_f.give(b)

    for t in range(1, n_stage):
        for fold in a_folds:
            fold.finish(add_rows)
            fold.start()
    line_f.take(z, add_three)
    put = pltpu.make_async_copy(ff_mine.at[z, own], ff_out.at[d], local.at[0])
    put.start()
    put.wait()
    pieces = [(0, 0, vec, first), (1, 0, vec, second)]
    if vec % 32 == 0:
        pieces += [(2, 0, vec // 2, first), (2, vec // 2, vec // 2, second)]
    else:
        pieces += [(2, 0, vec, first)]
    sf = [
        Spread(lambda s, g=g, lo=lo, n=n: ff_out.at[s, g, pl.ds(lo, n)], way + [1], d, z, s_send.at[i], s_recv.at[i])
        for i, (g, lo, n, way) in enumerate(pieces)
    ]
    for p in sf:
        p.start()
    for fold in a_folds:
        fold.finish(add_rows)
    n_pieces = len(layout.pieces())
    groups = {}
    for i, (packed, low, count, _, _, _) in enumerate(layout.pieces()):
        groups.setdefault((packed, count), []).append((low, i))
    for (packed, count), found in groups.items():
        size = chunk_of(count)

        @pl.loop(0, count // size)
        def _(i, packed=packed, found=found, size=size):
            for s in range(n_tp):
                total = jnp.zeros((size, 128), F32)
                for low, j in found:
                    block = a_mine[own, pl.ds(low + i * size, size)]
                    total += mm_nt(block, ones[s * n_pieces + j])
                a_cols[s, pl.ds(packed + i * size, size)] = total.astype(BF)

    for stage in range(len(first) + 1):
        for p in sf:
            p.wait()
            if stage < len(first):
                p.start()
        if stage == 0:
            for b in order:

                @pl.when(b != z)
                def _(b=b):
                    line_a.take(b, add_rows)
                    line_a.give(b)

    line_a.take(z, add_rows)
    a_out[...] = a_cols[z].astype(F32)
    for copy in zv:
        copy.wait()
    for k in range(1, n_tp):
        v_out[...] += v_got[v_base + k - 1]
    own_x.wait()
    for copy in zx:
        copy.wait_recv()
    for copy in f_core + a_swap + zx:
        copy.wait_send()
    for b in range(n_tp):
        line_f.drain(b)
        line_a.drain(b)
    for p in sf:
        p.drain()


def scatter_grads(ff, a0, a1, vectors, x_in, n_dp, n_tp):
    width = a0.shape[2]
    rows = a0.shape[1] + a1.shape[1]
    vec, hid = ff[0].shape[2:]
    packed = Pack(rows, width // n_tp).total
    cut = rows // 2 // 16 * 16
    half = n_dp // 2
    anyspace = pl.BlockSpec(memory_space=pl.ANY)
    vmem = pl.BlockSpec(memory_space=pltpu.VMEM)
    dma = pltpu.SemaphoreType.DMA
    pairs = lambda v: v.reshape((half, 2) + v.shape[1:])
    most = max(4, n_tp, 2)
    return pl.pallas_call(
        functools.partial(scatter_kernel, n_dp, n_tp, cut),
        out_shape=(
            jax.ShapeDtypeStruct((n_dp, 3, vec, hid), BF),
            jax.ShapeDtypeStruct((packed, 128), F32),
            jax.ShapeDtypeStruct(vectors.shape, F32),
            jax.ShapeDtypeStruct((n_tp, x_in.shape[0], x_in.shape[1] // n_tp, width), BF),
        ),
        in_specs=[anyspace] * 5 + [vmem, anyspace],
        out_specs=(anyspace, vmem, vmem, anyspace),
        scratch_shapes=[
            pltpu.VMEM((n_tp, half, 3, vec, hid), BF),
            pltpu.VMEM((half, rows, width), BF),
            pltpu.VMEM((n_tp, half, 3, vec, hid), BF),
            pltpu.VMEM((half, rows, width), BF),
            pltpu.VMEM((n_tp, half - 1, 3, vec, hid), BF),
            pltpu.VMEM((half - 1, rows, width), BF),
            pltpu.VMEM((n_tp, packed, 128), BF),
            pltpu.VMEM((2, n_tp, 3, vec, hid), BF),
            pltpu.VMEM((2, n_tp, packed, 128), BF),
            pltpu.VMEM(((half - 1).bit_length() + n_tp,) + vectors.shape, F32),
            pltpu.VMEM((n_tp * len(Pack(rows, width // n_tp).pieces()), 128, width), BF),
            dma((4, most)),
            dma((4, most)),
            dma((4, most)),
            dma((n_tp, half - 1)),
            dma((n_tp, half - 1)),
            dma((2, half - 1)),
            dma((2, half - 1)),
            dma((2, n_tp)),
            dma((2, n_tp)),
            dma((2, n_tp)),
            dma((2, n_tp)),
            dma((2, n_tp - 1)),
            dma((2, n_tp - 1)),
            dma((4, n_dp - 1)),
            dma((4, n_dp - 1)),
            dma(((half - 1).bit_length() + 1,)),
            dma(((half - 1).bit_length() + 1,)),
            dma((2,)),
        ],
        compiler_params=pltpu.CompilerParams(
            collective_id=1, has_side_effects=True, vmem_limit_bytes=60 * 1024 * 1024
        ),
        name="scatter_grads",
    )(*[pairs(g) for g in ff], pairs(a0), pairs(a1), vectors, x_in)


def body(
    tokens,
    lengths,
    cotangent,
    norm1_gain,
    norm1_bias,
    in_weight,
    in_bias,
    filter_base,
    filter_mod,
    out_weight,
    out_bias,
    norm2_gain,
    norm2_bias,
    gate_weight,
    up_weight,
    down_weight,
    down_bias,
):
    micro, local, group, width = tokens.shape
    n_tp = lax.axis_size("tp")
    n_dp = lax.axis_size("dp")
    z = lax.axis_index("tp")
    d = lax.axis_index("dp")
    slot_len = local * n_tp
    own = micro * group // n_tp
    per_micro = min(group, own)
    ch = in_weight.shape[2]
    vec = width // n_dp
    hid = gate_weight.shape[1]
    table = jnp.asarray(packed_table(slot_len))
    scale = 0.5 / slot_len

    rows = slot_len // n_dp
    last = n_dp - 1
    upper = d > last - d
    filters = jnp.stack([filter_base, filter_mod])
    across = [(i, (n_dp - i) % n_dp) for i in range(n_dp) if i % (n_dp // 2)] + [(0, n_dp // 2), (n_dp // 2, 0)]
    got = lax.ppermute(filters[:, :, rows:], "dp", [(i, last - i) for i in range(n_dp)])
    got_edge = lax.ppermute(filters[:, :, :1], "dp", across)
    direct = jnp.where(upper, got, filters[:, :, :rows]).astype(F32)
    mirror_lower = jnp.concatenate([got[:, :, 1:], got_edge], axis=2)
    mirror_upper = filters[:, :, 1 : rows + 1]
    mirror = jnp.flip(jnp.where(upper, mirror_upper, mirror_lower), 2).astype(F32)
    nyquist = got_edge[:, 0, 0].astype(F32)
    edge = ((jnp.arange(rows) == 0) & (d == 0))[None, :, None]
    half_real = jnp.where(edge, direct[:, 0], direct[:, 0] + mirror[:, 0])
    half_imag = jnp.where(edge, nyquist[:, None], direct[:, 1] - mirror[:, 1])
    half = jnp.stack([half_real, half_imag], 1).astype(BF).reshape(4 * rows, ch)
    slice_of = [2 * i if 2 * i < n_dp else 2 * (last - i) + 1 for i in range(n_dp)]

    a_in = jnp.concatenate([in_weight.transpose(1, 0, 2).reshape(3 * vec, ch), out_weight.T, half])
    vectors = jnp.stack([norm1_gain, norm1_bias, norm2_gain, norm2_bias, out_bias, down_bias])
    vectors = jnp.concatenate([vectors, in_bias])
    vectors = jnp.pad(vectors, ((0, 16 - 9), (0, width - vec)))
    share = hid // n_dp
    ff_in = jnp.concatenate(
        [
            lax.dynamic_slice_in_dim(gate_weight, d * vec, vec, 0),
            lax.dynamic_slice_in_dim(up_weight, d * vec, vec, 0),
            lax.dynamic_slice_in_dim(down_weight, d * share, share, 0).reshape(vec, hid),
        ]
    )
    x_in = tokens.transpose(0, 2, 1, 3).reshape(n_tp, own, local, width)
    layout = Pack(a_in.shape[0], ch)
    ffw, aw, x_own = gather_weights(ff_in, layout.pack(a_in), a_in.shape[0], vectors, x_in, n_dp, n_tp)
    cotangent, _ = lax.optimization_barrier((cotangent, aw))
    vectors = aw[:, 4 * vec + 4 * rows :, :vec].astype(F32).transpose(1, 0, 2).reshape(16, width)
    slots = [slice_of.index(k) for k in range(n_dp)]
    direct = vec % 16 == 0 and hid == width
    if direct:
        ws = [(ffw, (n_dp, n_tp, vec, hid), g) for g in range(3)]
        a_view = aw
    else:
        natural = [
            ffw[:, :, g * vec : (g + 1) * vec].transpose(1, 0, 2, 3).reshape(n_tp, width, hid) for g in range(2)
        ]
        natural.append(
            ffw[:, :, 2 * vec :].reshape(n_dp, n_tp, share, width).transpose(1, 0, 2, 3).reshape(n_tp, hid, width)
        )
        ws = [(w[None], (1,) + w.shape, 0) for w in natural]
        a_view = aw[:, : 4 * vec].reshape(n_dp, 4, vec, width).transpose(1, 0, 2, 3).reshape(1, 4 * width, width)
    feed_weights = (ws[0][0], ws)

    def to_owner(x):
        pieces = x.transpose(0, 2, 1, 3).reshape(n_tp, own, local, width)
        return lax.all_to_all(pieces, "tp", 0, 1, tiled=False).reshape(own, slot_len, width)

    def to_slots(x):
        pieces = x.reshape(own, n_tp, local, width)
        whole = lax.all_to_all(pieces, "tp", 1, 0, tiled=False)
        return whole.reshape(micro, group, local, width).transpose(0, 2, 1, 3)

    c_own = to_owner(cotangent)
    flat_len = lax.dynamic_slice_in_dim(lengths.reshape(-1), z * own, own, 0)
    first = 4 * vec // rows
    n1, values, gating, nsum, mixing = project(x_own, flat_len, a_view, vectors)
    spec, conv, gated = spectral(values, gating, mixing, flat_len, table, aw, first, rows, slots, scale)
    middle, n2, act, side, hidden, out = feed(x_own, gated, flat_len, a_view, feed_weights, vectors)
    layer_out = to_slots(out)
    e, *d_ff = feed_back(c_own, n2, act, side, hidden, flat_len, feed_weights)
    mg, cg, gtg, d_out, sums = branch_back(e, middle, c_own, gated, gating, conv, flat_len, a_view, vectors)
    layer_out, cg = lax.optimization_barrier((layer_out, cg))
    vg, d_filter, cgv = spectral_back(cg, spec, mixing, flat_len, table, aw, first, rows, slots, scale)
    ig, d_first, sums = input_back(vg, gtg, n1, x_own, mg, nsum, cgv, flat_len, a_view, d_out, sums, vectors)
    if not direct:
        d_ff = [
            g[0].reshape(n_tp, n_dp, vec, hid).transpose(1, 0, 2, 3) for g in d_ff[:2]
        ] + [d_ff[2][0].reshape(n_tp, n_dp, vec, hid).transpose(1, 0, 2, 3)]
        d_first = d_first.reshape(4, n_dp, vec, width).transpose(1, 0, 2, 3).reshape(n_dp, 4 * vec, width)
    ffg, ag, vecs, input_grad = scatter_grads(d_ff, d_first, d_filter, sums, ig, n_dp, n_tp)
    input_grad = input_grad.reshape(micro, group, local, width).transpose(0, 2, 1, 3)
    ag = layout.unpack(ag)
    gate_grad = ffg[:, 0].reshape(width, hid).astype(F32)
    up_grad = ffg[:, 1].reshape(width, hid).astype(F32)
    down_grad = ffg[:, 2].reshape(hid, width).astype(F32)
    in_grad = ag[: 3 * vec].reshape(3, vec, ch).transpose(1, 0, 2)
    out_grad = ag[3 * vec : 4 * vec].T
    fgrad = ag[4 * vec :].astype(BF).reshape(2, 2, rows, ch)
    other = lax.ppermute(fgrad, "dp", [(i, last - i) for i in range(n_dp)])
    low_slice = jnp.where(upper, other, fgrad)
    high_slice = jnp.where(upper, fgrad, other)
    both = jnp.concatenate([low_slice, high_slice], axis=2)
    follow = lax.ppermute(fgrad[:, :, :1], "dp", across)
    zero = jnp.zeros_like(follow[:, 0])
    follow = jnp.where(d == n_dp // 2, jnp.stack([follow[:, 1], zero], 1), follow)
    mirrored = jnp.flip(jnp.concatenate([both[:, :, 1:], follow], axis=2), 2)
    mirrored = jnp.stack([mirrored[:, 0], -mirrored[:, 1]], 1)
    plain = jnp.stack(
        [both[:, 0], jnp.where((d == 0) & (jnp.arange(2 * rows) == 0)[None, :, None], 0.0, both[:, 1].astype(F32)).astype(BF)], 1
    )
    full = jnp.where(upper, mirrored, plain).astype(F32)

    piece = width // (n_dp * n_tp)
    vecs = lax.dynamic_slice_in_dim(vecs, (d * n_tp + z) * piece, piece, 1)
    return (
        layer_out,
        input_grad,
        vecs[0],
        vecs[1],
        in_grad,
        vecs[6:9],
        full[0],
        full[1],
        out_grad,
        vecs[4],
        vecs[2],
        vecs[3],
        gate_grad,
        up_grad,
        down_grad,
        vecs[5],
    )


def solution(mesh):
    in_specs = (
        P(None, "tp", "dp", None),
        P(None, "dp"),
        P(None, "tp", "dp", None),
        P("dp"),
        P("dp"),
        P("dp", None, "tp"),
        P(None, "dp"),
        P(None, "dp", "tp"),
        P(None, "dp", "tp"),
        P("tp", "dp"),
        P("dp"),
        P("dp"),
        P("dp"),
        P(None, "tp"),
        P(None, "tp"),
        P("tp", None),
        P("dp"),
    )
    out_specs = (
        P(None, "tp", "dp", None),
        P(None, "tp", "dp", None),
        P(("dp", "tp")),
        P(("dp", "tp")),
        P("dp", None, "tp"),
        P(None, ("dp", "tp")),
        P(None, "dp", "tp"),
        P(None, "dp", "tp"),
        P("tp", "dp"),
        P(("dp", "tp")),
        P(("dp", "tp")),
        P(("dp", "tp")),
        P(None, "tp"),
        P(None, "tp"),
        P("tp", None),
        P(("dp", "tp")),
    )
    return jax.shard_map(body, mesh=mesh, in_specs=in_specs, out_specs=out_specs, check_vma=False)
```

```python
import functools
import math

import jax
import jax.numpy as jnp
import numpy as np
from jax import lax
from jax.experimental import pallas as pl
from jax.experimental.pallas import tpu as pltpu
from jax.sharding import PartitionSpec as P

EPSILON = 1e-05
ROWS = 64
BF = jnp.bfloat16
F32 = jnp.float32
GELU_A = math.sqrt(2.0 / math.pi)
GELU_B = 0.044715


def packed_table(slot_len):
    frequency = np.arange(slot_len, dtype=np.int64)[:, None]
    position = np.arange(slot_len, dtype=np.int64)[None, :]
    angles = (frequency * position % (2 * slot_len)).astype(np.float32) * np.float32(math.pi / slot_len)
    top = np.cos(angles)
    low = -np.sin(angles)
    low[0] = 1.0 - 2.0 * (np.arange(slot_len) % 2)
    return np.concatenate([top, low]).astype(np.float32).astype(jnp.bfloat16)


def shift(x, axis, step):
    n = lax.axis_size(axis)
    return lax.ppermute(x, axis, [(i, (i + step) % n) for i in range(n)])


def exchange(pieces, place, n):
    out = [(place, lax.dynamic_index_in_dim(pieces, place, 0, keepdims=False))]
    for step in range(1, n):
        block = lax.dynamic_index_in_dim(pieces, (place + step) % n, 0, keepdims=False)
        out.append(((place + n - step) % n, shift(block, "tp", step)))
    return out


def mm(a, b):
    return lax.dot_general(a, b, (((1,), (0,)), ((), ())), preferred_element_type=F32)


def mm_nt(a, b):
    return lax.dot_general(a, b, (((1,), (1,)), ((), ())), preferred_element_type=F32)


def mm_tn(a, b):
    return lax.dot_general(a, b, (((0,), (0,)), ((), ())), preferred_element_type=F32)


def mean_of(v):
    return jnp.sum(v, axis=-1, keepdims=True) * (1.0 / v.shape[-1])


def standardize(v):
    centred = v - mean_of(v)
    inverse = lax.rsqrt(mean_of(centred * centred) + EPSILON)
    return centred * inverse, inverse


def norm_back(e, gain, s, q):
    eg = e * gain
    return q * (eg - mean_of(eg) - s * mean_of(eg * s))


def gelu_parts(v):
    square = v * v
    th = jnp.tanh(v * (GELU_A + (GELU_A * GELU_B) * square))
    rise = 0.5 + 0.5 * th
    act = v * rise
    slope = rise + act * (1.0 - th) * (GELU_A + (3.0 * GELU_A * GELU_B) * square)
    return act, slope


def live(rows, first, count):
    at = lax.broadcasted_iota(jnp.int32, (rows, 1), 0) + first
    return jnp.where(at < count, 1.0, 0.0)


def joined(ref):
    v = ref[...]
    return v.reshape(-1, v.shape[-1])


def two_part_dot(a, b, dims):
    high = a.astype(BF)
    low = (a - high.astype(F32)).astype(BF)
    return lax.dot_general(high, b, (dims, ((), ())), preferred_element_type=F32) + lax.dot_general(
        low, b, (dims, ((), ())), preferred_element_type=F32
    )


def top_row(v, rows=8):
    r = lax.broadcasted_iota(jnp.int32, (rows, v.shape[1]), 0)
    return jnp.where(r == 0, jnp.broadcast_to(v, (rows, v.shape[1])), 0.0)


def project_kernel(tile, lens, x, wv, wg, wc, vec, values, gating, nsum, mixing):
    s, t = pl.program_id(0), pl.program_id(1)
    count = lens[s]
    valid = live(tile, t * tile, count)
    std, _ = standardize(x[0].astype(F32))
    normed = (std * vec[0:1] + vec[1:2]).astype(BF)
    values[0] = ((mm(normed, joined(wv)) + vec[6:7]) * valid).astype(BF)
    gating[0] = (mm(normed, joined(wg)) + vec[7:8]).astype(BF)
    part = top_row(jnp.sum(normed.astype(F32) * valid, axis=0, keepdims=True))

    @pl.when(t == 0)
    def _():
        nsum[0] = part

    @pl.when(t > 0)
    def _():
        nsum[0] += part

    @pl.when(t == pl.num_programs(1) - 1)
    def _():
        length = count.astype(F32)
        cond = two_part_dot(nsum[0], joined(wc), ((1,), (0,))) + length * vec[8:9]
        mixing[0] = jnp.tanh(cond / length)


def filters_of(refs, slots, mix):
    base_r, base_i, mod_r, mod_i = [jnp.concatenate([ref[j] for j in slots]).astype(F32) for ref in refs]
    return base_r + mix * mod_r, base_i + mix * mod_i, mod_r, mod_i


def spectral_kernel(slots, scale, values, gating, mixing, table, f0, f1, f2, f3, spec, conv, gated):
    own = values.shape[0]
    n = values.shape[1]
    raw = [mm(table[...], values[s]) for s in range(own)]
    edge = lax.broadcasted_iota(jnp.int32, (n, 1), 0) == 0
    outs = []
    for s in range(own):
        v = raw[s]
        spec[s] = v.astype(BF)
        sr, si = v[:n], v[n:]
        fr, fi, _, _ = filters_of((f0, f1, f2, f3), slots, mixing[s, 0:1])
        fr2 = jnp.where(edge, fi, fr)
        fi = jnp.where(edge, 0.0, fi)
        prod = jnp.concatenate([(fr * sr - fi * si).astype(BF), (fr2 * si + fi * sr).astype(BF)])
        outs.append(mm_tn(table[...], prod))
    for s in range(own):
        out = outs[s] * scale
        conv[s] = out.astype(BF)
        gated[s] = (out * gating[s].astype(F32)).astype(BF)


def feed_kernel(tile, n_tp, lens, x, gated, w_out, wg, wu, wd, vec, middle, n2, act, side, hidden, out):
    s, t = pl.program_id(0), pl.program_id(1)
    valid = live(tile, t * tile, lens[s])
    mid = x[0].astype(F32) + valid * (mm_nt(gated[0], joined(w_out)) + vec[4:5])
    middle[0] = mid.astype(BF)
    std, _ = standardize(mid)
    normed = (std * vec[2:3] + vec[3:4]).astype(BF)
    n2[0] = normed
    feed = jnp.zeros(mid.shape, F32)
    for p in range(n_tp):
        gate = mm(normed, joined(wg.at[:, p]))
        up = mm(normed, joined(wu.at[:, p]))
        a, slope = gelu_parts(gate)
        act[0, p] = a.astype(BF)
        side[0, p] = (up * slope).astype(BF)
        h = (a * up).astype(BF)
        hidden[0, p] = h
        feed += mm(h, joined(wd.at[:, p]))
    out[:, 0] = (mid + valid * (feed + vec[5:6])).astype(BF).reshape(out.shape[0], out.shape[2], out.shape[3])


def feed_back_kernel(tile, lens, cot, n2, act, side, hidden, wg, wu, wd, e_out, d_gate, d_up, d_down, e_acc, acc_g, acc_u, acc_d, fgs, ggs, ugs):
    p, s = pl.program_id(0), pl.program_id(1)
    n = cot.shape[1]

    @pl.when(p == 0)
    def _():
        e_acc[s] = jnp.zeros(e_acc.shape[1:], F32)

    @pl.when(s == 0)
    def _():
        for acc in (acc_g, acc_u, acc_d):
            acc[...] = jnp.zeros(acc.shape, F32)

    down, gate, up = joined(wd.at[:, 0]), joined(wg.at[:, 0]), joined(wu.at[:, 0])
    for i in range(n // tile):
        here = pl.ds(i * tile, tile)
        fg = (cot[0, here].astype(F32) * live(tile, i * tile, lens[s])).astype(BF)
        fgs[here] = fg
        hg = mm_nt(fg, down)
        ggs[here] = (hg * side[0, 0, here].astype(F32)).astype(BF)
        ugs[here] = (hg * act[0, 0, here].astype(F32)).astype(BF)
    for i in range(n // tile):
        here = pl.ds(i * tile, tile)
        e_acc[s, here] += mm_nt(ggs[here], gate) + mm_nt(ugs[here], up)
    normed = n2[0]
    acc_g[...] += mm_tn(normed, ggs[...])
    acc_u[...] += mm_tn(normed, ugs[...])
    acc_d[...] += mm_tn(hidden[0, 0], fgs[...])

    @pl.when(p == pl.num_programs(0) - 1)
    def _():
        e_out[0] = e_acc[s].astype(BF)

    @pl.when(s == pl.num_programs(1) - 1)
    def _():
        for acc, out in zip((acc_g, acc_u, acc_d), (d_gate, d_up, d_down)):
            out[:, 0] = acc[...].astype(BF).reshape(out.shape[0], out.shape[2], out.shape[3])


def eights(v):
    return jnp.sum(v.reshape(-1, 8, v.shape[-1]), axis=0)


def branch_back_kernel(tile, lens, e, middle, cot, gating, conv, w_out, vec, mg_out, cg, gtg, d_out, sums, acc, bgs, gts, part_sums):
    s, t = pl.program_id(0), pl.program_id(1)
    begin = (s == 0) & (t == 0)
    end = (s == pl.num_programs(0) - 1) & (t == pl.num_programs(1) - 1)

    @pl.when(begin)
    def _():
        acc[...] = jnp.zeros(acc.shape, F32)
        part_sums[...] = jnp.zeros(part_sums.shape, F32)

    count = lens[s]
    gain = vec[2:3]
    step = min(ROWS, tile)
    for i in range(tile // step):
        here = pl.ds(i * step, step)
        valid = live(step, t * tile + i * step, count)
        up = cot[0, here].astype(F32)
        std, inverse = standardize(middle[0, here].astype(F32))
        grad = e[0, here].astype(F32)
        mg = up + norm_back(grad, gain, std, inverse)
        mg_out[0, here] = mg.astype(BF)
        bgr = (mg * valid).astype(BF)
        bgs[here] = bgr
        fg = (up * valid).astype(BF).astype(F32)
        for j, v in enumerate((grad * std, grad, bgr.astype(F32), fg)):
            part_sums[j] += eights(v)
    ggr = mm(bgs[...], joined(w_out))
    for i in range(tile // step):
        here = pl.ds(i * step, step)
        gate, out = gating[0, here].astype(F32), conv[0, here].astype(F32)
        g = ggr[i * step : (i + 1) * step]
        cg[0, here] = (g * gate).astype(BF)
        gtg[0, here] = (g * out).astype(BF)
        gts[here] = (out * gate).astype(BF)
    acc[...] += mm_tn(bgs[...], gts[...])

    @pl.when(end)
    def _():
        d_out[...] = acc[...].astype(BF).reshape(d_out.shape)
        sums[...] = jnp.zeros(sums.shape, F32)
        for j in range(4):
            sums[j : j + 1] = jnp.sum(part_sums[j], axis=0, keepdims=True)


def spectral_back_kernel(slots, scale, lens, cg, spec, mixing, table, f0, f1, f2, f3, vg, fgrad, cgv):
    own = cg.shape[0]
    n = cg.shape[1]
    size = n // len(slots)
    raw = [mm(table[...], cg[s]) for s in range(own)]
    edge = lax.broadcasted_iota(jnp.int32, (n, 1), 0) == 0
    outs, total = [], None
    for s in range(own):
        v = raw[s] * scale
        pr, pi = v[:n], v[n:]
        mix = mixing[s, 0:1]
        fr, fi, mod_r, mod_i = filters_of((f0, f1, f2, f3), slots, mix)
        fr2 = jnp.where(edge, fi, fr)
        fi = jnp.where(edge, 0.0, fi)
        sg = jnp.concatenate([(fr * pr + fi * pi).astype(BF), (fr2 * pi - fi * pr).astype(BF)])
        outs.append(mm_tn(table[...], sg))
        sr, si = spec[s, :n].astype(F32), spec[s, n:].astype(F32)
        both = pi * si
        dr = pr * sr + jnp.where(edge, 0.0, both)
        di = jnp.where(edge, both, pi * sr - pr * si)
        mixg = jnp.sum(mod_r * dr + mod_i * di, axis=0, keepdims=True)
        step = mixg * (1.0 - mix * mix) / lens[s].astype(F32)
        cgv[s] = top_row(step.astype(BF).astype(F32))
        parts = (dr, di, mix * dr, mix * di)
        total = parts if total is None else tuple(t + p for t, p in zip(total, parts))
    for s in range(own):
        vg[s] = (outs[s] * live(n, 0, lens[s])).astype(BF)
    for j in range(len(slots)):
        k = slots.index(j)
        for i in range(4):
            fgrad[j, pl.ds(i * size, size)] = total[i][k * size : (k + 1) * size].astype(BF)


def input_back_kernel(tile, lens, vg, gtg, x, mg, nsum, cgv, wv, wg, wc, d_out, sums_in, vec, ig, d_in, sums, acc_v, acc_g, acc_c):
    s, t = pl.program_id(0), pl.program_id(1)
    begin = (s == 0) & (t == 0)
    end = (s == pl.num_programs(0) - 1) & (t == pl.num_programs(1) - 1)
    count = lens[s]

    @pl.when(begin)
    def _():
        for acc in (acc_v, acc_g, acc_c):
            acc[...] = jnp.zeros(acc.shape, F32)
        sums[...] = jnp.zeros(sums.shape, F32)
        sums[2:6] = sums_in[0:4]

    valid = live(tile, t * tile, count)
    cvec = mm_nt(cgv[0].astype(BF), joined(wc))[0:1]
    vgb, gtb = vg[0], gtg[0]
    e = mm_nt(vgb, joined(wv)) + mm_nt(gtb, joined(wg)) + valid * cvec
    std, inverse = standardize(x[0].astype(F32))
    ig[0] = (mg[0].astype(F32) + norm_back(e, vec[0:1], std, inverse)).astype(BF)
    normed = (std * vec[0:1] + vec[1:2]).astype(BF)
    part_v, part_g = mm_tn(normed, vgb), mm_tn(normed, gtb)
    rows = [e * std, e, vgb.astype(F32), gtb.astype(F32)]
    rows = [jnp.sum(r, axis=0, keepdims=True) for r in rows]

    acc_v[...] += part_v
    acc_g[...] += part_g
    for i, r in zip((0, 1, 6, 7), rows):
        sums[i : i + 1] += r

    @pl.when(t == 0)
    def _():
        acc_c[...] += two_part_dot(nsum[0], cgv[0].astype(BF), ((0,), (0,)))
        sums[8:9] += cgv[0, 0:1] * count.astype(F32)

    @pl.when(end)
    def _():
        r = d_out.shape[1]
        shape = (d_in.shape[0], r, d_in.shape[2])
        for i, acc in enumerate((acc_v, acc_g, acc_c)):
            d_in[:, i * r : (i + 1) * r] = acc[...].astype(BF).reshape(shape)
        d_in[:, 3 * r :] = d_out[...]


def call(kernel, grid, lens, ins, in_specs, outs, out_specs, scratch, flops, name, limit=56):
    spec = pltpu.PrefetchScalarGridSpec(
        num_scalar_prefetch=1, grid=grid, in_specs=in_specs, out_specs=out_specs, scratch_shapes=scratch
    )
    moved = sum(math.prod(v.shape) * v.dtype.itemsize for v in list(ins) + list(outs))
    return pl.pallas_call(
        kernel,
        grid_spec=spec,
        out_shape=tuple(outs),
        compiler_params=pltpu.CompilerParams(
            dimension_semantics=("arbitrary",) * len(grid), vmem_limit_bytes=limit * 1024 * 1024
        ),
        cost_estimate=pl.CostEstimate(flops=int(flops), bytes_accessed=int(moved), transcendentals=0),
        name=name,
    )(lens, *ins)


def once(block, index):
    return pl.BlockSpec(block, lambda *_: index, pipeline_mode=pl.Buffered(1))


def shape_of(shape, dtype):
    return jax.ShapeDtypeStruct(shape, dtype)


def project(x, lens, aw, vec):
    own, n, width = x.shape
    tile = min(512, n)
    nd, r = aw.shape[0], width // aw.shape[0]
    tok = pl.BlockSpec((1, tile, width), lambda s, t, *_: (s, t, 0))
    one = pl.BlockSpec((1, 8, width), lambda s, t, *_: (s, 0, 0))
    weights = [once((nd, r, width), (0, g, 0)) for g in range(3)]
    sd = shape_of(x.shape, BF)
    row = shape_of((own, 8, width), F32)
    return call(
        functools.partial(project_kernel, tile),
        (own, n // tile),
        lens,
        [x, aw, aw, aw, vec],
        [tok] + weights + [once(vec.shape, (0, 0))],
        [sd, sd, row, row],
        (tok, tok, one, one),
        [],
        4 * own * n * width * width,
        "project",
    )


def filter_specs(fw, n_dp, rows, cb, first):
    return [
        pl.BlockSpec((n_dp, rows, cb), lambda *g, i=i: (0, first + i, g[0])) for i in range(4)
    ]


def spectral(values, gating, mixing, lens, table, fw, first, rows, slots, scale):
    own, n, width = values.shape
    cb = min(256, width)
    n_dp = fw.shape[0]
    tok = pl.BlockSpec((own, n, cb), lambda c, *_: (0, 0, c))
    both = pl.BlockSpec((own, 2 * n, cb), lambda c, *_: (0, 0, c))
    one = pl.BlockSpec((own, 8, cb), lambda c, *_: (0, 0, c))

    def kernel(lens, *refs):
        spectral_kernel(slots, scale, *refs)

    return call(
        kernel,
        (width // cb,),
        lens,
        [values, gating, mixing, table] + [fw] * 4,
        [tok, tok, one, once(table.shape, (0, 0))] + filter_specs(fw, n_dp, rows, cb, first),
        [shape_of((own, 2 * n, width), BF), shape_of(values.shape, BF), shape_of(values.shape, BF)],
        (both, tok, tok),
        [],
        8 * own * n * n * width,
        "spectral",
    )


def feed(x, gated, lens, aw, ws, n_tp, hid, vec):
    own, n, width = x.shape
    tile = min(512, n)
    local = n // n_tp
    r = width // aw.shape[0]
    tok = pl.BlockSpec((1, tile, width), lambda s, t, *_: (s, t, 0))
    wide = pl.BlockSpec((1, n_tp, tile, hid), lambda s, t, *_: (s, 0, t, 0))
    parts = pl.BlockSpec((tile // local, 1, local, width), lambda s, t, *_: (t, s, 0, 0))
    big = shape_of((own, n_tp, n, hid), BF)
    return call(
        functools.partial(feed_kernel, tile, n_tp),
        (own, n // tile),
        lens,
        [x, gated, aw] + [w[0] for w in ws] + [vec],
        [tok, tok, once((aw.shape[0], r, width), (0, 3, 0))] + [once(w[1], w[2]) for w in ws] + [once(vec.shape, (0, 0))],
        [shape_of(x.shape, BF), shape_of(x.shape, BF), big, big, big, shape_of((n_tp, own, local, width), BF)],
        (tok, tok, wide, wide, wide, parts),
        [],
        2 * own * n * width * (width + 3 * n_tp * hid),
        "feed",
        limit=60,
    )


def feed_back(cot, n2, act, side, hidden, lens, ffw):
    own, n, width = cot.shape
    n_tp, hid = act.shape[1], act.shape[3]
    tile = min(512, n)
    tok = pl.BlockSpec((1, n, width), lambda p, s, *_: (s, 0, 0))
    wide = pl.BlockSpec((1, 1, n, hid), lambda p, s, *_: (s, p, 0, 0))
    w_specs = [pl.BlockSpec(w[3], lambda p, s, *_, f=w[4]: f(p)) for w in ffw]
    nd = [next(v for v in w[3]) for w in ffw]
    sides = [(width, hid), (width, hid), (hid, width)]
    shapes = [(k, n_tp, a // k, b) for k, (a, b) in zip(nd, sides)]
    d_specs = [pl.BlockSpec((shape[0], 1) + shape[2:], lambda p, s, *_: (0, p, 0, 0)) for shape in shapes]
    d_shapes = [shape_of(shape, BF) for shape in shapes]
    return call(
        functools.partial(feed_back_kernel, tile),
        (n_tp, own),
        lens,
        [cot, n2, act, side, hidden] + [w[0] for w in ffw],
        [tok, tok, wide, wide, wide] + w_specs,
        [shape_of(cot.shape, BF)] + d_shapes,
        (pl.BlockSpec((1, n, width), lambda p, s, *_: (jnp.where(p == n_tp - 1, s, 0), 0, 0)), *d_specs),
        [
            pltpu.VMEM(cot.shape, F32),
            pltpu.VMEM((width, hid), F32),
            pltpu.VMEM((width, hid), F32),
            pltpu.VMEM((hid, width), F32),
            pltpu.VMEM((n, width), BF),
            pltpu.VMEM((n, hid), BF),
            pltpu.VMEM((n, hid), BF),
        ],
        12 * own * n * width * n_tp * hid,
        "feed_back",
        limit=60,
    )


def branch_back(e, middle, cot, gating, conv, lens, aw, vec):
    own, n, width = cot.shape
    tile = min(512, n)
    nd, r = aw.shape[0], width // aw.shape[0]
    tok = pl.BlockSpec((1, tile, width), lambda s, t, *_: (s, t, 0))
    return call(
        functools.partial(branch_back_kernel, tile),
        (own, n // tile),
        lens,
        [e, middle, cot, gating, conv, aw, vec],
        [tok] * 5 + [once((nd, r, width), (0, 3, 0)), once(vec.shape, (0, 0))],
        [
            shape_of(cot.shape, BF),
            shape_of(cot.shape, BF),
            shape_of(cot.shape, BF),
            shape_of((nd, r, width), BF),
            shape_of((8, width), F32),
        ],
        (tok, tok, tok, pl.BlockSpec((nd, r, width), lambda *_: (0, 0, 0)), pl.BlockSpec((8, width), lambda *_: (0, 0))),
        [
            pltpu.VMEM((width, width), F32),
            pltpu.VMEM((tile, width), BF),
            pltpu.VMEM((tile, width), BF),
            pltpu.VMEM((4, 8, width), F32),
        ],
        4 * own * n * width * width,
        "branch_back",
    )


def spectral_back(cg, spec, mixing, lens, table, fw, first, rows, slots, scale):
    own, n, width = cg.shape
    cb = min(256, width)
    n_dp = fw.shape[0]
    tok = pl.BlockSpec((own, n, cb), lambda c, *_: (0, 0, c))
    both = pl.BlockSpec((own, 2 * n, cb), lambda c, *_: (0, 0, c))
    one = pl.BlockSpec((own, 8, cb), lambda c, *_: (0, 0, c))
    return call(
        functools.partial(spectral_back_kernel, slots, scale),
        (width // cb,),
        lens,
        [cg, spec, mixing, table] + [fw] * 4,
        [tok, both, one, once(table.shape, (0, 0))] + filter_specs(fw, n_dp, rows, cb, first),
        [shape_of(cg.shape, BF), shape_of((n_dp, 4 * rows, width), BF), shape_of((own, 8, width), F32)],
        (tok, pl.BlockSpec((n_dp, 4 * rows, cb), lambda c, *_: (0, 0, c)), one),
        [],
        8 * own * n * n * width,
        "spectral_back",
    )


def input_back(vg, gtg, x, mg, nsum, cgv, lens, aw, d_out, sums, vec):
    own, n, width = x.shape
    tile = min(512, n)
    nd, r = aw.shape[0], width // aw.shape[0]
    tok = pl.BlockSpec((1, tile, width), lambda s, t, *_: (s, t, 0))
    one = pl.BlockSpec((1, 8, width), lambda s, t, *_: (s, 0, 0))
    weights = [once((nd, r, width), (0, g, 0)) for g in range(3)]
    return call(
        functools.partial(input_back_kernel, tile),
        (own, n // tile),
        lens,
        [vg, gtg, x, mg, nsum, cgv, aw, aw, aw, d_out, sums, vec],
        [tok] * 4 + [one] * 2 + weights + [once((nd, r, width), (0, 0, 0)), once((8, width), (0, 0)), once(vec.shape, (0, 0))],
        [shape_of(x.shape, BF), shape_of((nd, 4 * r, width), BF), shape_of((16, width), F32)],
        (tok, pl.BlockSpec((nd, 4 * r, width), lambda *_: (0, 0, 0)), pl.BlockSpec((16, width), lambda *_: (0, 0))),
        [pltpu.VMEM((width, width), F32)] * 3,
        8 * own * n * width * width,
        "input_back",
    )


MESH = pl.DeviceIdType.MESH


def flip(index, step):
    return index + step - 2 * step * ((index // step) % 2)


def bit_orders(n_dp):
    bits = [1 << b for b in range(1, (n_dp - 1).bit_length())]
    return bits, bits[::-1]


def greet(d, z, n_dp, n_tp, pairs=False):
    barrier = pltpu.get_barrier_semaphore()
    count = greet_pairs(d, z, n_dp) if pairs else 0
    step = 1
    while step < n_dp:
        pl.semaphore_signal(barrier, inc=1, device_id=(flip(d, step), z), device_id_type=MESH)
        step *= 2
        count += 1
    for k in range(1, n_tp):
        pl.semaphore_signal(barrier, inc=1, device_id=(d, lax.rem(z + k, n_tp)), device_id_type=MESH)
        count += 1
    pl.semaphore_wait(barrier, count)


def across_of(d, n):
    return lax.rem(n - d, n) + (n // 2) * (1 - (d % (n // 2) + n // 2 - 1) // (n // 2)) * (1 - 2 * (d // (n // 2)))


def one_hot(rows, cols, test):
    r = lax.broadcasted_iota(jnp.int32, (rows, cols), 0)
    c = lax.broadcasted_iota(jnp.int32, (rows, cols), 1)
    return jnp.where(test(r, c), 1.0, 0.0).astype(BF)


def greet_pairs(d, z, n_dp):
    barrier = pltpu.get_barrier_semaphore()
    for peer in (n_dp - 1 - d, across_of(d, n_dp)):
        pl.semaphore_signal(barrier, inc=1, device_id=(peer, z), device_id_type=MESH)
    return 2


def remote(src, dst, send, recv, target):
    copy = pltpu.make_async_remote_copy(
        src_ref=src, dst_ref=dst, send_sem=send, recv_sem=recv, device_id=target, device_id_type=MESH
    )
    copy.start()
    return copy


class Pack:
    def __init__(self, rows, ch):
        self.rows, self.ch = rows, ch
        self.main = ch // 128
        self.rest = ch % 128
        self.dense = self.rest == 64 and rows % 32 == 0
        self.tail = 0 if not self.rest else rows // 2 if self.dense else rows
        self.total = self.main * rows + self.tail

    def pack(self, v):
        parts = [v[:, i * 128 : (i + 1) * 128] for i in range(self.main)]
        if self.rest:
            left = v[:, self.main * 128 :]
            if self.dense:
                parts.append(jnp.concatenate([left[: self.tail], left[self.tail :]], axis=1))
            else:
                parts.append(jnp.pad(left, ((0, 0), (0, 128 - self.rest))))
        return jnp.concatenate(parts)

    def unpack(self, v):
        parts = [v[i * self.rows : (i + 1) * self.rows] for i in range(self.main)]
        if self.rest:
            left = v[self.main * self.rows :]
            if self.dense:
                parts.append(jnp.concatenate([left[:, :64], left[:, 64:]]))
            else:
                parts.append(left[:, : self.rest])
        return jnp.concatenate(parts, axis=1)

    def pieces(self):
        out = [(i * self.rows, 0, self.rows, 0, 128, i * 128) for i in range(self.main)]
        at = self.main * self.rows
        if self.dense:
            out += [(at, 0, self.tail, 0, 64, self.main * 128), (at, self.tail, self.tail, 64, 64, self.main * 128)]
        elif self.rest:
            out += [(at, 0, self.rows, 0, self.rest, self.main * 128)]
        return out


def lanes_to(width, lane, lanes, column):
    r = lax.broadcasted_iota(jnp.int32, (128, width), 0)
    c = lax.broadcasted_iota(jnp.int32, (128, width), 1)
    inside = (r >= lane) & (r < lane + lanes)
    return jnp.where(inside & (c - r == column - lane), 1.0, 0.0).astype(BF)


def fill_places(ones, layout, width, n_tp):
    pieces = layout.pieces()
    for s in range(n_tp):
        for i, (_, _, _, lane, lanes, column) in enumerate(pieces):
            ones[s * len(pieces) + i] = lanes_to(width, lane, lanes, s * layout.ch + column)


class Line:
    def __init__(self, part, d, z, n, send, recv):
        self.part, self.d, self.z, self.n, self.send, self.recv = part, d, z, n, send, recv

    def _copy(self, way, t, block):
        target = (self.d, self.z + 1 if way == 0 else self.z - 1)
        return pltpu.make_async_remote_copy(
            src_ref=self.part(block),
            dst_ref=self.part(block),
            send_sem=self.send.at[way, t],
            recv_sem=self.recv.at[way, t],
            device_id=target,
            device_id_type=MESH,
        )

    def start(self, t):
        z, n = self.z, self.n

        @pl.when((z >= t) & (z < n - 1))
        def _():
            self._copy(0, t, z - t).start()

        @pl.when((z + t < n) & (z > 0))
        def _():
            self._copy(1, t, z + t).start()

    def wait(self, t):
        z, n = self.z, self.n

        @pl.when(z >= t + 1)
        def _():
            self._copy(0, t, z - 1 - t).wait_recv()

        @pl.when(z + t + 1 < n)
        def _():
            self._copy(1, t, z + 1 + t).wait_recv()

    def drain(self):
        z, n = self.z, self.n
        for t in range(n - 1):

            @pl.when((z >= t) & (z < n - 1))
            def _(t=t):
                self._copy(0, t, z - t).wait_send()

            @pl.when((z + t < n) & (z > 0))
            def _(t=t):
                self._copy(1, t, z + t).wait_send()


class Spread:
    def __init__(self, part, order, d, z, send, recv):
        self.part, self.z, self.send, self.recv = part, z, send, recv
        held, self.steps, used = [d], [], 0
        for step in order:
            self.steps.append((flip(d, step), [(slot, used + i) for i, slot in enumerate(held)]))
            used += len(held)
            held = held + [flip(slot, step) for slot in held]
        self.stage = 0

    def copies(self, stage):
        target, sent = self.steps[stage]
        return [
            pltpu.make_async_remote_copy(
                src_ref=self.part(slot),
                dst_ref=self.part(slot),
                send_sem=self.send.at[i],
                recv_sem=self.recv.at[i],
                device_id=(target, self.z),
                device_id_type=MESH,
            )
            for slot, i in sent
        ]

    def start(self):
        for copy in self.copies(self.stage):
            copy.start()

    def wait(self):
        for copy in self.copies(self.stage):
            copy.wait_recv()
        self.stage += 1

    def drain(self):
        for stage in range(len(self.steps)):
            for copy in self.copies(stage):
                copy.wait_send()


def chunk_of(rows):
    return next((c for c in (128, 96, 64, 48, 32, 16) if rows % c == 0), rows)


def add_rows(dst, src):
    rows = dst.shape[0]
    size = chunk_of(rows)

    @pl.loop(0, rows // size)
    def _(i):
        at = pl.ds(i * size, size)
        dst[at] = (dst[at].astype(F32) + src[at].astype(F32)).astype(BF)


def lane_place(rows, cols, offset):
    r = lax.broadcasted_iota(jnp.int32, (rows, cols), 0)
    c = lax.broadcasted_iota(jnp.int32, (rows, cols), 1)
    return jnp.where(c - r == offset, 1.0, 0.0).astype(BF)


def gather_kernel(
    n_dp, n_tp, cut, a_rows, mirror, w0, w1, w2, a_in, f_in, vec_in, x_in, ff_out, a_out, x_out, a_z, a_nat, ones, f_got, f_edge,
    la_send, la_recv, lf_send, lf_recv, x_send, x_recv, s_send, s_recv, f_send, f_recv, local,
):
    d, z = lax.axis_index("dp"), lax.axis_index("tp")
    width = a_nat.shape[1]
    ch = width // n_tp
    rows = a_nat.shape[0] - vec_in.shape[0]
    layout = Pack(a_rows, ch)
    own_ff = [pltpu.make_async_copy(w, ff_out.at[:, z, g], local.at[3 + g]) for g, w in enumerate((w0, w1, w2))]
    for copy in own_ff:
        copy.start()
    own_a = pltpu.make_async_copy(a_in, a_z.at[z, pl.ds(0, layout.total)], local.at[1])
    own_a.start()
    greet(d, z, n_dp, n_tp, mirror)
    if mirror:
        k = f_in.shape[2] // 2
        swaps = [
            remote(f_in.at[:, :, pl.ds(k, k)], f_got, f_send.at[0], f_recv.at[0], (n_dp - 1 - d, z)),
            remote(f_in.at[:, :, pl.ds(0, k)], f_edge, f_send.at[1], f_recv.at[1], (across_of(d, n_dp), z)),
        ]
        turn = one_hot(k, k, lambda r, c: r + c == k)
        corner = one_hot(k, k, lambda r, c: r + c == 0)
        upper = d > n_dp - 1 - d
        lane = lax.broadcasted_iota(jnp.int32, (1, k), 1)
        special = jnp.logical_and(lane == 0, d == 0)
        for copy in swaps:
            copy.wait()
        sums = []
        for c in range(4):
            low, high = f_in[c, :, :k], f_in[c, :, k:]
            direct = jnp.where(upper, f_got[c], low).astype(F32)
            image = mm(jnp.where(upper, low, f_got[c]), turn) + mm(jnp.where(upper, high, f_edge[c]), corner)
            if c % 2 == 0:
                nyquist = image
                folded = jnp.where(special, direct, direct + image)
            else:
                folded = jnp.where(special, nyquist, direct - image)
            a_z[z, pl.ds(layout.total + c * ch, ch)] = folded.astype(BF)
    line_a = Line(lambda s: a_z.at[s], d, z, n_tp, la_send, la_recv)
    line_f = Line(lambda s: ff_out.at[d, s], d, z, n_tp, lf_send, lf_recv)
    first, second = bit_orders(n_dp)
    vec = w0.shape[1]

    def block_spreads(block):
        out = []
        for h, order in enumerate((first, second)):
            at = 2 + 2 * block + h
            if vec % 32 == 0:
                part = lambda s, h=h: ff_out.at[s, block, :, pl.ds(h * (vec // 2), vec // 2)]
            else:
                part = lambda s, h=h: ff_out.at[s, block, pl.ds(h, 1 + h)]
            out.append(Spread(part, order + [1], d, z, s_send.at[at], s_recv.at[at]))
        return out

    own_a.wait()
    line_a.start(0)
    fill_places(ones, layout, width, n_tp)
    for t in range(n_tp - 1):
        line_a.wait(t)
        if t + 1 < n_tp - 1:
            line_a.start(t + 1)
    for copy in own_ff:
        copy.wait()
    line_f.start(0)
    half_rows = a_rows // 2
    n_pieces = len(layout.pieces())
    size = chunk_of(half_rows)
    for side in range(2):
        found = []
        for j, (packed, low, count, _, _, _) in enumerate(layout.pieces()):
            if low <= side * half_rows < low + count:
                found.append((packed + side * half_rows - low, j))

        @pl.loop(0, half_rows // size)
        def _(i, found=found, side=side):
            total = jnp.zeros((size, width), F32)
            for s in range(n_tp):
                for packed, j in found:
                    total += mm(a_z[s, pl.ds(packed + i * size, size)], ones[s * n_pieces + j])
            a_nat[pl.ds(side * half_rows + i * size, size)] = total.astype(BF)

    if mirror:
        for c in range(4):
            total = jnp.zeros((k, width), F32)
            for s in range(n_tp):
                place = one_hot(ch, width, lambda r, col, s=s: col - r == s * ch)
                total += mm_tn(a_z[s, pl.ds(layout.total + c * ch, ch)], place)
            a_nat[pl.ds(a_rows + c * k, k)] = total.astype(BF)
    a_nat[rows:] = vec_in[...]
    put = pltpu.make_async_copy(a_nat, a_out.at[d], local.at[2])
    put.start()
    put.wait()
    total_rows = a_nat.shape[0]
    sa = [
        Spread(lambda s: a_out.at[s, pl.ds(0, cut)], first + [1], d, z, s_send.at[0], s_recv.at[0]),
        Spread(lambda s: a_out.at[s, pl.ds(cut, total_rows - cut)], second + [1], d, z, s_send.at[1], s_recv.at[1]),
    ]
    for p in sa:
        p.start()
    stages = len(first) + 1

    def advance(group):
        for p in group:
            p.wait()
            if p.stage < stages:
                p.start()

    blocks = []
    for t in range(n_tp - 1):
        line_f.wait(t)
        if t + 1 < n_tp - 1:
            line_f.start(t + 1)
        for exists, block in ((z >= t + 1, z - 1 - t), (z + t + 1 < n_tp, z + 1 + t)):
            group = block_spreads(block)
            blocks.append((exists, group))

            @pl.when(exists)
            def _(group=group):
                for p in group:
                    p.start()

        if t == 0:
            advance(sa)
    size = x_in.shape[2]
    here = pl.ds(z * size, size)
    own_x = pltpu.make_async_copy(x_in.at[z], x_out.at[:, here], local.at[0])
    own_x.start()
    zx = []
    for k in range(1, n_tp):
        peer = lax.rem(z + k, n_tp)
        zx.append(remote(x_in.at[peer], x_out.at[:, here], x_send.at[k - 1], x_recv.at[k - 1], (d, peer)))
    for stage in range(stages):
        for exists, group in blocks:

            @pl.when(exists)
            def _(group=group):
                advance(group)

        if stage + 1 < stages:
            advance(sa)
    for p in sa:
        p.drain()
    for exists, group in blocks:

        @pl.when(exists)
        def _(group=group):
            for p in group:
                p.drain()

    own_x.wait()
    for copy in zx:
        copy.wait_recv()
    for copy in zx:
        copy.wait_send()
    line_a.drain()
    line_f.drain()


def gather_weights(ff, a_in, a_rows, f_in, vec_in, x_in, n_dp, n_tp):
    width = vec_in.shape[1]
    mirror = f_in.shape[2] % 256 == 0
    ch = width // n_tp
    rows = a_rows + (2 * f_in.shape[2] if mirror else 0)
    k = f_in.shape[2] // 2
    total = rows + vec_in.shape[0]
    cut = total // 2 // 16 * 16
    anyspace = pl.BlockSpec(memory_space=pl.ANY)
    vmem = pl.BlockSpec(memory_space=pltpu.VMEM)
    return pl.pallas_call(
        functools.partial(gather_kernel, n_dp, n_tp, cut, a_rows, mirror),
        out_shape=(
            jax.ShapeDtypeStruct((n_dp, n_tp, 3) + ff[0].shape[1:], BF),
            jax.ShapeDtypeStruct((n_dp, total, width), BF),
            jax.ShapeDtypeStruct((x_in.shape[1], n_tp * x_in.shape[2], width), BF),
        ),
        in_specs=[anyspace] * 4 + [vmem, vmem, anyspace],
        out_specs=(anyspace, anyspace, anyspace),
        scratch_shapes=[
            pltpu.VMEM((n_tp, a_in.shape[0] + (4 * ch if mirror else 0), 128), BF),
            pltpu.VMEM((total, width), BF),
            pltpu.VMEM((n_tp * len(Pack(a_rows, ch).pieces()), 128, width), BF),
            pltpu.VMEM((4, ch, k), BF),
            pltpu.VMEM((4, ch, k), BF),
            pltpu.SemaphoreType.DMA((2, n_tp - 1)),
            pltpu.SemaphoreType.DMA((2, n_tp - 1)),
            pltpu.SemaphoreType.DMA((2, n_tp - 1)),
            pltpu.SemaphoreType.DMA((2, n_tp - 1)),
            pltpu.SemaphoreType.DMA((n_tp - 1,)),
            pltpu.SemaphoreType.DMA((n_tp - 1,)),
            pltpu.SemaphoreType.DMA((2 + 2 * n_tp, n_dp - 1)),
            pltpu.SemaphoreType.DMA((2 + 2 * n_tp, n_dp - 1)),
            pltpu.SemaphoreType.DMA((2,)),
            pltpu.SemaphoreType.DMA((2,)),
            pltpu.SemaphoreType.DMA((6,)),
        ],
        compiler_params=pltpu.CompilerParams(
            collective_id=0, has_side_effects=True, vmem_limit_bytes=48 * 1024 * 1024
        ),
        name="gather_weights",
    )(*ff, a_in, f_in, vec_in, x_in)


class Fold:
    def __init__(self, part, mine, two, order, own, d, z, send, recv):
        self.part, self.mine, self.two, self.z, self.send, self.recv = part, mine, two, z, send, recv
        self.steps, used = [], 0

        def at(mask):
            index, step = own, 1
            while step <= mask:
                if mask & step:
                    index = flip(index, step)
                step *= 2
            return index

        for t, step in enumerate(order):
            masks = [0]
            for later in order[t + 1 :]:
                masks = masks + [m + later for m in masks]
            moves = [(at(m + step), at(m), used + j) for j, m in enumerate(masks)]
            used += len(moves)
            self.steps.append((flip(d, 2 * step), moves))
        self.stage = 0

    def copies(self, stage):
        target, moves = self.steps[stage]
        return [
            pltpu.make_async_remote_copy(
                src_ref=self.part(self.mine, away),
                dst_ref=self.part(self.two, k),
                send_sem=self.send.at[k],
                recv_sem=self.recv.at[k],
                device_id=(target, self.z),
                device_id_type=MESH,
            )
            for away, _, k in moves
        ]

    def start(self):
        for copy in self.copies(self.stage):
            copy.start()

    def finish(self, add):
        for copy, (_, keep, k) in zip(self.copies(self.stage), self.steps[self.stage][1]):
            copy.wait()
            add(self.part(self.mine, keep), self.part(self.two, k))
        self.stage += 1


class LineSum:
    def __init__(self, mine, got, d, z, n, send, recv):
        self.mine, self.got, self.d, self.z, self.n, self.send, self.recv = mine, got, d, z, n, send, recv

    def _copy(self, way, block):
        return pltpu.make_async_remote_copy(
            src_ref=self.mine(block),
            dst_ref=self.got(way, block),
            send_sem=self.send.at[way, block],
            recv_sem=self.recv.at[way, block],
            device_id=(self.d, self.z - 1 if way == 0 else self.z + 1),
            device_id_type=MESH,
        )

    def take(self, block, add):
        z, n = self.z, self.n

        @pl.when((block <= z) & (z < n - 1))
        def _():
            self._copy(0, block).wait_recv()
            add(self.mine(block), self.got(0, block))

        @pl.when((block >= z) & (z > 0))
        def _():
            self._copy(1, block).wait_recv()
            add(self.mine(block), self.got(1, block))

    def give(self, block):
        @pl.when(block < self.z)
        def _():
            self._copy(0, block).start()

        @pl.when(block > self.z)
        def _():
            self._copy(1, block).start()

    def drain(self, block):
        @pl.when(block < self.z)
        def _():
            self._copy(0, block).wait_send()

        @pl.when(block > self.z)
        def _():
            self._copy(1, block).wait_send()


def scatter_kernel(
    n_dp, n_tp, cut, mirror, g0, g1, g2, a0, a1, v_in, x_in, ff_out, a_out, f_out, v_out, x_out,
    ff_mine, a_mine, ff_core, a_core, ff_two, a_two, a_cols, ff_got, a_got, v_got, ones, f_own, f_got, f_edge,
    load, core_send, core_recv, f_send, f_recv, h_send, h_recv, lf_send, lf_recv, la_send, la_recv, lb_send, lb_recv,
    z_send, z_recv, s_send, s_recv, v_send, v_recv, f_swap_send, f_swap_recv, local,
):
    d, z = lax.axis_index("dp"), lax.axis_index("tp")
    width = a0.shape[3]
    rows = a0.shape[2] + a1.shape[2]
    ch = width // n_tp
    a_rows = a0.shape[2] if mirror else rows
    layout = Pack(a_rows, ch)
    vec = g0.shape[3]
    half = n_dp // 2
    side = d % 2
    own = d // 2
    other = (flip(d, 1), z)
    late = z // (n_tp // 2)
    order = [n_tp - 1 - j + late * (2 * j - n_tp + 1) for j in range(n_tp)]
    greet(d, z, n_dp, n_tp, mirror)
    f_core, f_load, a_swap, a_load = [], [], [], []

    def swap_a(g, src, at):
        part = pl.ds(at, src.shape[2])
        a_swap.append(remote(src.at[:, 1 - side], a_core.at[:, part], core_send.at[3, g], core_recv.at[3, g], other))
        copy = pltpu.make_async_copy(src.at[:, side], a_mine.at[:, part], load.at[3, g])
        copy.start()
        a_load.append(copy)

    swap_a(1, a1, a0.shape[2])
    for j, b in enumerate(order):
        for g, src in enumerate((g0, g1, g2)):
            f_core.append(
                remote(src.at[:, 1 - side, b], ff_core.at[b, :, g], core_send.at[g, j], core_recv.at[g, j], other)
            )
            copy = pltpu.make_async_copy(src.at[:, side, b], ff_mine.at[b, :, g], load.at[g, j])
            copy.start()
            f_load.append(copy)
    swap_a(0, a0, 0)
    slot = x_out.shape[2]
    own_x = pltpu.make_async_copy(x_in.at[:, pl.ds(z * slot, slot)], x_out.at[z], local.at[1])
    own_x.start()
    zx = []
    for k in range(1, n_tp):
        peer = lax.rem(z + k, n_tp)
        zx.append(
            remote(x_in.at[:, pl.ds(peer * slot, slot)], x_out.at[z], z_send.at[1, k - 1], z_recv.at[1, k - 1], (d, peer))
        )
    v_out[...] = v_in[...]
    first, second = bit_orders(n_dp)
    for i, step in enumerate([1] + first):
        copy = remote(v_out, v_got.at[i], v_send.at[i], v_recv.at[i], (flip(d, step), z))
        copy.wait()
        v_out[...] += v_got[i]
    v_base = len(first) + 1
    zv = []
    for k in range(1, n_tp):
        peer = lax.rem(z + k, n_tp)
        zv.append(remote(v_out, v_got.at[v_base + k - 1], z_send.at[0, k - 1], z_recv.at[0, k - 1], (d, peer)))
    fill_places(ones, layout, width, n_tp)

    def add_three(dst, src):
        for g in range(3):
            add_rows(dst.at[g], src.at[g])

    ways = ([s // 2 for s in first[::-1]], [s // 2 for s in second[::-1]])
    n_stage = len(ways[0])
    held = layout.total

    def a_ready(i):
        a_load[i].wait()
        a_swap[i].wait_recv()
        src = (a1, a0)[i]
        part = pl.ds(0 if i else a0.shape[2], src.shape[2])
        for e in range(half):
            add_rows(a_mine.at[e, part], a_core.at[e, part])

    def a_group(base, count, at):
        cut = count // 2 // 16 * 16
        return [
            Fold(
                lambda ref, e, lo=lo, size=size: ref.at[e, pl.ds(lo, size)],
                a_mine, a_two, ways[h], own, d, z, h_send.at[at + h], h_recv.at[at + h],
            )
            for h, (lo, size) in enumerate(((base, cut), (base + cut, count - cut)))
        ]

    def start(group):
        for p in group:
            p.start()

    def step(group, add):
        for fold in group:
            fold.finish(add)
            if fold.stage < n_stage:
                fold.start()

    a_ready(0)
    side_folds = a_group(a_rows, rows - a_rows, 2) if mirror else []
    start(side_folds)
    folds = []
    for j, b in enumerate(order):
        for g in range(3):
            f_load[3 * j + g].wait()
            f_core[3 * j + g].wait_recv()
        for i in range(half):
            add_three(ff_mine.at[b, i], ff_core.at[b, i])
        fold = Fold(
            lambda ref, e, b=b: ref.at[b, e], ff_mine, ff_two, ways[j % 2], own, d, z, f_send.at[j], f_recv.at[j]
        )
        fold.start()
        folds.append(fold)
    a_ready(1)
    main_folds = a_group(0, a_rows, 0)
    line_f = LineSum(lambda b: ff_mine.at[b, own], lambda w, b: ff_got.at[w, b], d, z, n_tp, lf_send, lf_recv)
    line_a = LineSum(
        lambda b: a_cols.at[b, pl.ds(0, held)], lambda w, b: a_got.at[w, b, pl.ds(0, held)], d, z, n_tp, la_send, la_recv
    )
    line_b = LineSum(
        lambda b: a_cols.at[b, pl.ds(held, 4 * ch)],
        lambda w, b: a_got.at[w, b, pl.ds(held, 4 * ch)],
        d, z, n_tp, lb_send, lb_recv,
    )

    def pass_on(line, b, add):
        @pl.when(b != z)
        def _():
            line.take(b, add)
            line.give(b)

    for t in range(n_stage - 1):
        step(side_folds, add_rows)
        step(folds, add_three)
        if t == 0:
            start(main_folds)
    if mirror:
        step(side_folds, add_rows)
        k = a1.shape[2] // 4
        for s in range(n_tp):
            place = one_hot(ch, width, lambda r, col, s=s: col - r == s * ch)
            for c in range(4):
                block = a_mine[own, pl.ds(a_rows + c * k, k)]
                a_cols[s, pl.ds(held + c * ch, ch)] = mm_nt(place, block).astype(BF)
        for b in order:
            pass_on(line_b, b, add_rows)
    for fold, b in zip(folds, order):
        fold.finish(add_three)
        pass_on(line_f, b, add_three)
    swaps = []
    if mirror:
        line_b.take(z, add_rows)
        for c in range(4):
            f_own[c] = a_cols[z, pl.ds(held + c * ch, ch)]
        swaps.append(remote(f_own, f_got, f_swap_send.at[0], f_swap_recv.at[0], (n_dp - 1 - d, z)))
        swaps.append(remote(f_own, f_edge, f_swap_send.at[1], f_swap_recv.at[1], (across_of(d, n_dp), z)))
    for t in range(1, n_stage):
        step(main_folds, add_rows)
    line_f.take(z, add_three)
    put = pltpu.make_async_copy(ff_mine.at[z, own], ff_out.at[d], local.at[0])
    put.start()
    put.wait()
    pieces = [(0, 0, vec, first), (1, 0, vec, second)]
    if vec % 32 == 0:
        pieces += [(2, 0, vec // 2, first), (2, vec // 2, vec // 2, second)]
    else:
        pieces += [(2, 0, vec, first)]
    sf = [
        Spread(lambda s, g=g, lo=lo, n=n: ff_out.at[s, g, pl.ds(lo, n)], way + [1], d, z, s_send.at[i], s_recv.at[i])
        for i, (g, lo, n, way) in enumerate(pieces)
    ]
    start(sf)
    step(main_folds, add_rows)
    n_pieces = len(layout.pieces())
    groups = {}
    for i, (packed, low, count, _, _, _) in enumerate(layout.pieces()):
        groups.setdefault((packed, count), []).append((low, i))
    for (packed, count), found in groups.items():
        size = chunk_of(count)

        @pl.loop(0, count // size)
        def _(i, packed=packed, found=found, size=size):
            for s in range(n_tp):
                total = jnp.zeros((size, 128), F32)
                for low, j in found:
                    block = a_mine[own, pl.ds(low + i * size, size)]
                    total += mm_nt(block, ones[s * n_pieces + j])
                a_cols[s, pl.ds(packed + i * size, size)] = total.astype(BF)

    for stage in range(len(first) + 1):
        for p in sf:
            p.wait()
            if stage < len(first):
                p.start()
        if stage == 0:
            for b in order:
                pass_on(line_a, b, add_rows)

    line_a.take(z, add_rows)
    if mirror:
        upper = d > n_dp - 1 - d
        turn_low = one_hot(k, 2 * k, lambda r, col: r + col == 2 * k)
        turn_high = one_hot(k, 2 * k, lambda r, col: r + k + col == 2 * k)
        corner = one_hot(k, 2 * k, lambda r, col: r + col == 0)
        stay_low = one_hot(k, 2 * k, lambda r, col: r == col)
        stay_high = one_hot(k, 2 * k, lambda r, col: r + k == col)
        lane = lax.broadcasted_iota(jnp.int32, (1, 2 * k), 1)
        zero_at = jnp.logical_and(lane == 0, d == 0)
        for copy in swaps:
            copy.wait()
        for c in range(4):
            low, high = jnp.where(upper, f_got[c], f_own[c]), jnp.where(upper, f_own[c], f_got[c])
            plain = mm(low, stay_low) + mm(high, stay_high)
            if c % 2 == 0:
                edge = jnp.where(d == n_dp // 2, f_edge[c + 1], f_edge[c])
                turned = mm(low, turn_low) + mm(high, turn_high) + mm(edge, corner)
            else:
                plain = jnp.where(zero_at, 0.0, plain)
                edge = jnp.where(d == n_dp // 2, 0.0, f_edge[c].astype(F32)).astype(BF)
                turned = -(mm(low, turn_low) + mm(high, turn_high) + mm(edge, corner))
            f_out[c] = jnp.where(upper, turned, plain)
    a_out[...] = a_cols[z, pl.ds(0, layout.total)].astype(F32)
    for copy in zv:
        copy.wait()
    for k in range(1, n_tp):
        v_out[...] += v_got[v_base + k - 1]
    own_x.wait()
    for copy in zx:
        copy.wait_recv()
    for copy in f_core + a_swap + zx:
        copy.wait_send()
    for b in range(n_tp):
        line_f.drain(b)
        line_a.drain(b)
        if mirror:
            line_b.drain(b)
    for p in sf:
        p.drain()


def scatter_grads(ff, a0, a1, vectors, x_in, n_dp, n_tp):
    width = a0.shape[2]
    rows = a0.shape[1] + a1.shape[1]
    vec, hid = ff[0].shape[2:]
    ch = width // n_tp
    k = a1.shape[1] // 4
    mirror = k % 128 == 0
    a_rows = a0.shape[1] if mirror else rows
    held = Pack(a_rows, ch).total
    packed = held + (4 * ch if mirror else 0)
    cut = rows // 2 // 16 * 16
    half = n_dp // 2
    anyspace = pl.BlockSpec(memory_space=pl.ANY)
    vmem = pl.BlockSpec(memory_space=pltpu.VMEM)
    dma = pltpu.SemaphoreType.DMA
    pairs = lambda v: v.reshape((half, 2) + v.shape[1:])
    most = max(4, n_tp, 2)
    return pl.pallas_call(
        functools.partial(scatter_kernel, n_dp, n_tp, cut, mirror),
        out_shape=(
            jax.ShapeDtypeStruct((n_dp, 3, vec, hid), BF),
            jax.ShapeDtypeStruct((held, 128), F32),
            jax.ShapeDtypeStruct((4, ch, 2 * k), F32),
            jax.ShapeDtypeStruct(vectors.shape, F32),
            jax.ShapeDtypeStruct((n_tp, x_in.shape[0], x_in.shape[1] // n_tp, width), BF),
        ),
        in_specs=[anyspace] * 5 + [vmem, anyspace],
        out_specs=(anyspace, vmem, vmem, vmem, anyspace),
        scratch_shapes=[
            pltpu.VMEM((n_tp, half, 3, vec, hid), BF),
            pltpu.VMEM((half, rows, width), BF),
            pltpu.VMEM((n_tp, half, 3, vec, hid), BF),
            pltpu.VMEM((half, rows, width), BF),
            pltpu.VMEM((n_tp, half - 1, 3, vec, hid), BF),
            pltpu.VMEM((half - 1, rows, width), BF),
            pltpu.VMEM((n_tp, packed, 128), BF),
            pltpu.VMEM((2, n_tp, 3, vec, hid), BF),
            pltpu.VMEM((2, n_tp, packed, 128), BF),
            pltpu.VMEM(((half - 1).bit_length() + n_tp,) + vectors.shape, F32),
            pltpu.VMEM((n_tp * len(Pack(a_rows, ch).pieces()), 128, width), BF),
            pltpu.VMEM((4, ch, k), BF),
            pltpu.VMEM((4, ch, k), BF),
            pltpu.VMEM((4, ch, k), BF),
            dma((4, most)),
            dma((4, most)),
            dma((4, most)),
            dma((n_tp, half - 1)),
            dma((n_tp, half - 1)),
            dma((4, half - 1)),
            dma((4, half - 1)),
            dma((2, n_tp)),
            dma((2, n_tp)),
            dma((2, n_tp)),
            dma((2, n_tp)),
            dma((2, n_tp)),
            dma((2, n_tp)),
            dma((2, n_tp - 1)),
            dma((2, n_tp - 1)),
            dma((4, n_dp - 1)),
            dma((4, n_dp - 1)),
            dma(((half - 1).bit_length() + 1,)),
            dma(((half - 1).bit_length() + 1,)),
            dma((2,)),
            dma((2,)),
            dma((2,)),
        ],
        compiler_params=pltpu.CompilerParams(
            collective_id=1, has_side_effects=True, vmem_limit_bytes=60 * 1024 * 1024
        ),
        name="scatter_grads",
    )(*[pairs(g) for g in ff], pairs(a0), pairs(a1), vectors, x_in)


def body(
    tokens,
    lengths,
    cotangent,
    norm1_gain,
    norm1_bias,
    in_weight,
    in_bias,
    filter_base,
    filter_mod,
    out_weight,
    out_bias,
    norm2_gain,
    norm2_bias,
    gate_weight,
    up_weight,
    down_weight,
    down_bias,
):
    micro, local, group, width = tokens.shape
    n_tp = lax.axis_size("tp")
    n_dp = lax.axis_size("dp")
    z = lax.axis_index("tp")
    d = lax.axis_index("dp")
    slot_len = local * n_tp
    own = micro * group // n_tp
    per_micro = min(group, own)
    ch = in_weight.shape[2]
    vec = width // n_dp
    hid = gate_weight.shape[1]
    table = jnp.asarray(packed_table(slot_len))
    scale = 0.5 / slot_len

    rows = slot_len // n_dp
    last = n_dp - 1
    upper = d > last - d
    mirror = rows % 128 == 0
    filters = jnp.stack([filter_base, filter_mod])
    across = [(i, (n_dp - i) % n_dp) for i in range(n_dp) if i % (n_dp // 2)] + [(0, n_dp // 2), (n_dp // 2, 0)]
    if not mirror:
        got = lax.ppermute(filters[:, :, rows:], "dp", [(i, last - i) for i in range(n_dp)])
        got_edge = lax.ppermute(filters[:, :, :1], "dp", across)
        direct = jnp.where(upper, got, filters[:, :, :rows]).astype(F32)
        mirror_lower = jnp.concatenate([got[:, :, 1:], got_edge], axis=2)
        mirror_upper = filters[:, :, 1 : rows + 1]
        image = jnp.flip(jnp.where(upper, mirror_upper, mirror_lower), 2).astype(F32)
        nyquist = got_edge[:, 0, 0].astype(F32)
        edge = ((jnp.arange(rows) == 0) & (d == 0))[None, :, None]
        half_real = jnp.where(edge, direct[:, 0], direct[:, 0] + image[:, 0])
        half_imag = jnp.where(edge, nyquist[:, None], direct[:, 1] - image[:, 1])
        half = jnp.stack([half_real, half_imag], 1).astype(BF).reshape(4 * rows, ch)

    slice_of = [2 * i if 2 * i < n_dp else 2 * (last - i) + 1 for i in range(n_dp)]

    a_in = [in_weight.transpose(1, 0, 2).reshape(3 * vec, ch), out_weight.T] + ([] if mirror else [half])
    a_in = jnp.concatenate(a_in)
    f_in = filters.transpose(0, 1, 3, 2).reshape(4, ch, 2 * rows)
    vectors = jnp.stack([norm1_gain, norm1_bias, norm2_gain, norm2_bias, out_bias, down_bias])
    vectors = jnp.concatenate([vectors, in_bias])
    vectors = jnp.pad(vectors, ((0, 16 - 9), (0, width - vec)))
    share = hid // n_dp
    ff = [w.reshape(n_dp, vec, hid) for w in (gate_weight, up_weight, down_weight)]
    x_in = tokens.transpose(0, 2, 1, 3).reshape(n_tp, own, local, width)
    layout = Pack(a_in.shape[0], ch)
    ffw, aw, x_own = gather_weights(ff, layout.pack(a_in), a_in.shape[0], f_in, vectors, x_in, n_dp, n_tp)
    cotangent, _ = lax.optimization_barrier((cotangent, aw))
    vectors = aw[:, 4 * vec + 4 * rows :, :vec].astype(F32).transpose(1, 0, 2).reshape(16, width)
    slots = [slice_of.index(k) for k in range(n_dp)]
    direct = vec % 16 == 0 and hid == width
    if direct:
        ws = [
            (ffw, (n_dp, n_tp, None, vec, hid), (0, 0, g, 0, 0), (n_dp, 1, None, vec, hid), lambda p, g=g: (0, p, g, 0, 0))
            for g in range(3)
        ]
        a_view = aw
    else:
        natural = [ffw[:, :, g].transpose(1, 0, 2, 3).reshape(n_tp, width, hid) for g in range(2)]
        natural.append(ffw[:, :, 2].reshape(n_dp, n_tp, share, width).transpose(1, 0, 2, 3).reshape(n_tp, hid, width))
        ws = [
            (w[None], (1,) + w.shape, (0, 0, 0, 0), (1, 1) + w.shape[1:], lambda p: (0, p, 0, 0)) for w in natural
        ]
        a_view = aw[:, : 4 * vec].reshape(n_dp, 4, vec, width).transpose(1, 0, 2, 3).reshape(1, 4 * width, width)

    def to_owner(x):
        pieces = x.transpose(0, 2, 1, 3).reshape(n_tp, own, local, width)
        return lax.all_to_all(pieces, "tp", 0, 1, tiled=False).reshape(own, slot_len, width)

    def to_slots(x):
        whole = lax.all_to_all(x.reshape(n_tp, own * local, width), "tp", 0, 0, tiled=False)
        return whole.reshape(micro, group, local, width).transpose(0, 2, 1, 3)

    c_own = to_owner(cotangent)
    flat_len = lax.dynamic_slice_in_dim(lengths.reshape(-1), z * own, own, 0)
    first = 4 * vec // rows
    values, gating, nsum, mixing = project(x_own, flat_len, a_view, vectors)
    spec, conv, gated = spectral(values, gating, mixing, flat_len, table, aw, first, rows, slots, scale)
    middle, n2, act, side, hidden, out = feed(x_own, gated, flat_len, a_view, ws, n_tp, hid, vectors)
    layer_out = to_slots(out)
    e, *d_ff = feed_back(c_own, n2, act, side, hidden, flat_len, ws)
    mg, cg, gtg, d_out, sums = branch_back(e, middle, c_own, gating, conv, flat_len, a_view, vectors)
    layer_out, cg = lax.optimization_barrier((layer_out, cg))
    vg, d_filter, cgv = spectral_back(cg, spec, mixing, flat_len, table, aw, first, rows, slots, scale)
    ig, d_first, sums = input_back(vg, gtg, x_own, mg, nsum, cgv, flat_len, a_view, d_out, sums, vectors)
    if not direct:
        d_ff = [
            g[0].reshape(n_tp, n_dp, vec, hid).transpose(1, 0, 2, 3) for g in d_ff[:2]
        ] + [d_ff[2][0].reshape(n_tp, n_dp, vec, hid).transpose(1, 0, 2, 3)]
        d_first = d_first.reshape(4, n_dp, vec, width).transpose(1, 0, 2, 3).reshape(n_dp, 4 * vec, width)
    ffg, ag, full, vecs, input_grad = scatter_grads(d_ff, d_first, d_filter, sums, ig, n_dp, n_tp)
    input_grad = input_grad.reshape(micro, group, local, width).transpose(0, 2, 1, 3)
    ag = layout.unpack(ag)
    gate_grad = ffg[:, 0].reshape(width, hid).astype(F32)
    up_grad = ffg[:, 1].reshape(width, hid).astype(F32)
    down_grad = ffg[:, 2].reshape(hid, width).astype(F32)
    in_grad = ag[: 3 * vec].reshape(3, vec, ch).transpose(1, 0, 2)
    out_grad = ag[3 * vec : 4 * vec].T
    if mirror:
        full = full.reshape(2, 2, ch, 2 * rows).transpose(0, 1, 3, 2)
    else:
        fgrad = ag[4 * vec :].astype(BF).reshape(2, 2, rows, ch)
        other = lax.ppermute(fgrad, "dp", [(i, last - i) for i in range(n_dp)])
        low_slice = jnp.where(upper, other, fgrad)
        high_slice = jnp.where(upper, fgrad, other)
        both = jnp.concatenate([low_slice, high_slice], axis=2)
        follow = lax.ppermute(fgrad[:, :, :1], "dp", across)
        zero = jnp.zeros_like(follow[:, 0])
        follow = jnp.where(d == n_dp // 2, jnp.stack([follow[:, 1], zero], 1), follow)
        mirrored = jnp.flip(jnp.concatenate([both[:, :, 1:], follow], axis=2), 2)
        mirrored = jnp.stack([mirrored[:, 0], -mirrored[:, 1]], 1)
        plain = jnp.stack(
            [both[:, 0], jnp.where((d == 0) & (jnp.arange(2 * rows) == 0)[None, :, None], 0.0, both[:, 1].astype(F32)).astype(BF)], 1
        )
        full = jnp.where(upper, mirrored, plain).astype(F32)
    piece = width // (n_dp * n_tp)
    vecs = lax.dynamic_slice_in_dim(vecs, (d * n_tp + z) * piece, piece, 1)
    return (
        layer_out,
        input_grad,
        vecs[0],
        vecs[1],
        in_grad,
        vecs[6:9],
        full[0],
        full[1],
        out_grad,
        vecs[4],
        vecs[2],
        vecs[3],
        gate_grad,
        up_grad,
        down_grad,
        vecs[5],
    )


def solution(mesh):
    in_specs = (
        P(None, "tp", "dp", None),
        P(None, "dp"),
        P(None, "tp", "dp", None),
        P("dp"),
        P("dp"),
        P("dp", None, "tp"),
        P(None, "dp"),
        P(None, "dp", "tp"),
        P(None, "dp", "tp"),
        P("tp", "dp"),
        P("dp"),
        P("dp"),
        P("dp"),
        P(None, "tp"),
        P(None, "tp"),
        P("tp", None),
        P("dp"),
    )
    out_specs = (
        P(None, "tp", "dp", None),
        P(None, "tp", "dp", None),
        P(("dp", "tp")),
        P(("dp", "tp")),
        P("dp", None, "tp"),
        P(None, ("dp", "tp")),
        P(None, "dp", "tp"),
        P(None, "dp", "tp"),
        P("tp", "dp"),
        P(("dp", "tp")),
        P(("dp", "tp")),
        P(("dp", "tp")),
        P(None, "tp"),
        P(None, "tp"),
        P("tp", None),
        P(("dp", "tp")),
    )
    return jax.shard_map(body, mesh=mesh, in_specs=in_specs, out_specs=out_specs, check_vma=False)
```

```python
import functools
import math

import jax
import jax.numpy as jnp
import numpy as np
from jax import lax
from jax.experimental import pallas as pl
from jax.experimental.pallas import tpu as pltpu
from jax.sharding import PartitionSpec as P

EPSILON = 1e-05
ROWS = 64
BF = jnp.bfloat16
F32 = jnp.float32
GELU_A = math.sqrt(2.0 / math.pi)
GELU_B = 0.044715


def packed_table(slot_len):
    frequency = np.arange(slot_len, dtype=np.int64)[:, None]
    position = np.arange(slot_len, dtype=np.int64)[None, :]
    angles = (frequency * position % (2 * slot_len)).astype(np.float32) * np.float32(math.pi / slot_len)
    top = np.cos(angles)
    low = -np.sin(angles)
    low[0] = 1.0 - 2.0 * (np.arange(slot_len) % 2)
    return np.concatenate([top, low]).astype(np.float32).astype(jnp.bfloat16)


def shift(x, axis, step):
    n = lax.axis_size(axis)
    return lax.ppermute(x, axis, [(i, (i + step) % n) for i in range(n)])


def exchange(pieces, place, n):
    out = [(place, lax.dynamic_index_in_dim(pieces, place, 0, keepdims=False))]
    for step in range(1, n):
        block = lax.dynamic_index_in_dim(pieces, (place + step) % n, 0, keepdims=False)
        out.append(((place + n - step) % n, shift(block, "tp", step)))
    return out


def mm(a, b):
    return lax.dot_general(a, b, (((1,), (0,)), ((), ())), preferred_element_type=F32)


def mm_nt(a, b):
    return lax.dot_general(a, b, (((1,), (1,)), ((), ())), preferred_element_type=F32)


def mm_tn(a, b):
    return lax.dot_general(a, b, (((0,), (0,)), ((), ())), preferred_element_type=F32)


def mean_of(v):
    return jnp.sum(v, axis=-1, keepdims=True) * (1.0 / v.shape[-1])


def standardize(v):
    centred = v - mean_of(v)
    inverse = lax.rsqrt(mean_of(centred * centred) + EPSILON)
    return centred * inverse, inverse


def norm_back(e, gain, s, q):
    eg = e * gain
    return q * (eg - mean_of(eg) - s * mean_of(eg * s))


def gelu_parts(v):
    square = v * v
    th = jnp.tanh(v * (GELU_A + (GELU_A * GELU_B) * square))
    rise = 0.5 + 0.5 * th
    act = v * rise
    slope = rise + act * (1.0 - th) * (GELU_A + (3.0 * GELU_A * GELU_B) * square)
    return act, slope


def live(rows, first, count):
    at = lax.broadcasted_iota(jnp.int32, (rows, 1), 0) + first
    return jnp.where(at < count, 1.0, 0.0)


def joined(ref):
    v = ref[...]
    return v.reshape(-1, v.shape[-1])


def two_part_dot(a, b, dims):
    high = a.astype(BF)
    low = (a - high.astype(F32)).astype(BF)
    return lax.dot_general(high, b, (dims, ((), ())), preferred_element_type=F32) + lax.dot_general(
        low, b, (dims, ((), ())), preferred_element_type=F32
    )


def top_row(v, rows=8):
    r = lax.broadcasted_iota(jnp.int32, (rows, v.shape[1]), 0)
    return jnp.where(r == 0, jnp.broadcast_to(v, (rows, v.shape[1])), 0.0)


def mix_kernel(
    tile, tiles, slots, scale, lens, x, wv, wg, wc, vec, table, f0, f1, f2, f3,
    gating, nsum, mixing, spec, conv, gated, vals, gats,
):
    i = pl.program_id(0)
    own, n = vals.shape[1], vals.shape[2]
    blocks, cb = vals.shape[0], vals.shape[3]

    @pl.when(i < own * tiles)
    def _():
        s, t = i // tiles, lax.rem(i, tiles)
        here = pl.ds(t * tile, tile)
        count = lens[s]
        valid = live(tile, t * tile, count)
        std, _ = standardize(x[0].astype(F32))
        normed = (std * vec[0:1] + vec[1:2]).astype(BF)
        v = ((mm(normed, joined(wv)) + vec[6:7]) * valid).astype(BF)
        g = (mm(normed, joined(wg)) + vec[7:8]).astype(BF)
        gating[0] = g
        for c in range(blocks):
            vals[c, s, here] = v[:, c * cb : (c + 1) * cb]
            gats[c, s, here] = g[:, c * cb : (c + 1) * cb]
        part = top_row(jnp.sum(normed.astype(F32) * valid, axis=0, keepdims=True))

        @pl.when(t == 0)
        def _():
            nsum[s] = part

        @pl.when(t > 0)
        def _():
            nsum[s] += part

        @pl.when(t == tiles - 1)
        def _():
            length = count.astype(F32)
            cond = two_part_dot(nsum[s], joined(wc), ((1,), (0,))) + length * vec[8:9]
            mixing[s] = jnp.tanh(cond / length)

    @pl.when(i >= own * tiles)
    def _():
        c = i - own * tiles
        columns = pl.ds(pl.multiple_of(c * cb, cb), cb)
        raw = [mm(table[...], vals[c, s]) for s in range(own)]
        edge = lax.broadcasted_iota(jnp.int32, (n, 1), 0) == 0
        outs = []
        for s in range(own):
            v = raw[s]
            spec[s] = v.astype(BF)
            sr, si = v[:n], v[n:]
            fr, fi, _, _ = filters_of((f0, f1, f2, f3), slots, mixing[s, 0:1, columns])
            fr2 = jnp.where(edge, fi, fr)
            fi = jnp.where(edge, 0.0, fi)
            prod = jnp.concatenate([(fr * sr - fi * si).astype(BF), (fr2 * si + fi * sr).astype(BF)])
            outs.append(mm_tn(table[...], prod))
        for s in range(own):
            out = outs[s] * scale
            conv[s] = out.astype(BF)
            gated[s] = (out * gats[c, s].astype(F32)).astype(BF)


def filters_of(refs, slots, mix):
    base_r, base_i, mod_r, mod_i = [jnp.concatenate([ref[j] for j in slots]).astype(F32) for ref in refs]
    return base_r + mix * mod_r, base_i + mix * mod_i, mod_r, mod_i


def feed_kernel(tile, n_tp, lens, x, gated, w_out, hg, hu, hd, vec, middle, n2, act, side, hidden, out, wg, wu, wd, sems):
    s, t = pl.program_id(0), pl.program_id(1)
    begin = (s == 0) & (t == 0)
    copies = [
        pltpu.make_async_copy(src.at[:, :, g] if len(src.shape) == 5 else src, dst, sems.at[g])
        for g, (src, dst) in enumerate(((hg, wg), (hu, wu), (hd, wd)))
    ]

    @pl.when(begin)
    def _():
        for copy in copies:
            copy.start()

    valid = live(tile, t * tile, lens[s])
    mid = x[0].astype(F32) + valid * (mm_nt(gated[0], joined(w_out)) + vec[4:5])
    middle[0] = mid.astype(BF)
    std, _ = standardize(mid)
    normed = (std * vec[2:3] + vec[3:4]).astype(BF)
    n2[0] = normed

    @pl.when(begin)
    def _():
        for copy in copies:
            copy.wait()

    feed = jnp.zeros(mid.shape, F32)
    for p in range(n_tp):
        gate = mm(normed, joined(wg.at[:, p]))
        up = mm(normed, joined(wu.at[:, p]))
        a, slope = gelu_parts(gate)
        act[0, p] = a.astype(BF)
        side[0, p] = (up * slope).astype(BF)
        h = (a * up).astype(BF)
        hidden[0, p] = h
        feed += mm(h, joined(wd.at[:, p]))
    out[:, 0] = (mid + valid * (feed + vec[5:6])).astype(BF).reshape(out.shape[0], out.shape[2], out.shape[3])


def feed_back_kernel(tile, lens, cot, n2, act, side, hidden, wg, wu, wd, e_out, d_gate, d_up, d_down, e_acc, acc_g, acc_u, acc_d, fgs, ggs, ugs):
    p, s = pl.program_id(0), pl.program_id(1)
    n = cot.shape[1]

    @pl.when(p == 0)
    def _():
        e_acc[s] = jnp.zeros(e_acc.shape[1:], F32)

    down, gate, up = joined(wd.at[:, 0]), joined(wg.at[:, 0]), joined(wu.at[:, 0])
    for i in range(n // tile):
        here = pl.ds(i * tile, tile)
        fg = (cot[0, here].astype(F32) * live(tile, i * tile, lens[s])).astype(BF)
        fgs[here] = fg
        hg = mm_nt(fg, down)
        ggs[here] = (hg * side[0, 0, here].astype(F32)).astype(BF)
        ugs[here] = (hg * act[0, 0, here].astype(F32)).astype(BF)
    for i in range(n // tile):
        here = pl.ds(i * tile, tile)
        e_acc[s, here] += mm_nt(ggs[here], gate) + mm_nt(ugs[here], up)
    own = e_acc.shape[0]
    sides = ((acc_g, d_gate, n2.at[0], ggs), (acc_u, d_up, n2.at[0], ugs), (acc_d, d_down, hidden.at[0, 0], fgs))

    def put(out, v):
        out[:, 0] = v.astype(BF).reshape(out.shape[0], out.shape[2], out.shape[3])

    if own == 1:
        for acc, out, left, right in sides:
            put(out, mm_tn(left[...], right[...]))
    else:

        @pl.when(s == 0)
        def _():
            for acc, out, left, right in sides:
                acc[...] = mm_tn(left[...], right[...])

        @pl.when(s == own - 1)
        def _():
            for acc, out, left, right in sides:
                put(out, acc[...] + mm_tn(left[...], right[...]))

    if own > 2:

        @pl.when((s > 0) & (s < own - 1))
        def _():
            for acc, out, left, right in sides:
                acc[...] += mm_tn(left[...], right[...])

    @pl.when(p == pl.num_programs(0) - 1)
    def _():
        e_out[0] = e_acc[s].astype(BF)


def eights(v):
    return jnp.sum(v.reshape(-1, 8, v.shape[-1]), axis=0)


def branch_back_kernel(tile, lens, e, middle, cot, gating, conv, w_out, vec, mg_out, cg, gtg, d_out, sums, acc, bgs, gts, part_sums):
    s, t = pl.program_id(0), pl.program_id(1)
    begin = (s == 0) & (t == 0)
    end = (s == pl.num_programs(0) - 1) & (t == pl.num_programs(1) - 1)

    @pl.when(begin)
    def _():
        acc[...] = jnp.zeros(acc.shape, F32)
        part_sums[...] = jnp.zeros(part_sums.shape, F32)

    count = lens[s]
    gain = vec[2:3]
    step = min(ROWS, tile)
    for i in range(tile // step):
        here = pl.ds(i * step, step)
        valid = live(step, t * tile + i * step, count)
        up = cot[0, here].astype(F32)
        std, inverse = standardize(middle[0, here].astype(F32))
        grad = e[0, here].astype(F32)
        mg = up + norm_back(grad, gain, std, inverse)
        mg_out[0, here] = mg.astype(BF)
        bgr = (mg * valid).astype(BF)
        bgs[here] = bgr
        fg = (up * valid).astype(BF).astype(F32)
        for j, v in enumerate((grad * std, grad, bgr.astype(F32), fg)):
            part_sums[j] += eights(v)
    ggr = mm(bgs[...], joined(w_out))
    for i in range(tile // step):
        here = pl.ds(i * step, step)
        gate, out = gating[0, here].astype(F32), conv[0, here].astype(F32)
        g = ggr[i * step : (i + 1) * step]
        cg[0, here] = (g * gate).astype(BF)
        gtg[0, here] = (g * out).astype(BF)
        gts[here] = (out * gate).astype(BF)
    acc[...] += mm_tn(bgs[...], gts[...])

    @pl.when(end)
    def _():
        d_out[...] = acc[...].astype(BF).reshape(d_out.shape)
        sums[...] = jnp.zeros(sums.shape, F32)
        for j in range(4):
            sums[j : j + 1] = jnp.sum(part_sums[j], axis=0, keepdims=True)


def spectral_back_kernel(slots, scale, lens, cg, spec, mixing, table, f0, f1, f2, f3, vg, fgrad, cgv):
    own = cg.shape[0]
    n = cg.shape[1]
    size = n // len(slots)
    raw = [mm(table[...], cg[s]) for s in range(own)]
    edge = lax.broadcasted_iota(jnp.int32, (n, 1), 0) == 0
    outs, total = [], None
    for s in range(own):
        v = raw[s] * scale
        pr, pi = v[:n], v[n:]
        mix = mixing[s, 0:1]
        fr, fi, mod_r, mod_i = filters_of((f0, f1, f2, f3), slots, mix)
        fr2 = jnp.where(edge, fi, fr)
        fi = jnp.where(edge, 0.0, fi)
        sg = jnp.concatenate([(fr * pr + fi * pi).astype(BF), (fr2 * pi - fi * pr).astype(BF)])
        outs.append(mm_tn(table[...], sg))
        sr, si = spec[s, :n].astype(F32), spec[s, n:].astype(F32)
        both = pi * si
        dr = pr * sr + jnp.where(edge, 0.0, both)
        di = jnp.where(edge, both, pi * sr - pr * si)
        mixg = jnp.sum(mod_r * dr + mod_i * di, axis=0, keepdims=True)
        step = mixg * (1.0 - mix * mix) / lens[s].astype(F32)
        cgv[s] = top_row(step.astype(BF).astype(F32))
        parts = (dr, di, mix * dr, mix * di)
        total = parts if total is None else tuple(t + p for t, p in zip(total, parts))
    for s in range(own):
        vg[s] = (outs[s] * live(n, 0, lens[s])).astype(BF)
    for j in range(len(slots)):
        k = slots.index(j)
        for i in range(4):
            fgrad[j, pl.ds(i * size, size)] = total[i][k * size : (k + 1) * size].astype(BF)


def input_back_kernel(tile, lens, vg, gtg, x, mg, nsum, cgv, wv, wg, wc, d_out, sums_in, vec, ig, d_in, sums, acc_v, acc_g, acc_c):
    s, t = pl.program_id(0), pl.program_id(1)
    begin = (s == 0) & (t == 0)
    end = (s == pl.num_programs(0) - 1) & (t == pl.num_programs(1) - 1)
    count = lens[s]

    @pl.when(begin)
    def _():
        for acc in (acc_v, acc_g, acc_c):
            acc[...] = jnp.zeros(acc.shape, F32)
        sums[...] = jnp.zeros(sums.shape, F32)
        sums[2:6] = sums_in[0:4]

    valid = live(tile, t * tile, count)
    cvec = mm_nt(cgv[0].astype(BF), joined(wc))[0:1]
    vgb, gtb = vg[0], gtg[0]
    e = mm_nt(vgb, joined(wv)) + mm_nt(gtb, joined(wg)) + valid * cvec
    std, inverse = standardize(x[0].astype(F32))
    ig[0] = (mg[0].astype(F32) + norm_back(e, vec[0:1], std, inverse)).astype(BF)
    normed = (std * vec[0:1] + vec[1:2]).astype(BF)
    part_v, part_g = mm_tn(normed, vgb), mm_tn(normed, gtb)
    rows = [e * std, e, vgb.astype(F32), gtb.astype(F32)]
    rows = [jnp.sum(r, axis=0, keepdims=True) for r in rows]

    acc_v[...] += part_v
    acc_g[...] += part_g
    for i, r in zip((0, 1, 6, 7), rows):
        sums[i : i + 1] += r

    @pl.when(t == 0)
    def _():
        acc_c[...] += two_part_dot(nsum[0], cgv[0].astype(BF), ((0,), (0,)))
        sums[8:9] += cgv[0, 0:1] * count.astype(F32)

    @pl.when(end)
    def _():
        r = d_out.shape[1]
        shape = (d_in.shape[0], r, d_in.shape[2])
        for i, acc in enumerate((acc_v, acc_g, acc_c)):
            d_in[:, i * r : (i + 1) * r] = acc[...].astype(BF).reshape(shape)
        d_in[:, 3 * r :] = d_out[...]


def call(kernel, grid, lens, ins, in_specs, outs, out_specs, scratch, flops, name, limit=56):
    spec = pltpu.PrefetchScalarGridSpec(
        num_scalar_prefetch=1, grid=grid, in_specs=in_specs, out_specs=out_specs, scratch_shapes=scratch
    )
    moved = sum(math.prod(v.shape) * v.dtype.itemsize for v in list(ins) + list(outs))
    return pl.pallas_call(
        kernel,
        grid_spec=spec,
        out_shape=tuple(outs),
        compiler_params=pltpu.CompilerParams(
            dimension_semantics=("arbitrary",) * len(grid), vmem_limit_bytes=limit * 1024 * 1024
        ),
        cost_estimate=pl.CostEstimate(flops=int(flops), bytes_accessed=int(moved), transcendentals=0),
        name=name,
    )(lens, *ins)


def once(block, index):
    return pl.BlockSpec(block, lambda *_: index, pipeline_mode=pl.Buffered(1))


def shape_of(shape, dtype):
    return jax.ShapeDtypeStruct(shape, dtype)


def filter_specs(fw, n_dp, rows, cb, first):
    return [
        pl.BlockSpec((n_dp, rows, cb), lambda *g, i=i: (0, first + i, g[0])) for i in range(4)
    ]


def mix(x, lens, aw, vec, table, fw, first, rows, slots, scale):
    own, n, width = x.shape
    tile = min(512, n)
    tiles = n // tile
    steps = own * tiles
    cb = min(256, width)
    blocks = width // cb
    nd, r = aw.shape[0], width // aw.shape[0]
    n_dp = fw.shape[0]

    def tok(i, *_):
        j = jnp.minimum(i, steps - 1)
        return j // tiles, lax.rem(j, tiles), 0

    def chan(i):
        return jnp.maximum(i - steps, 0)

    token = pl.BlockSpec((1, tile, width), tok)
    whole = pl.BlockSpec((own, 8, width), lambda *_: (0, 0, 0))
    column = pl.BlockSpec((own, n, cb), lambda i, *_: (0, 0, chan(i)))
    double = pl.BlockSpec((own, 2 * n, cb), lambda i, *_: (0, 0, chan(i)))
    weights = [once((nd, r, width), (0, g, 0)) for g in range(3)]
    filters = [pl.BlockSpec((n_dp, rows, cb), lambda i, *_, k=k: (0, first + k, chan(i))) for k in range(4)]
    sd = shape_of(x.shape, BF)
    row = shape_of((own, 8, width), F32)
    return call(
        functools.partial(mix_kernel, tile, tiles, slots, scale),
        (steps + blocks,),
        lens,
        [x, aw, aw, aw, vec, table] + [fw] * 4,
        [token] + weights + [once(vec.shape, (0, 0)), once(table.shape, (0, 0))] + filters,
        [sd, row, row, shape_of((own, 2 * n, width), BF), sd, sd],
        (token, whole, whole, double, column, column),
        [pltpu.VMEM((blocks, own, n, cb), BF), pltpu.VMEM((blocks, own, n, cb), BF)],
        4 * own * n * width * width + 8 * own * n * n * width,
        "mix",
    )


def feed(x, gated, lens, aw, ws, n_tp, hid, vec):
    own, n, width = x.shape
    local = n // n_tp
    tile = max(256, local)
    r = width // aw.shape[0]
    tok = pl.BlockSpec((1, tile, width), lambda s, t, *_: (s, t, 0))
    wide = pl.BlockSpec((1, n_tp, tile, hid), lambda s, t, *_: (s, 0, t, 0))
    parts = pl.BlockSpec((tile // local, 1, local, width), lambda s, t, *_: (t, s, 0, 0))
    big = shape_of((own, n_tp, n, hid), BF)
    return call(
        functools.partial(feed_kernel, tile, n_tp),
        (own, n // tile),
        lens,
        [x, gated, aw] + [w[0] for w in ws] + [vec],
        [tok, tok, once((aw.shape[0], r, width), (0, 3, 0))] + [pl.BlockSpec(memory_space=pl.ANY)] * 3 + [once(vec.shape, (0, 0))],
        [shape_of(x.shape, BF), shape_of(x.shape, BF), big, big, big, shape_of((n_tp, own, local, width), BF)],
        (tok, tok, wide, wide, wide, parts),
        [pltpu.VMEM(tuple(v for v in w[1] if v is not None), BF) for w in ws] + [pltpu.SemaphoreType.DMA((3,))],
        2 * own * n * width * (width + 3 * n_tp * hid),
        "feed",
        limit=60,
    )


def feed_back(cot, n2, act, side, hidden, lens, ffw):
    own, n, width = cot.shape
    n_tp, hid = act.shape[1], act.shape[3]
    tile = min(512, n)
    tok = pl.BlockSpec((1, n, width), lambda p, s, *_: (s, 0, 0))
    wide = pl.BlockSpec((1, 1, n, hid), lambda p, s, *_: (s, p, 0, 0))
    w_specs = [pl.BlockSpec(w[3], lambda p, s, *_, f=w[4]: f(p)) for w in ffw]
    nd = [next(v for v in w[3]) for w in ffw]
    sides = [(width, hid), (width, hid), (hid, width)]
    shapes = [(k, n_tp, a // k, b) for k, (a, b) in zip(nd, sides)]
    d_specs = [pl.BlockSpec((shape[0], 1) + shape[2:], lambda p, s, *_: (0, p, 0, 0)) for shape in shapes]
    d_shapes = [shape_of(shape, BF) for shape in shapes]
    return call(
        functools.partial(feed_back_kernel, tile),
        (n_tp, own),
        lens,
        [cot, n2, act, side, hidden] + [w[0] for w in ffw],
        [tok, tok, wide, wide, wide] + w_specs,
        [shape_of(cot.shape, BF)] + d_shapes,
        (pl.BlockSpec((1, n, width), lambda p, s, *_: (jnp.where(p == n_tp - 1, s, 0), 0, 0)), *d_specs),
        [
            pltpu.VMEM(cot.shape, F32),
            pltpu.VMEM((width, hid), F32),
            pltpu.VMEM((width, hid), F32),
            pltpu.VMEM((hid, width), F32),
            pltpu.VMEM((n, width), BF),
            pltpu.VMEM((n, hid), BF),
            pltpu.VMEM((n, hid), BF),
        ],
        12 * own * n * width * n_tp * hid,
        "feed_back",
        limit=60,
    )


def branch_back(e, middle, cot, gating, conv, lens, aw, vec):
    own, n, width = cot.shape
    tile = min(512, n)
    nd, r = aw.shape[0], width // aw.shape[0]
    tok = pl.BlockSpec((1, tile, width), lambda s, t, *_: (s, t, 0))
    return call(
        functools.partial(branch_back_kernel, tile),
        (own, n // tile),
        lens,
        [e, middle, cot, gating, conv, aw, vec],
        [tok] * 5 + [once((nd, r, width), (0, 3, 0)), once(vec.shape, (0, 0))],
        [
            shape_of(cot.shape, BF),
            shape_of(cot.shape, BF),
            shape_of(cot.shape, BF),
            shape_of((nd, r, width), BF),
            shape_of((8, width), F32),
        ],
        (tok, tok, tok, pl.BlockSpec((nd, r, width), lambda *_: (0, 0, 0)), pl.BlockSpec((8, width), lambda *_: (0, 0))),
        [
            pltpu.VMEM((width, width), F32),
            pltpu.VMEM((tile, width), BF),
            pltpu.VMEM((tile, width), BF),
            pltpu.VMEM((4, 8, width), F32),
        ],
        4 * own * n * width * width,
        "branch_back",
    )


def spectral_back(cg, spec, mixing, lens, table, fw, first, rows, slots, scale):
    own, n, width = cg.shape
    cb = min(256, width)
    n_dp = fw.shape[0]
    tok = pl.BlockSpec((own, n, cb), lambda c, *_: (0, 0, c))
    both = pl.BlockSpec((own, 2 * n, cb), lambda c, *_: (0, 0, c))
    one = pl.BlockSpec((own, 8, cb), lambda c, *_: (0, 0, c))
    return call(
        functools.partial(spectral_back_kernel, slots, scale),
        (width // cb,),
        lens,
        [cg, spec, mixing, table] + [fw] * 4,
        [tok, both, one, once(table.shape, (0, 0))] + filter_specs(fw, n_dp, rows, cb, first),
        [shape_of(cg.shape, BF), shape_of((n_dp, 4 * rows, width), BF), shape_of((own, 8, width), F32)],
        (tok, pl.BlockSpec((n_dp, 4 * rows, cb), lambda c, *_: (0, 0, c)), one),
        [],
        8 * own * n * n * width,
        "spectral_back",
    )


def input_back(vg, gtg, x, mg, nsum, cgv, lens, aw, d_out, sums, vec):
    own, n, width = x.shape
    tile = min(512, n)
    nd, r = aw.shape[0], width // aw.shape[0]
    tok = pl.BlockSpec((1, tile, width), lambda s, t, *_: (s, t, 0))
    one = pl.BlockSpec((1, 8, width), lambda s, t, *_: (s, 0, 0))
    weights = [once((nd, r, width), (0, g, 0)) for g in range(3)]
    return call(
        functools.partial(input_back_kernel, tile),
        (own, n // tile),
        lens,
        [vg, gtg, x, mg, nsum, cgv, aw, aw, aw, d_out, sums, vec],
        [tok] * 4 + [one] * 2 + weights + [once((nd, r, width), (0, 0, 0)), once((8, width), (0, 0)), once(vec.shape, (0, 0))],
        [shape_of(x.shape, BF), shape_of((nd, 4 * r, width), BF), shape_of((16, width), F32)],
        (tok, pl.BlockSpec((nd, 4 * r, width), lambda *_: (0, 0, 0)), pl.BlockSpec((16, width), lambda *_: (0, 0))),
        [pltpu.VMEM((width, width), F32)] * 3,
        8 * own * n * width * width,
        "input_back",
    )


MESH = pl.DeviceIdType.MESH


def flip(index, step):
    return index + step - 2 * step * ((index // step) % 2)


def bit_orders(n_dp):
    bits = [1 << b for b in range(1, (n_dp - 1).bit_length())]
    return bits, bits[::-1]


def greet(d, z, n_dp, n_tp, pairs=False):
    barrier = pltpu.get_barrier_semaphore()
    count = greet_pairs(d, z, n_dp) if pairs else 0
    step = 1
    while step < n_dp:
        pl.semaphore_signal(barrier, inc=1, device_id=(flip(d, step), z), device_id_type=MESH)
        step *= 2
        count += 1
    for k in range(1, n_tp):
        pl.semaphore_signal(barrier, inc=1, device_id=(d, lax.rem(z + k, n_tp)), device_id_type=MESH)
        count += 1
    pl.semaphore_wait(barrier, count)


def across_of(d, n):
    return lax.rem(n - d, n) + (n // 2) * (1 - (d % (n // 2) + n // 2 - 1) // (n // 2)) * (1 - 2 * (d // (n // 2)))


def one_hot(rows, cols, test):
    r = lax.broadcasted_iota(jnp.int32, (rows, cols), 0)
    c = lax.broadcasted_iota(jnp.int32, (rows, cols), 1)
    return jnp.where(test(r, c), 1.0, 0.0).astype(BF)


def greet_pairs(d, z, n_dp):
    barrier = pltpu.get_barrier_semaphore()
    for peer in (n_dp - 1 - d, across_of(d, n_dp)):
        pl.semaphore_signal(barrier, inc=1, device_id=(peer, z), device_id_type=MESH)
    return 2


def remote(src, dst, send, recv, target):
    copy = pltpu.make_async_remote_copy(
        src_ref=src, dst_ref=dst, send_sem=send, recv_sem=recv, device_id=target, device_id_type=MESH
    )
    copy.start()
    return copy


class Pack:
    def __init__(self, rows, ch):
        self.rows, self.ch = rows, ch
        self.main = ch // 128
        self.rest = ch % 128
        self.dense = self.rest == 64 and rows % 32 == 0
        self.tail = 0 if not self.rest else rows // 2 if self.dense else rows
        self.total = self.main * rows + self.tail

    def pack(self, v):
        parts = [v[:, i * 128 : (i + 1) * 128] for i in range(self.main)]
        if self.rest:
            left = v[:, self.main * 128 :]
            if self.dense:
                parts.append(jnp.concatenate([left[: self.tail], left[self.tail :]], axis=1))
            else:
                parts.append(jnp.pad(left, ((0, 0), (0, 128 - self.rest))))
        return jnp.concatenate(parts)

    def unpack(self, v):
        parts = [v[i * self.rows : (i + 1) * self.rows] for i in range(self.main)]
        if self.rest:
            left = v[self.main * self.rows :]
            if self.dense:
                parts.append(jnp.concatenate([left[:, :64], left[:, 64:]]))
            else:
                parts.append(left[:, : self.rest])
        return jnp.concatenate(parts, axis=1)

    def pieces(self):
        out = [(i * self.rows, 0, self.rows, 0, 128, i * 128) for i in range(self.main)]
        at = self.main * self.rows
        if self.dense:
            out += [(at, 0, self.tail, 0, 64, self.main * 128), (at, self.tail, self.tail, 64, 64, self.main * 128)]
        elif self.rest:
            out += [(at, 0, self.rows, 0, self.rest, self.main * 128)]
        return out


def lanes_to(width, lane, lanes, column):
    r = lax.broadcasted_iota(jnp.int32, (128, width), 0)
    c = lax.broadcasted_iota(jnp.int32, (128, width), 1)
    inside = (r >= lane) & (r < lane + lanes)
    return jnp.where(inside & (c - r == column - lane), 1.0, 0.0).astype(BF)


def fill_places(ones, layout, width, n_tp):
    pieces = layout.pieces()
    for s in range(n_tp):
        for i, (_, _, _, lane, lanes, column) in enumerate(pieces):
            ones[s * len(pieces) + i] = lanes_to(width, lane, lanes, s * layout.ch + column)


class Line:
    def __init__(self, part, d, z, n, send, recv):
        self.part, self.d, self.z, self.n, self.send, self.recv = part, d, z, n, send, recv

    def _copy(self, way, t, block):
        target = (self.d, self.z + 1 if way == 0 else self.z - 1)
        return pltpu.make_async_remote_copy(
            src_ref=self.part(block),
            dst_ref=self.part(block),
            send_sem=self.send.at[way, t],
            recv_sem=self.recv.at[way, t],
            device_id=target,
            device_id_type=MESH,
        )

    def start(self, t):
        z, n = self.z, self.n

        @pl.when((z >= t) & (z < n - 1))
        def _():
            self._copy(0, t, z - t).start()

        @pl.when((z + t < n) & (z > 0))
        def _():
            self._copy(1, t, z + t).start()

    def wait(self, t):
        z, n = self.z, self.n

        @pl.when(z >= t + 1)
        def _():
            self._copy(0, t, z - 1 - t).wait_recv()

        @pl.when(z + t + 1 < n)
        def _():
            self._copy(1, t, z + 1 + t).wait_recv()

    def drain(self):
        z, n = self.z, self.n
        for t in range(n - 1):

            @pl.when((z >= t) & (z < n - 1))
            def _(t=t):
                self._copy(0, t, z - t).wait_send()

            @pl.when((z + t < n) & (z > 0))
            def _(t=t):
                self._copy(1, t, z + t).wait_send()


class Spread:
    def __init__(self, part, order, d, z, send, recv):
        self.part, self.z, self.send, self.recv = part, z, send, recv
        held, self.steps, used = [d], [], 0
        for step in order:
            self.steps.append((flip(d, step), [(slot, used + i) for i, slot in enumerate(held)]))
            used += len(held)
            held = held + [flip(slot, step) for slot in held]
        self.stage = 0

    def copies(self, stage):
        target, sent = self.steps[stage]
        return [
            pltpu.make_async_remote_copy(
                src_ref=self.part(slot),
                dst_ref=self.part(slot),
                send_sem=self.send.at[i],
                recv_sem=self.recv.at[i],
                device_id=(target, self.z),
                device_id_type=MESH,
            )
            for slot, i in sent
        ]

    def start(self):
        for copy in self.copies(self.stage):
            copy.start()

    def wait(self):
        for copy in self.copies(self.stage):
            copy.wait_recv()
        self.stage += 1

    def drain(self):
        for stage in range(len(self.steps)):
            for copy in self.copies(stage):
                copy.wait_send()


def chunk_of(rows):
    return next((c for c in (128, 96, 64, 48, 32, 16) if rows % c == 0), rows)


def add_rows(dst, src):
    rows = dst.shape[0]
    size = chunk_of(rows)

    @pl.loop(0, rows // size)
    def _(i):
        at = pl.ds(i * size, size)
        dst[at] = dst[at] + src[at]


def lane_place(rows, cols, offset):
    r = lax.broadcasted_iota(jnp.int32, (rows, cols), 0)
    c = lax.broadcasted_iota(jnp.int32, (rows, cols), 1)
    return jnp.where(c - r == offset, 1.0, 0.0).astype(BF)


def gather_kernel(
    n_dp, n_tp, cut, a_rows, mirror, w0, w1, w2, a_in, f_in, vec_in, x_in, ff_out, a_out, x_out, a_z, a_nat, ones, f_got, f_edge,
    la_send, la_recv, lf_send, lf_recv, x_send, x_recv, s_send, s_recv, f_send, f_recv, local,
):
    d, z = lax.axis_index("dp"), lax.axis_index("tp")
    width = a_nat.shape[1]
    ch = width // n_tp
    rows = a_nat.shape[0] - vec_in.shape[0]
    layout = Pack(a_rows, ch)
    own_ff = [pltpu.make_async_copy(w, ff_out.at[:, z, g], local.at[3 + g]) for g, w in enumerate((w0, w1, w2))]
    for copy in own_ff:
        copy.start()
    own_a = pltpu.make_async_copy(a_in, a_z.at[z, pl.ds(0, layout.total)], local.at[1])
    own_a.start()
    greet(d, z, n_dp, n_tp, mirror)
    if mirror:
        k = f_in.shape[2] // 2
        swaps = [
            remote(f_in.at[:, :, pl.ds(k, k)], f_got, f_send.at[0], f_recv.at[0], (n_dp - 1 - d, z)),
            remote(f_in.at[:, :, pl.ds(0, k)], f_edge, f_send.at[1], f_recv.at[1], (across_of(d, n_dp), z)),
        ]
        turn = one_hot(k, k, lambda r, c: r + c == k)
        corner = one_hot(k, k, lambda r, c: r + c == 0)
        upper = d > n_dp - 1 - d
        lane = lax.broadcasted_iota(jnp.int32, (1, k), 1)
        special = jnp.logical_and(lane == 0, d == 0)
        for copy in swaps:
            copy.wait()
        sums = []
        for c in range(4):
            low, high = f_in[c, :, :k], f_in[c, :, k:]
            direct = jnp.where(upper, f_got[c], low).astype(F32)
            image = mm(jnp.where(upper, low, f_got[c]), turn) + mm(jnp.where(upper, high, f_edge[c]), corner)
            if c % 2 == 0:
                nyquist = image
                folded = jnp.where(special, direct, direct + image)
            else:
                folded = jnp.where(special, nyquist, direct - image)
            a_z[z, pl.ds(layout.total + c * ch, ch)] = folded.astype(BF)
    line_a = Line(lambda s: a_z.at[s], d, z, n_tp, la_send, la_recv)
    line_f = Line(lambda s: ff_out.at[d, s], d, z, n_tp, lf_send, lf_recv)
    first, second = bit_orders(n_dp)
    vec = w0.shape[1]

    def block_spreads(block):
        out = []
        for h, order in enumerate((first, second)):
            at = 2 + 2 * block + h
            if vec % 32 == 0:
                part = lambda s, h=h: ff_out.at[s, block, :, pl.ds(h * (vec // 2), vec // 2)]
            else:
                part = lambda s, h=h: ff_out.at[s, block, pl.ds(h, 1 + h)]
            out.append(Spread(part, order + [1], d, z, s_send.at[at], s_recv.at[at]))
        return out

    own_a.wait()
    line_a.start(0)
    fill_places(ones, layout, width, n_tp)
    for t in range(n_tp - 1):
        line_a.wait(t)
        if t + 1 < n_tp - 1:
            line_a.start(t + 1)
    for copy in own_ff:
        copy.wait()
    line_f.start(0)
    half_rows = a_rows // 2
    n_pieces = len(layout.pieces())
    size = chunk_of(half_rows)
    for side in range(2):
        found = []
        for j, (packed, low, count, _, _, _) in enumerate(layout.pieces()):
            if low <= side * half_rows < low + count:
                found.append((packed + side * half_rows - low, j))

        @pl.loop(0, half_rows // size)
        def _(i, found=found, side=side):
            total = jnp.zeros((size, width), F32)
            for s in range(n_tp):
                for packed, j in found:
                    total += mm(a_z[s, pl.ds(packed + i * size, size)], ones[s * n_pieces + j])
            a_nat[pl.ds(side * half_rows + i * size, size)] = total.astype(BF)

    if mirror:
        for c in range(4):
            total = jnp.zeros((k, width), F32)
            for s in range(n_tp):
                place = one_hot(ch, width, lambda r, col, s=s: col - r == s * ch)
                total += mm_tn(a_z[s, pl.ds(layout.total + c * ch, ch)], place)
            a_nat[pl.ds(a_rows + c * k, k)] = total.astype(BF)
    a_nat[rows:] = vec_in[...]
    put = pltpu.make_async_copy(a_nat, a_out.at[d], local.at[2])
    put.start()
    put.wait()
    total_rows = a_nat.shape[0]
    sa = [
        Spread(lambda s: a_out.at[s, pl.ds(0, cut)], first + [1], d, z, s_send.at[0], s_recv.at[0]),
        Spread(lambda s: a_out.at[s, pl.ds(cut, total_rows - cut)], second + [1], d, z, s_send.at[1], s_recv.at[1]),
    ]
    for p in sa:
        p.start()
    stages = len(first) + 1

    def advance(group):
        for p in group:
            p.wait()
            if p.stage < stages:
                p.start()

    blocks = []
    for t in range(n_tp - 1):
        line_f.wait(t)
        if t + 1 < n_tp - 1:
            line_f.start(t + 1)
        for exists, block in ((z >= t + 1, z - 1 - t), (z + t + 1 < n_tp, z + 1 + t)):
            group = block_spreads(block)
            blocks.append((exists, group))

            @pl.when(exists)
            def _(group=group):
                for p in group:
                    p.start()

        if t == 0:
            advance(sa)
    size = x_in.shape[2]
    here = pl.ds(z * size, size)
    own_x = pltpu.make_async_copy(x_in.at[z], x_out.at[:, here], local.at[0])
    own_x.start()
    zx = []
    for k in range(1, n_tp):
        peer = lax.rem(z + k, n_tp)
        zx.append(remote(x_in.at[peer], x_out.at[:, here], x_send.at[k - 1], x_recv.at[k - 1], (d, peer)))
    for stage in range(stages):
        for exists, group in blocks:

            @pl.when(exists)
            def _(group=group):
                advance(group)

        if stage + 1 < stages:
            advance(sa)
    for p in sa:
        p.drain()
    for exists, group in blocks:

        @pl.when(exists)
        def _(group=group):
            for p in group:
                p.drain()

    own_x.wait()
    for copy in zx:
        copy.wait_recv()
    for copy in zx:
        copy.wait_send()
    line_a.drain()
    line_f.drain()


def gather_weights(ff, a_in, a_rows, f_in, vec_in, x_in, n_dp, n_tp):
    width = vec_in.shape[1]
    mirror = f_in.shape[2] % 256 == 0
    ch = width // n_tp
    rows = a_rows + (2 * f_in.shape[2] if mirror else 0)
    k = f_in.shape[2] // 2
    total = rows + vec_in.shape[0]
    cut = total // 2 // 16 * 16
    anyspace = pl.BlockSpec(memory_space=pl.ANY)
    vmem = pl.BlockSpec(memory_space=pltpu.VMEM)
    return pl.pallas_call(
        functools.partial(gather_kernel, n_dp, n_tp, cut, a_rows, mirror),
        out_shape=(
            jax.ShapeDtypeStruct((n_dp, n_tp, 3) + ff[0].shape[1:], BF),
            jax.ShapeDtypeStruct((n_dp, total, width), BF),
            jax.ShapeDtypeStruct((x_in.shape[1], n_tp * x_in.shape[2], width), BF),
        ),
        in_specs=[anyspace] * 4 + [vmem, vmem, anyspace],
        out_specs=(anyspace, anyspace, anyspace),
        scratch_shapes=[
            pltpu.VMEM((n_tp, a_in.shape[0] + (4 * ch if mirror else 0), 128), BF),
            pltpu.VMEM((total, width), BF),
            pltpu.VMEM((n_tp * len(Pack(a_rows, ch).pieces()), 128, width), BF),
            pltpu.VMEM((4, ch, k), BF),
            pltpu.VMEM((4, ch, k), BF),
            pltpu.SemaphoreType.DMA((2, n_tp - 1)),
            pltpu.SemaphoreType.DMA((2, n_tp - 1)),
            pltpu.SemaphoreType.DMA((2, n_tp - 1)),
            pltpu.SemaphoreType.DMA((2, n_tp - 1)),
            pltpu.SemaphoreType.DMA((n_tp - 1,)),
            pltpu.SemaphoreType.DMA((n_tp - 1,)),
            pltpu.SemaphoreType.DMA((2 + 2 * n_tp, n_dp - 1)),
            pltpu.SemaphoreType.DMA((2 + 2 * n_tp, n_dp - 1)),
            pltpu.SemaphoreType.DMA((2,)),
            pltpu.SemaphoreType.DMA((2,)),
            pltpu.SemaphoreType.DMA((6,)),
        ],
        compiler_params=pltpu.CompilerParams(
            collective_id=0, has_side_effects=True, vmem_limit_bytes=48 * 1024 * 1024
        ),
        name="gather_weights",
    )(*ff, a_in, f_in, vec_in, x_in)


class Fold:
    def __init__(self, part, mine, two, order, own, d, z, send, recv):
        self.part, self.mine, self.two, self.z, self.send, self.recv = part, mine, two, z, send, recv
        self.steps, used = [], 0

        def at(mask):
            index, step = own, 1
            while step <= mask:
                if mask & step:
                    index = flip(index, step)
                step *= 2
            return index

        for t, step in enumerate(order):
            masks = [0]
            for later in order[t + 1 :]:
                masks = masks + [m + later for m in masks]
            moves = [(at(m + step), at(m), used + j) for j, m in enumerate(masks)]
            used += len(moves)
            self.steps.append((flip(d, 2 * step), moves))
        self.stage = 0

    def copies(self, stage):
        target, moves = self.steps[stage]
        return [
            pltpu.make_async_remote_copy(
                src_ref=self.part(self.mine, away),
                dst_ref=self.part(self.two, k),
                send_sem=self.send.at[k],
                recv_sem=self.recv.at[k],
                device_id=(target, self.z),
                device_id_type=MESH,
            )
            for away, _, k in moves
        ]

    def start(self):
        for copy in self.copies(self.stage):
            copy.start()

    def finish(self, add):
        for copy, (_, keep, k) in zip(self.copies(self.stage), self.steps[self.stage][1]):
            copy.wait()
            add(self.part(self.mine, keep), self.part(self.two, k))
        self.stage += 1


class LineSum:
    def __init__(self, mine, got, d, z, n, send, recv):
        self.mine, self.got, self.d, self.z, self.n, self.send, self.recv = mine, got, d, z, n, send, recv

    def _copy(self, way, block):
        return pltpu.make_async_remote_copy(
            src_ref=self.mine(block),
            dst_ref=self.got(way, block),
            send_sem=self.send.at[way, block],
            recv_sem=self.recv.at[way, block],
            device_id=(self.d, self.z - 1 if way == 0 else self.z + 1),
            device_id_type=MESH,
        )

    def take(self, block, add):
        z, n = self.z, self.n

        @pl.when((block <= z) & (z < n - 1))
        def _():
            self._copy(0, block).wait_recv()
            add(self.mine(block), self.got(0, block))

        @pl.when((block >= z) & (z > 0))
        def _():
            self._copy(1, block).wait_recv()
            add(self.mine(block), self.got(1, block))

    def give(self, block):
        @pl.when(block < self.z)
        def _():
            self._copy(0, block).start()

        @pl.when(block > self.z)
        def _():
            self._copy(1, block).start()

    def drain(self, block):
        @pl.when(block < self.z)
        def _():
            self._copy(0, block).wait_send()

        @pl.when(block > self.z)
        def _():
            self._copy(1, block).wait_send()


def scatter_kernel(
    n_dp, n_tp, cut, mirror, g0, g1, g2, a0, a1, v_in, x_in, ff_out, a_out, f_out, v_out, x_out,
    ff_mine, a_mine, ff_core, a_core, ff_two, a_two, a_cols, ff_got, a_got, v_got, ones, f_own, f_got, f_edge,
    load, core_send, core_recv, f_send, f_recv, h_send, h_recv, lf_send, lf_recv, la_send, la_recv, lb_send, lb_recv,
    z_send, z_recv, s_send, s_recv, v_send, v_recv, f_swap_send, f_swap_recv, local,
):
    d, z = lax.axis_index("dp"), lax.axis_index("tp")
    width = a0.shape[3]
    rows = a0.shape[2] + a1.shape[2]
    ch = width // n_tp
    a_rows = a0.shape[2] if mirror else rows
    layout = Pack(a_rows, ch)
    vec = g0.shape[3]
    half = n_dp // 2
    side = d % 2
    own = d // 2
    other = (flip(d, 1), z)
    late = z // (n_tp // 2)
    order = [n_tp - 1 - j + late * (2 * j - n_tp + 1) for j in range(n_tp)]
    greet(d, z, n_dp, n_tp, mirror)
    f_core, f_load, a_swap, a_load = [], [], [], []

    def swap_a(g, src, at):
        part = pl.ds(at, src.shape[2])
        a_swap.append(remote(src.at[:, 1 - side], a_core.at[:, part], core_send.at[3, g], core_recv.at[3, g], other))
        copy = pltpu.make_async_copy(src.at[:, side], a_mine.at[:, part], load.at[3, g])
        copy.start()
        a_load.append(copy)

    swap_a(1, a1, a0.shape[2])
    for j, b in enumerate(order):
        for g, src in enumerate((g0, g1, g2)):
            f_core.append(
                remote(src.at[:, 1 - side, b], ff_core.at[b, :, g], core_send.at[g, j], core_recv.at[g, j], other)
            )
            copy = pltpu.make_async_copy(src.at[:, side, b], ff_mine.at[b, :, g], load.at[g, j])
            copy.start()
            f_load.append(copy)
    swap_a(0, a0, 0)
    slot = x_out.shape[2]
    own_x = pltpu.make_async_copy(x_in.at[:, pl.ds(z * slot, slot)], x_out.at[z], local.at[1])
    own_x.start()
    zx = []
    for k in range(1, n_tp):
        peer = lax.rem(z + k, n_tp)
        zx.append(
            remote(x_in.at[:, pl.ds(peer * slot, slot)], x_out.at[z], z_send.at[1, k - 1], z_recv.at[1, k - 1], (d, peer))
        )
    v_out[...] = v_in[...]
    first, second = bit_orders(n_dp)
    for i, step in enumerate([1] + first):
        copy = remote(v_out, v_got.at[i], v_send.at[i], v_recv.at[i], (flip(d, step), z))
        copy.wait()
        v_out[...] += v_got[i]
    v_base = len(first) + 1
    zv = []
    for k in range(1, n_tp):
        peer = lax.rem(z + k, n_tp)
        zv.append(remote(v_out, v_got.at[v_base + k - 1], z_send.at[0, k - 1], z_recv.at[0, k - 1], (d, peer)))
    fill_places(ones, layout, width, n_tp)

    def add_three(dst, src):
        for g in range(3):
            add_rows(dst.at[g], src.at[g])

    ways = ([s // 2 for s in first[::-1]], [s // 2 for s in second[::-1]])
    n_stage = len(ways[0])
    held = layout.total

    def a_ready(i):
        a_load[i].wait()
        a_swap[i].wait_recv()
        src = (a1, a0)[i]
        part = pl.ds(0 if i else a0.shape[2], src.shape[2])
        for e in range(half):
            add_rows(a_mine.at[e, part], a_core.at[e, part])

    def a_group(base, count, at):
        cut = count // 2 // 16 * 16
        return [
            Fold(
                lambda ref, e, lo=lo, size=size: ref.at[e, pl.ds(lo, size)],
                a_mine, a_two, ways[h], own, d, z, h_send.at[at + h], h_recv.at[at + h],
            )
            for h, (lo, size) in enumerate(((base, cut), (base + cut, count - cut)))
        ]

    def start(group):
        for p in group:
            p.start()

    def step(group, add):
        for fold in group:
            fold.finish(add)
            if fold.stage < n_stage:
                fold.start()

    a_ready(0)
    side_folds = a_group(a_rows, rows - a_rows, 2) if mirror else []
    start(side_folds)
    folds = []
    for j, b in enumerate(order):
        for g in range(3):
            f_load[3 * j + g].wait()
            f_core[3 * j + g].wait_recv()
        for i in range(half):
            add_three(ff_mine.at[b, i], ff_core.at[b, i])
        fold = Fold(
            lambda ref, e, b=b: ref.at[b, e], ff_mine, ff_two, ways[j % 2], own, d, z, f_send.at[j], f_recv.at[j]
        )
        fold.start()
        folds.append(fold)
    a_ready(1)
    main_folds = a_group(0, a_rows, 0)
    line_f = LineSum(lambda b: ff_mine.at[b, own], lambda w, b: ff_got.at[w, b], d, z, n_tp, lf_send, lf_recv)
    line_a = LineSum(
        lambda b: a_cols.at[b, pl.ds(0, held)], lambda w, b: a_got.at[w, b, pl.ds(0, held)], d, z, n_tp, la_send, la_recv
    )
    line_b = LineSum(
        lambda b: a_cols.at[b, pl.ds(held, 4 * ch)],
        lambda w, b: a_got.at[w, b, pl.ds(held, 4 * ch)],
        d, z, n_tp, lb_send, lb_recv,
    )

    def pass_on(line, b, add):
        @pl.when(b != z)
        def _():
            line.take(b, add)
            line.give(b)

    for t in range(n_stage - 1):
        step(side_folds, add_rows)
        step(folds, add_three)
        if t == 0:
            start(main_folds)
    if mirror:
        step(side_folds, add_rows)
        k = a1.shape[2] // 4
        for s in range(n_tp):
            place = one_hot(ch, width, lambda r, col, s=s: col - r == s * ch)
            for c in range(4):
                block = a_mine[own, pl.ds(a_rows + c * k, k)]
                a_cols[s, pl.ds(held + c * ch, ch)] = mm_nt(place, block).astype(BF)
        for b in order:
            pass_on(line_b, b, add_rows)
    for fold, b in zip(folds, order):
        fold.finish(add_three)
        pass_on(line_f, b, add_three)
    swaps = []
    if mirror:
        line_b.take(z, add_rows)
        for c in range(4):
            f_own[c] = a_cols[z, pl.ds(held + c * ch, ch)]
        swaps.append(remote(f_own, f_got, f_swap_send.at[0], f_swap_recv.at[0], (n_dp - 1 - d, z)))
        swaps.append(remote(f_own, f_edge, f_swap_send.at[1], f_swap_recv.at[1], (across_of(d, n_dp), z)))
    for t in range(1, n_stage):
        step(main_folds, add_rows)
    line_f.take(z, add_three)
    put = pltpu.make_async_copy(ff_mine.at[z, own], ff_out.at[d], local.at[0])
    put.start()
    put.wait()
    pieces = [(0, 0, vec, first), (1, 0, vec, second)]
    if vec % 32 == 0:
        pieces += [(2, 0, vec // 2, first), (2, vec // 2, vec // 2, second)]
    else:
        pieces += [(2, 0, vec, first)]
    sf = [
        Spread(lambda s, g=g, lo=lo, n=n: ff_out.at[s, g, pl.ds(lo, n)], way + [1], d, z, s_send.at[i], s_recv.at[i])
        for i, (g, lo, n, way) in enumerate(pieces)
    ]
    start(sf)
    step(main_folds, add_rows)
    n_pieces = len(layout.pieces())
    groups = {}
    for i, (packed, low, count, _, _, _) in enumerate(layout.pieces()):
        groups.setdefault((packed, count), []).append((low, i))
    for (packed, count), found in groups.items():
        size = chunk_of(count)

        @pl.loop(0, count // size)
        def _(i, packed=packed, found=found, size=size):
            for s in range(n_tp):
                total = jnp.zeros((size, 128), F32)
                for low, j in found:
                    block = a_mine[own, pl.ds(low + i * size, size)]
                    total += mm_nt(block, ones[s * n_pieces + j])
                a_cols[s, pl.ds(packed + i * size, size)] = total.astype(BF)

    for stage in range(len(first) + 1):
        for p in sf:
            p.wait()
            if stage < len(first):
                p.start()
        if stage == 0:
            for b in order:
                pass_on(line_a, b, add_rows)

    line_a.take(z, add_rows)
    if mirror:
        upper = d > n_dp - 1 - d
        turn_low = one_hot(k, 2 * k, lambda r, col: r + col == 2 * k)
        turn_high = one_hot(k, 2 * k, lambda r, col: r + k + col == 2 * k)
        corner = one_hot(k, 2 * k, lambda r, col: r + col == 0)
        stay_low = one_hot(k, 2 * k, lambda r, col: r == col)
        stay_high = one_hot(k, 2 * k, lambda r, col: r + k == col)
        lane = lax.broadcasted_iota(jnp.int32, (1, 2 * k), 1)
        zero_at = jnp.logical_and(lane == 0, d == 0)
        for copy in swaps:
            copy.wait()
        for c in range(4):
            low, high = jnp.where(upper, f_got[c], f_own[c]), jnp.where(upper, f_own[c], f_got[c])
            plain = mm(low, stay_low) + mm(high, stay_high)
            if c % 2 == 0:
                edge = jnp.where(d == n_dp // 2, f_edge[c + 1], f_edge[c])
                turned = mm(low, turn_low) + mm(high, turn_high) + mm(edge, corner)
            else:
                plain = jnp.where(zero_at, 0.0, plain)
                edge = jnp.where(d == n_dp // 2, 0.0, f_edge[c].astype(F32)).astype(BF)
                turned = -(mm(low, turn_low) + mm(high, turn_high) + mm(edge, corner))
            f_out[c] = jnp.where(upper, turned, plain)
    a_out[...] = a_cols[z, pl.ds(0, layout.total)].astype(F32)
    for copy in zv:
        copy.wait()
    for k in range(1, n_tp):
        v_out[...] += v_got[v_base + k - 1]
    own_x.wait()
    for copy in zx:
        copy.wait_recv()
    for copy in f_core + a_swap + zx:
        copy.wait_send()
    for b in range(n_tp):
        line_f.drain(b)
        line_a.drain(b)
        if mirror:
            line_b.drain(b)
    for p in sf:
        p.drain()


def scatter_grads(ff, a0, a1, vectors, x_in, n_dp, n_tp):
    width = a0.shape[2]
    rows = a0.shape[1] + a1.shape[1]
    vec, hid = ff[0].shape[2:]
    ch = width // n_tp
    k = a1.shape[1] // 4
    mirror = k % 128 == 0
    a_rows = a0.shape[1] if mirror else rows
    held = Pack(a_rows, ch).total
    packed = held + (4 * ch if mirror else 0)
    cut = rows // 2 // 16 * 16
    half = n_dp // 2
    anyspace = pl.BlockSpec(memory_space=pl.ANY)
    vmem = pl.BlockSpec(memory_space=pltpu.VMEM)
    dma = pltpu.SemaphoreType.DMA
    pairs = lambda v: v.reshape((half, 2) + v.shape[1:])
    most = max(4, n_tp, 2)
    return pl.pallas_call(
        functools.partial(scatter_kernel, n_dp, n_tp, cut, mirror),
        out_shape=(
            jax.ShapeDtypeStruct((n_dp, 3, vec, hid), BF),
            jax.ShapeDtypeStruct((held, 128), F32),
            jax.ShapeDtypeStruct((4, ch, 2 * k), F32),
            jax.ShapeDtypeStruct(vectors.shape, F32),
            jax.ShapeDtypeStruct((n_tp, x_in.shape[0], x_in.shape[1] // n_tp, width), BF),
        ),
        in_specs=[anyspace] * 5 + [vmem, anyspace],
        out_specs=(anyspace, vmem, vmem, vmem, anyspace),
        scratch_shapes=[
            pltpu.VMEM((n_tp, half, 3, vec, hid), BF),
            pltpu.VMEM((half, rows, width), BF),
            pltpu.VMEM((n_tp, half, 3, vec, hid), BF),
            pltpu.VMEM((half, rows, width), BF),
            pltpu.VMEM((n_tp, half - 1, 3, vec, hid), BF),
            pltpu.VMEM((half - 1, rows, width), BF),
            pltpu.VMEM((n_tp, packed, 128), BF),
            pltpu.VMEM((2, n_tp, 3, vec, hid), BF),
            pltpu.VMEM((2, n_tp, packed, 128), BF),
            pltpu.VMEM(((half - 1).bit_length() + n_tp,) + vectors.shape, F32),
            pltpu.VMEM((n_tp * len(Pack(a_rows, ch).pieces()), 128, width), BF),
            pltpu.VMEM((4, ch, k), BF),
            pltpu.VMEM((4, ch, k), BF),
            pltpu.VMEM((4, ch, k), BF),
            dma((4, most)),
            dma((4, most)),
            dma((4, most)),
            dma((n_tp, half - 1)),
            dma((n_tp, half - 1)),
            dma((4, half - 1)),
            dma((4, half - 1)),
            dma((2, n_tp)),
            dma((2, n_tp)),
            dma((2, n_tp)),
            dma((2, n_tp)),
            dma((2, n_tp)),
            dma((2, n_tp)),
            dma((2, n_tp - 1)),
            dma((2, n_tp - 1)),
            dma((4, n_dp - 1)),
            dma((4, n_dp - 1)),
            dma(((half - 1).bit_length() + 1,)),
            dma(((half - 1).bit_length() + 1,)),
            dma((2,)),
            dma((2,)),
            dma((2,)),
        ],
        compiler_params=pltpu.CompilerParams(
            collective_id=1, has_side_effects=True, vmem_limit_bytes=60 * 1024 * 1024
        ),
        name="scatter_grads",
    )(*[pairs(g) for g in ff], pairs(a0), pairs(a1), vectors, x_in)


def body(
    tokens,
    lengths,
    cotangent,
    norm1_gain,
    norm1_bias,
    in_weight,
    in_bias,
    filter_base,
    filter_mod,
    out_weight,
    out_bias,
    norm2_gain,
    norm2_bias,
    gate_weight,
    up_weight,
    down_weight,
    down_bias,
):
    micro, local, group, width = tokens.shape
    n_tp = lax.axis_size("tp")
    n_dp = lax.axis_size("dp")
    z = lax.axis_index("tp")
    d = lax.axis_index("dp")
    slot_len = local * n_tp
    own = micro * group // n_tp
    per_micro = min(group, own)
    ch = in_weight.shape[2]
    vec = width // n_dp
    hid = gate_weight.shape[1]
    table = jnp.asarray(packed_table(slot_len))
    scale = 0.5 / slot_len

    rows = slot_len // n_dp
    last = n_dp - 1
    upper = d > last - d
    mirror = rows % 128 == 0
    filters = jnp.stack([filter_base, filter_mod])
    across = [(i, (n_dp - i) % n_dp) for i in range(n_dp) if i % (n_dp // 2)] + [(0, n_dp // 2), (n_dp // 2, 0)]
    if not mirror:
        got = lax.ppermute(filters[:, :, rows:], "dp", [(i, last - i) for i in range(n_dp)])
        got_edge = lax.ppermute(filters[:, :, :1], "dp", across)
        direct = jnp.where(upper, got, filters[:, :, :rows]).astype(F32)
        mirror_lower = jnp.concatenate([got[:, :, 1:], got_edge], axis=2)
        mirror_upper = filters[:, :, 1 : rows + 1]
        image = jnp.flip(jnp.where(upper, mirror_upper, mirror_lower), 2).astype(F32)
        nyquist = got_edge[:, 0, 0].astype(F32)
        edge = ((jnp.arange(rows) == 0) & (d == 0))[None, :, None]
        half_real = jnp.where(edge, direct[:, 0], direct[:, 0] + image[:, 0])
        half_imag = jnp.where(edge, nyquist[:, None], direct[:, 1] - image[:, 1])
        half = jnp.stack([half_real, half_imag], 1).astype(BF).reshape(4 * rows, ch)

    slice_of = [2 * i if 2 * i < n_dp else 2 * (last - i) + 1 for i in range(n_dp)]

    a_in = [in_weight.transpose(1, 0, 2).reshape(3 * vec, ch), out_weight.T] + ([] if mirror else [half])
    a_in = jnp.concatenate(a_in)
    f_in = filters.transpose(0, 1, 3, 2).reshape(4, ch, 2 * rows)
    vectors = jnp.stack([norm1_gain, norm1_bias, norm2_gain, norm2_bias, out_bias, down_bias])
    vectors = jnp.concatenate([vectors, in_bias])
    vectors = jnp.pad(vectors, ((0, 16 - 9), (0, width - vec)))
    share = hid // n_dp
    ff = [w.reshape(n_dp, vec, hid) for w in (gate_weight, up_weight, down_weight)]
    x_in = tokens.transpose(0, 2, 1, 3).reshape(n_tp, own, local, width)
    layout = Pack(a_in.shape[0], ch)
    ffw, aw, x_own = gather_weights(ff, layout.pack(a_in), a_in.shape[0], f_in, vectors, x_in, n_dp, n_tp)
    cotangent, _ = lax.optimization_barrier((cotangent, aw))
    vectors = aw[:, 4 * vec + 4 * rows :, :vec].astype(F32).transpose(1, 0, 2).reshape(16, width)
    slots = [slice_of.index(k) for k in range(n_dp)]
    direct = vec % 16 == 0 and hid == width
    if direct:
        ws = [
            (ffw, (n_dp, n_tp, None, vec, hid), (0, 0, g, 0, 0), (n_dp, 1, None, vec, hid), lambda p, g=g: (0, p, g, 0, 0))
            for g in range(3)
        ]
        a_view = aw
    else:
        natural = [ffw[:, :, g].transpose(1, 0, 2, 3).reshape(n_tp, width, hid) for g in range(2)]
        natural.append(ffw[:, :, 2].reshape(n_dp, n_tp, share, width).transpose(1, 0, 2, 3).reshape(n_tp, hid, width))
        ws = [
            (w[None], (1,) + w.shape, (0, 0, 0, 0), (1, 1) + w.shape[1:], lambda p: (0, p, 0, 0)) for w in natural
        ]
        a_view = aw[:, : 4 * vec].reshape(n_dp, 4, vec, width).transpose(1, 0, 2, 3).reshape(1, 4 * width, width)

    def to_owner(x):
        pieces = x.transpose(0, 2, 1, 3).reshape(n_tp, own, local, width)
        return lax.all_to_all(pieces, "tp", 0, 1, tiled=False).reshape(own, slot_len, width)

    def to_slots(x):
        whole = lax.all_to_all(x.reshape(n_tp, own * local, width), "tp", 0, 0, tiled=False)
        return whole.reshape(micro, group, local, width).transpose(0, 2, 1, 3)

    c_own = to_owner(cotangent)
    flat_len = lax.dynamic_slice_in_dim(lengths.reshape(-1), z * own, own, 0)
    first = 4 * vec // rows
    gating, nsum, mixing, spec, conv, gated = mix(x_own, flat_len, a_view, vectors, table, aw, first, rows, slots, scale)
    middle, n2, act, side, hidden, out = feed(x_own, gated, flat_len, a_view, ws, n_tp, hid, vectors)
    layer_out = to_slots(out)
    e, *d_ff = feed_back(c_own, n2, act, side, hidden, flat_len, ws)
    mg, cg, gtg, d_out, sums = branch_back(e, middle, c_own, gating, conv, flat_len, a_view, vectors)
    layer_out, cg = lax.optimization_barrier((layer_out, cg))
    vg, d_filter, cgv = spectral_back(cg, spec, mixing, flat_len, table, aw, first, rows, slots, scale)
    ig, d_first, sums = input_back(vg, gtg, x_own, mg, nsum, cgv, flat_len, a_view, d_out, sums, vectors)
    if not direct:
        d_ff = [
            g[0].reshape(n_tp, n_dp, vec, hid).transpose(1, 0, 2, 3) for g in d_ff[:2]
        ] + [d_ff[2][0].reshape(n_tp, n_dp, vec, hid).transpose(1, 0, 2, 3)]
        d_first = d_first.reshape(4, n_dp, vec, width).transpose(1, 0, 2, 3).reshape(n_dp, 4 * vec, width)
    ffg, ag, full, vecs, input_grad = scatter_grads(d_ff, d_first, d_filter, sums, ig, n_dp, n_tp)
    input_grad = input_grad.reshape(micro, group, local, width).transpose(0, 2, 1, 3)
    ag = layout.unpack(ag)
    gate_grad = ffg[:, 0].reshape(width, hid).astype(F32)
    up_grad = ffg[:, 1].reshape(width, hid).astype(F32)
    down_grad = ffg[:, 2].reshape(hid, width).astype(F32)
    in_grad = ag[: 3 * vec].reshape(3, vec, ch).transpose(1, 0, 2)
    out_grad = ag[3 * vec : 4 * vec].T
    if mirror:
        full = full.reshape(2, 2, ch, 2 * rows).transpose(0, 1, 3, 2)
    else:
        fgrad = ag[4 * vec :].astype(BF).reshape(2, 2, rows, ch)
        other = lax.ppermute(fgrad, "dp", [(i, last - i) for i in range(n_dp)])
        low_slice = jnp.where(upper, other, fgrad)
        high_slice = jnp.where(upper, fgrad, other)
        both = jnp.concatenate([low_slice, high_slice], axis=2)
        follow = lax.ppermute(fgrad[:, :, :1], "dp", across)
        zero = jnp.zeros_like(follow[:, 0])
        follow = jnp.where(d == n_dp // 2, jnp.stack([follow[:, 1], zero], 1), follow)
        mirrored = jnp.flip(jnp.concatenate([both[:, :, 1:], follow], axis=2), 2)
        mirrored = jnp.stack([mirrored[:, 0], -mirrored[:, 1]], 1)
        plain = jnp.stack(
            [both[:, 0], jnp.where((d == 0) & (jnp.arange(2 * rows) == 0)[None, :, None], 0.0, both[:, 1].astype(F32)).astype(BF)], 1
        )
        full = jnp.where(upper, mirrored, plain).astype(F32)
    piece = width // (n_dp * n_tp)
    vecs = lax.dynamic_slice_in_dim(vecs, (d * n_tp + z) * piece, piece, 1)
    return (
        layer_out,
        input_grad,
        vecs[0],
        vecs[1],
        in_grad,
        vecs[6:9],
        full[0],
        full[1],
        out_grad,
        vecs[4],
        vecs[2],
        vecs[3],
        gate_grad,
        up_grad,
        down_grad,
        vecs[5],
    )


def solution(mesh):
    in_specs = (
        P(None, "tp", "dp", None),
        P(None, "dp"),
        P(None, "tp", "dp", None),
        P("dp"),
        P("dp"),
        P("dp", None, "tp"),
        P(None, "dp"),
        P(None, "dp", "tp"),
        P(None, "dp", "tp"),
        P("tp", "dp"),
        P("dp"),
        P("dp"),
        P("dp"),
        P(None, "tp"),
        P(None, "tp"),
        P("tp", None),
        P("dp"),
    )
    out_specs = (
        P(None, "tp", "dp", None),
        P(None, "tp", "dp", None),
        P(("dp", "tp")),
        P(("dp", "tp")),
        P("dp", None, "tp"),
        P(None, ("dp", "tp")),
        P(None, "dp", "tp"),
        P(None, "dp", "tp"),
        P("tp", "dp"),
        P(("dp", "tp")),
        P(("dp", "tp")),
        P(("dp", "tp")),
        P(None, "tp"),
        P(None, "tp"),
        P("tp", None),
        P(("dp", "tp")),
    )
    return jax.shard_map(body, mesh=mesh, in_specs=in_specs, out_specs=out_specs, check_vma=False)
```

```python
import functools
import math

import jax
import jax.numpy as jnp
import numpy as np
from jax import lax
from jax.experimental import pallas as pl
from jax.experimental.pallas import tpu as pltpu
from jax.sharding import PartitionSpec as P

EPSILON = 1e-05
ROWS = 64
BF = jnp.bfloat16
F32 = jnp.float32
GELU_A = math.sqrt(2.0 / math.pi)
GELU_B = 0.044715


def packed_table(slot_len):
    frequency = np.arange(slot_len, dtype=np.int64)[:, None]
    position = np.arange(slot_len, dtype=np.int64)[None, :]
    angles = (frequency * position % (2 * slot_len)).astype(np.float32) * np.float32(math.pi / slot_len)
    top = np.cos(angles)
    low = -np.sin(angles)
    low[0] = 1.0 - 2.0 * (np.arange(slot_len) % 2)
    return np.concatenate([top, low]).astype(np.float32).astype(jnp.bfloat16)


def shift(x, axis, step):
    n = lax.axis_size(axis)
    return lax.ppermute(x, axis, [(i, (i + step) % n) for i in range(n)])


def exchange(pieces, place, n):
    out = [(place, lax.dynamic_index_in_dim(pieces, place, 0, keepdims=False))]
    for step in range(1, n):
        block = lax.dynamic_index_in_dim(pieces, (place + step) % n, 0, keepdims=False)
        out.append(((place + n - step) % n, shift(block, "tp", step)))
    return out


def mm(a, b):
    return lax.dot_general(a, b, (((1,), (0,)), ((), ())), preferred_element_type=F32)


def mm_nt(a, b):
    return lax.dot_general(a, b, (((1,), (1,)), ((), ())), preferred_element_type=F32)


def mm_tn(a, b):
    return lax.dot_general(a, b, (((0,), (0,)), ((), ())), preferred_element_type=F32)


def mean_of(v):
    return jnp.sum(v, axis=-1, keepdims=True) * (1.0 / v.shape[-1])


def standardize(v):
    centred = v - mean_of(v)
    inverse = lax.rsqrt(mean_of(centred * centred) + EPSILON)
    return centred * inverse, inverse


def norm_back(e, gain, s, q):
    eg = e * gain
    return q * (eg - mean_of(eg) - s * mean_of(eg * s))


def gelu_parts(v):
    square = v * v
    th = jnp.tanh(v * (GELU_A + (GELU_A * GELU_B) * square))
    rise = 0.5 + 0.5 * th
    act = v * rise
    slope = rise + act * (1.0 - th) * (GELU_A + (3.0 * GELU_A * GELU_B) * square)
    return act, slope


def live(rows, first, count):
    at = lax.broadcasted_iota(jnp.int32, (rows, 1), 0) + first
    return jnp.where(at < count, 1.0, 0.0)


def joined(ref):
    v = ref[...]
    return v.reshape(-1, v.shape[-1])


def two_part_dot(a, b, dims):
    high = a.astype(BF)
    low = (a - high.astype(F32)).astype(BF)
    return lax.dot_general(high, b, (dims, ((), ())), preferred_element_type=F32) + lax.dot_general(
        low, b, (dims, ((), ())), preferred_element_type=F32
    )


def top_row(v, rows=8):
    r = lax.broadcasted_iota(jnp.int32, (rows, v.shape[1]), 0)
    return jnp.where(r == 0, jnp.broadcast_to(v, (rows, v.shape[1])), 0.0)


def mix_kernel(
    tile, tiles, slots, scale, lens, x, wv, wg, wc, vec, table, f0, f1, f2, f3,
    gating, nsum, mixing, spec, conv, gated, vals, gats,
):
    i = pl.program_id(0)
    own, n = vals.shape[1], vals.shape[2]
    blocks, cb = vals.shape[0], vals.shape[3]

    @pl.when(i < own * tiles)
    def _():
        s, t = i // tiles, lax.rem(i, tiles)
        here = pl.ds(t * tile, tile)
        count = lens[s]
        valid = live(tile, t * tile, count)
        std, _ = standardize(x[0].astype(F32))
        normed = (std * vec[0:1] + vec[1:2]).astype(BF)
        v = ((mm(normed, joined(wv)) + vec[6:7]) * valid).astype(BF)
        g = (mm(normed, joined(wg)) + vec[7:8]).astype(BF)
        gating[0] = g
        for c in range(blocks):
            vals[c, s, here] = v[:, c * cb : (c + 1) * cb]
            gats[c, s, here] = g[:, c * cb : (c + 1) * cb]
        part = top_row(jnp.sum(normed.astype(F32) * valid, axis=0, keepdims=True))

        @pl.when(t == 0)
        def _():
            nsum[s] = part

        @pl.when(t > 0)
        def _():
            nsum[s] += part

        @pl.when(t == tiles - 1)
        def _():
            length = count.astype(F32)
            cond = two_part_dot(nsum[s], joined(wc), ((1,), (0,))) + length * vec[8:9]
            mixing[s] = jnp.tanh(cond / length)

    @pl.when(i >= own * tiles)
    def _():
        c = i - own * tiles
        columns = pl.ds(pl.multiple_of(c * cb, cb), cb)
        raw = [mm(table[...], vals[c, s]) for s in range(own)]
        edge = lax.broadcasted_iota(jnp.int32, (n, 1), 0) == 0
        outs = []
        for s in range(own):
            v = raw[s]
            spec[s] = v.astype(BF)
            sr, si = v[:n], v[n:]
            fr, fi, _, _ = filters_of((f0, f1, f2, f3), slots, mixing[s, 0:1, columns])
            fr2 = jnp.where(edge, fi, fr)
            fi = jnp.where(edge, 0.0, fi)
            prod = jnp.concatenate([(fr * sr - fi * si).astype(BF), (fr2 * si + fi * sr).astype(BF)])
            outs.append(mm_tn(table[...], prod))
        for s in range(own):
            out = outs[s] * scale
            conv[s] = out.astype(BF)
            gated[s] = (out * gats[c, s].astype(F32)).astype(BF)


def filters_of(refs, slots, mix):
    base_r, base_i, mod_r, mod_i = [jnp.concatenate([ref[j] for j in slots]).astype(F32) for ref in refs]
    return base_r + mix * mod_r, base_i + mix * mod_i, mod_r, mod_i


def feed_kernel(tile, n_tp, lens, x, gated, w_out, hg, hu, hd, vec, middle, n2, act, side, hidden, out, wg, wu, wd, sems):
    s, t = pl.program_id(0), pl.program_id(1)
    begin = (s == 0) & (t == 0)
    copies = [
        pltpu.make_async_copy(src.at[:, :, g] if len(src.shape) == 5 else src, dst, sems.at[g])
        for g, (src, dst) in enumerate(((hg, wg), (hu, wu), (hd, wd)))
    ]

    @pl.when(begin)
    def _():
        for copy in copies:
            copy.start()

    valid = live(tile, t * tile, lens[s])
    mid = x[0].astype(F32) + valid * (mm_nt(gated[0], joined(w_out)) + vec[4:5])
    middle[0] = mid.astype(BF)
    std, _ = standardize(mid)
    normed = (std * vec[2:3] + vec[3:4]).astype(BF)
    n2[0] = normed

    @pl.when(begin)
    def _():
        for copy in copies:
            copy.wait()

    feed = jnp.zeros(mid.shape, F32)
    for p in range(n_tp):
        gate = mm(normed, joined(wg.at[:, p]))
        up = mm(normed, joined(wu.at[:, p]))
        a, slope = gelu_parts(gate)
        act[0, p] = a.astype(BF)
        side[0, p] = (up * slope).astype(BF)
        h = (a * up).astype(BF)
        hidden[0, p] = h
        feed += mm(h, joined(wd.at[:, p]))
    out[:, 0] = (mid + valid * (feed + vec[5:6])).astype(BF).reshape(out.shape[0], out.shape[2], out.shape[3])


def feed_back_kernel(tile, lens, cot, n2, act, side, hidden, wg, wu, wd, e_out, d_gate, d_up, d_down, e_acc, acc_g, acc_u, acc_d, fgs, ggs, ugs):
    p, s = pl.program_id(0), pl.program_id(1)
    n = cot.shape[1]

    @pl.when(p == 0)
    def _():
        e_acc[s] = jnp.zeros(e_acc.shape[1:], F32)

    down, gate, up = joined(wd.at[:, 0]), joined(wg.at[:, 0]), joined(wu.at[:, 0])
    for i in range(n // tile):
        here = pl.ds(i * tile, tile)
        fg = (cot[0, here].astype(F32) * live(tile, i * tile, lens[s])).astype(BF)
        fgs[here] = fg
        hg = mm_nt(fg, down)
        ggs[here] = (hg * side[0, 0, here].astype(F32)).astype(BF)
        ugs[here] = (hg * act[0, 0, here].astype(F32)).astype(BF)
    for i in range(n // tile):
        here = pl.ds(i * tile, tile)
        e_acc[s, here] += mm_nt(ggs[here], gate) + mm_nt(ugs[here], up)
    own = e_acc.shape[0]
    sides = ((acc_g, d_gate, n2.at[0], ggs), (acc_u, d_up, n2.at[0], ugs), (acc_d, d_down, hidden.at[0, 0], fgs))

    def put(out, v):
        out[:, 0] = v.astype(BF).reshape(out.shape[0], out.shape[2], out.shape[3])

    if own == 1:
        for acc, out, left, right in sides:
            put(out, mm_tn(left[...], right[...]))
    else:

        @pl.when(s == 0)
        def _():
            for acc, out, left, right in sides:
                acc[...] = mm_tn(left[...], right[...])

        @pl.when(s == own - 1)
        def _():
            for acc, out, left, right in sides:
                put(out, acc[...] + mm_tn(left[...], right[...]))

    if own > 2:

        @pl.when((s > 0) & (s < own - 1))
        def _():
            for acc, out, left, right in sides:
                acc[...] += mm_tn(left[...], right[...])

    @pl.when(p == pl.num_programs(0) - 1)
    def _():
        e_out[0] = e_acc[s].astype(BF)


def eights(v):
    return jnp.sum(v.reshape(-1, 8, v.shape[-1]), axis=0)


def branch_back_kernel(tile, lens, e, middle, cot, gating, conv, w_out, vec, mg_out, cg, gtg, d_out, sums, acc, bgs, gts, part_sums):
    s, t = pl.program_id(0), pl.program_id(1)
    begin = (s == 0) & (t == 0)
    end = (s == pl.num_programs(0) - 1) & (t == pl.num_programs(1) - 1)

    @pl.when(begin)
    def _():
        acc[...] = jnp.zeros(acc.shape, F32)
        part_sums[...] = jnp.zeros(part_sums.shape, F32)

    count = lens[s]
    gain = vec[2:3]
    step = min(ROWS, tile)
    for i in range(tile // step):
        here = pl.ds(i * step, step)
        valid = live(step, t * tile + i * step, count)
        up = cot[0, here].astype(F32)
        std, inverse = standardize(middle[0, here].astype(F32))
        grad = e[0, here].astype(F32)
        mg = up + norm_back(grad, gain, std, inverse)
        mg_out[0, here] = mg.astype(BF)
        bgr = (mg * valid).astype(BF)
        bgs[here] = bgr
        fg = (up * valid).astype(BF).astype(F32)
        for j, v in enumerate((grad * std, grad, bgr.astype(F32), fg)):
            part_sums[j] += eights(v)
    ggr = mm(bgs[...], joined(w_out))
    for i in range(tile // step):
        here = pl.ds(i * step, step)
        gate, out = gating[0, here].astype(F32), conv[0, here].astype(F32)
        g = ggr[i * step : (i + 1) * step]
        cg[0, here] = (g * gate).astype(BF)
        gtg[0, here] = (g * out).astype(BF)
        gts[here] = (out * gate).astype(BF)
    acc[...] += mm_tn(bgs[...], gts[...])

    @pl.when(end)
    def _():
        d_out[...] = acc[...].astype(BF).reshape(d_out.shape)
        sums[...] = jnp.zeros(sums.shape, F32)
        for j in range(4):
            sums[j : j + 1] = jnp.sum(part_sums[j], axis=0, keepdims=True)


def spectral_back_kernel(slots, scale, lens, cg, spec, mixing, table, f0, f1, f2, f3, vg, fgrad, cgv):
    own = cg.shape[0]
    n = cg.shape[1]
    size = n // len(slots)
    raw = [mm(table[...], cg[s]) for s in range(own)]
    edge = lax.broadcasted_iota(jnp.int32, (n, 1), 0) == 0
    outs, total = [], None
    for s in range(own):
        v = raw[s] * scale
        pr, pi = v[:n], v[n:]
        mix = mixing[s, 0:1]
        fr, fi, mod_r, mod_i = filters_of((f0, f1, f2, f3), slots, mix)
        fr2 = jnp.where(edge, fi, fr)
        fi = jnp.where(edge, 0.0, fi)
        sg = jnp.concatenate([(fr * pr + fi * pi).astype(BF), (fr2 * pi - fi * pr).astype(BF)])
        outs.append(mm_tn(table[...], sg))
        sr, si = spec[s, :n].astype(F32), spec[s, n:].astype(F32)
        both = pi * si
        dr = pr * sr + jnp.where(edge, 0.0, both)
        di = jnp.where(edge, both, pi * sr - pr * si)
        mixg = jnp.sum(mod_r * dr + mod_i * di, axis=0, keepdims=True)
        step = mixg * (1.0 - mix * mix) / lens[s].astype(F32)
        cgv[s] = top_row(step.astype(BF).astype(F32))
        parts = (dr, di, mix * dr, mix * di)
        total = parts if total is None else tuple(t + p for t, p in zip(total, parts))
    for s in range(own):
        vg[s] = (outs[s] * live(n, 0, lens[s])).astype(BF)
    for j in range(len(slots)):
        k = slots.index(j)
        for i in range(4):
            fgrad[j, pl.ds(i * size, size)] = total[i][k * size : (k + 1) * size].astype(BF)


def input_back_kernel(tile, lens, vg, gtg, x, mg, nsum, cgv, wv, wg, wc, d_out, sums_in, vec, ig, d_in, sums, acc_v, acc_g, acc_c):
    s, t = pl.program_id(0), pl.program_id(1)
    begin = (s == 0) & (t == 0)
    end = (s == pl.num_programs(0) - 1) & (t == pl.num_programs(1) - 1)
    count = lens[s]

    @pl.when(begin)
    def _():
        for acc in (acc_v, acc_g, acc_c):
            acc[...] = jnp.zeros(acc.shape, F32)
        sums[...] = jnp.zeros(sums.shape, F32)
        sums[2:6] = sums_in[0:4]

    valid = live(tile, t * tile, count)
    cvec = mm_nt(cgv[0].astype(BF), joined(wc))[0:1]
    vgb, gtb = vg[0], gtg[0]
    e = mm_nt(vgb, joined(wv)) + mm_nt(gtb, joined(wg)) + valid * cvec
    std, inverse = standardize(x[0].astype(F32))
    ig[0] = (mg[0].astype(F32) + norm_back(e, vec[0:1], std, inverse)).astype(BF)
    normed = (std * vec[0:1] + vec[1:2]).astype(BF)
    part_v, part_g = mm_tn(normed, vgb), mm_tn(normed, gtb)
    rows = [e * std, e, vgb.astype(F32), gtb.astype(F32)]
    rows = [jnp.sum(r, axis=0, keepdims=True) for r in rows]

    acc_v[...] += part_v
    acc_g[...] += part_g
    for i, r in zip((0, 1, 6, 7), rows):
        sums[i : i + 1] += r

    @pl.when(t == 0)
    def _():
        acc_c[...] += two_part_dot(nsum[0], cgv[0].astype(BF), ((0,), (0,)))
        sums[8:9] += cgv[0, 0:1] * count.astype(F32)

    @pl.when(end)
    def _():
        r = d_out.shape[1]
        shape = (d_in.shape[0], r, d_in.shape[2])
        for i, acc in enumerate((acc_v, acc_g, acc_c)):
            d_in[:, i * r : (i + 1) * r] = acc[...].astype(BF).reshape(shape)
        d_in[:, 3 * r :] = d_out[...]


def call(kernel, grid, lens, ins, in_specs, outs, out_specs, scratch, flops, name, limit=56):
    spec = pltpu.PrefetchScalarGridSpec(
        num_scalar_prefetch=1, grid=grid, in_specs=in_specs, out_specs=out_specs, scratch_shapes=scratch
    )
    moved = sum(math.prod(v.shape) * v.dtype.itemsize for v in list(ins) + list(outs))
    return pl.pallas_call(
        kernel,
        grid_spec=spec,
        out_shape=tuple(outs),
        compiler_params=pltpu.CompilerParams(
            dimension_semantics=("arbitrary",) * len(grid), vmem_limit_bytes=limit * 1024 * 1024
        ),
        cost_estimate=pl.CostEstimate(flops=int(flops), bytes_accessed=int(moved), transcendentals=0),
        name=name,
    )(lens, *ins)


def once(block, index):
    return pl.BlockSpec(block, lambda *_: index, pipeline_mode=pl.Buffered(1))


def shape_of(shape, dtype):
    return jax.ShapeDtypeStruct(shape, dtype)


def filter_specs(fw, n_dp, rows, cb, first):
    return [
        pl.BlockSpec((n_dp, rows, cb), lambda *g, i=i: (0, first + i, g[0])) for i in range(4)
    ]


def mix(x, lens, aw, vec, table, fw, first, rows, slots, scale):
    own, n, width = x.shape
    tile = min(1024, n)
    tiles = n // tile
    steps = own * tiles
    cb = min(256, width)
    blocks = width // cb
    nd, r = aw.shape[0], width // aw.shape[0]
    n_dp = fw.shape[0]

    def tok(i, *_):
        j = jnp.minimum(i, steps - 1)
        return j // tiles, lax.rem(j, tiles), 0

    def chan(i):
        return jnp.maximum(i - steps, 0)

    token = pl.BlockSpec((1, tile, width), tok)
    whole = pl.BlockSpec((own, 8, width), lambda *_: (0, 0, 0))
    column = pl.BlockSpec((own, n, cb), lambda i, *_: (0, 0, chan(i)))
    double = pl.BlockSpec((own, 2 * n, cb), lambda i, *_: (0, 0, chan(i)))
    weights = [once((nd, r, width), (0, g, 0)) for g in range(3)]
    filters = [pl.BlockSpec((n_dp, rows, cb), lambda i, *_, k=k: (0, first + k, chan(i))) for k in range(4)]
    sd = shape_of(x.shape, BF)
    row = shape_of((own, 8, width), F32)
    return call(
        functools.partial(mix_kernel, tile, tiles, slots, scale),
        (steps + blocks,),
        lens,
        [x, aw, aw, aw, vec, table] + [fw] * 4,
        [token] + weights + [once(vec.shape, (0, 0)), once(table.shape, (0, 0))] + filters,
        [sd, row, row, shape_of((own, 2 * n, width), BF), sd, sd],
        (token, whole, whole, double, column, column),
        [pltpu.VMEM((blocks, own, n, cb), BF), pltpu.VMEM((blocks, own, n, cb), BF)],
        4 * own * n * width * width + 8 * own * n * n * width,
        "mix",
    )


def feed(x, gated, lens, aw, ws, n_tp, hid, vec):
    own, n, width = x.shape
    local = n // n_tp
    tile = max(256, local)
    r = width // aw.shape[0]
    tok = pl.BlockSpec((1, tile, width), lambda s, t, *_: (s, t, 0))
    wide = pl.BlockSpec((1, n_tp, tile, hid), lambda s, t, *_: (s, 0, t, 0))
    parts = pl.BlockSpec((tile // local, 1, local, width), lambda s, t, *_: (t, s, 0, 0))
    big = shape_of((own, n_tp, n, hid), BF)
    return call(
        functools.partial(feed_kernel, tile, n_tp),
        (own, n // tile),
        lens,
        [x, gated, aw] + [w[0] for w in ws] + [vec],
        [tok, tok, once((aw.shape[0], r, width), (0, 3, 0))] + [pl.BlockSpec(memory_space=pl.ANY)] * 3 + [once(vec.shape, (0, 0))],
        [shape_of(x.shape, BF), shape_of(x.shape, BF), big, big, big, shape_of((n_tp, own, local, width), BF)],
        (tok, tok, wide, wide, wide, parts),
        [pltpu.VMEM(tuple(v for v in w[1] if v is not None), BF) for w in ws] + [pltpu.SemaphoreType.DMA((3,))],
        2 * own * n * width * (width + 3 * n_tp * hid),
        "feed",
        limit=60,
    )


def feed_back(cot, n2, act, side, hidden, lens, ffw):
    own, n, width = cot.shape
    n_tp, hid = act.shape[1], act.shape[3]
    tile = min(512, n)
    tok = pl.BlockSpec((1, n, width), lambda p, s, *_: (s, 0, 0))
    wide = pl.BlockSpec((1, 1, n, hid), lambda p, s, *_: (s, p, 0, 0))
    w_specs = [pl.BlockSpec(w[3], lambda p, s, *_, f=w[4]: f(p)) for w in ffw]
    nd = [next(v for v in w[3]) for w in ffw]
    sides = [(width, hid), (width, hid), (hid, width)]
    shapes = [(k, n_tp, a // k, b) for k, (a, b) in zip(nd, sides)]
    d_specs = [pl.BlockSpec((shape[0], 1) + shape[2:], lambda p, s, *_: (0, p, 0, 0)) for shape in shapes]
    d_shapes = [shape_of(shape, BF) for shape in shapes]
    return call(
        functools.partial(feed_back_kernel, tile),
        (n_tp, own),
        lens,
        [cot, n2, act, side, hidden] + [w[0] for w in ffw],
        [tok, tok, wide, wide, wide] + w_specs,
        [shape_of(cot.shape, BF)] + d_shapes,
        (pl.BlockSpec((1, n, width), lambda p, s, *_: (jnp.where(p == n_tp - 1, s, 0), 0, 0)), *d_specs),
        [
            pltpu.VMEM(cot.shape, F32),
            pltpu.VMEM((width, hid), F32),
            pltpu.VMEM((width, hid), F32),
            pltpu.VMEM((hid, width), F32),
            pltpu.VMEM((n, width), BF),
            pltpu.VMEM((n, hid), BF),
            pltpu.VMEM((n, hid), BF),
        ],
        12 * own * n * width * n_tp * hid,
        "feed_back",
        limit=60,
    )


def branch_back(e, middle, cot, gating, conv, lens, aw, vec):
    own, n, width = cot.shape
    tile = min(512, n)
    nd, r = aw.shape[0], width // aw.shape[0]
    tok = pl.BlockSpec((1, tile, width), lambda s, t, *_: (s, t, 0))
    return call(
        functools.partial(branch_back_kernel, tile),
        (own, n // tile),
        lens,
        [e, middle, cot, gating, conv, aw, vec],
        [tok] * 5 + [once((nd, r, width), (0, 3, 0)), once(vec.shape, (0, 0))],
        [
            shape_of(cot.shape, BF),
            shape_of(cot.shape, BF),
            shape_of(cot.shape, BF),
            shape_of((nd, r, width), BF),
            shape_of((8, width), F32),
        ],
        (tok, tok, tok, pl.BlockSpec((nd, r, width), lambda *_: (0, 0, 0)), pl.BlockSpec((8, width), lambda *_: (0, 0))),
        [
            pltpu.VMEM((width, width), F32),
            pltpu.VMEM((tile, width), BF),
            pltpu.VMEM((tile, width), BF),
            pltpu.VMEM((4, 8, width), F32),
        ],
        4 * own * n * width * width,
        "branch_back",
    )


def spectral_back(cg, spec, mixing, lens, table, fw, first, rows, slots, scale):
    own, n, width = cg.shape
    cb = min(256, width)
    n_dp = fw.shape[0]
    tok = pl.BlockSpec((own, n, cb), lambda c, *_: (0, 0, c))
    both = pl.BlockSpec((own, 2 * n, cb), lambda c, *_: (0, 0, c))
    one = pl.BlockSpec((own, 8, cb), lambda c, *_: (0, 0, c))
    return call(
        functools.partial(spectral_back_kernel, slots, scale),
        (width // cb,),
        lens,
        [cg, spec, mixing, table] + [fw] * 4,
        [tok, both, one, once(table.shape, (0, 0))] + filter_specs(fw, n_dp, rows, cb, first),
        [shape_of(cg.shape, BF), shape_of((n_dp, 4 * rows, width), BF), shape_of((own, 8, width), F32)],
        (tok, pl.BlockSpec((n_dp, 4 * rows, cb), lambda c, *_: (0, 0, c)), one),
        [],
        8 * own * n * n * width,
        "spectral_back",
    )


def input_back(vg, gtg, x, mg, nsum, cgv, lens, aw, d_out, sums, vec):
    own, n, width = x.shape
    tile = min(512, n)
    nd, r = aw.shape[0], width // aw.shape[0]
    tok = pl.BlockSpec((1, tile, width), lambda s, t, *_: (s, t, 0))
    one = pl.BlockSpec((1, 8, width), lambda s, t, *_: (s, 0, 0))
    weights = [once((nd, r, width), (0, g, 0)) for g in range(3)]
    return call(
        functools.partial(input_back_kernel, tile),
        (own, n // tile),
        lens,
        [vg, gtg, x, mg, nsum, cgv, aw, aw, aw, d_out, sums, vec],
        [tok] * 4 + [one] * 2 + weights + [once((nd, r, width), (0, 0, 0)), once((8, width), (0, 0)), once(vec.shape, (0, 0))],
        [shape_of(x.shape, BF), shape_of((nd, 4 * r, width), BF), shape_of((16, width), F32)],
        (tok, pl.BlockSpec((nd, 4 * r, width), lambda *_: (0, 0, 0)), pl.BlockSpec((16, width), lambda *_: (0, 0))),
        [pltpu.VMEM((width, width), F32)] * 3,
        8 * own * n * width * width,
        "input_back",
    )


MESH = pl.DeviceIdType.MESH


def flip(index, step):
    return index + step - 2 * step * ((index // step) % 2)


def bit_orders(n_dp):
    bits = [1 << b for b in range(1, (n_dp - 1).bit_length())]
    return bits, bits[::-1]


def greet(d, z, n_dp, n_tp, pairs=False):
    barrier = pltpu.get_barrier_semaphore()
    count = greet_pairs(d, z, n_dp) if pairs else 0
    step = 1
    while step < n_dp:
        pl.semaphore_signal(barrier, inc=1, device_id=(flip(d, step), z), device_id_type=MESH)
        step *= 2
        count += 1
    for k in range(1, n_tp):
        pl.semaphore_signal(barrier, inc=1, device_id=(d, lax.rem(z + k, n_tp)), device_id_type=MESH)
        count += 1
    pl.semaphore_wait(barrier, count)


def across_of(d, n):
    return lax.rem(n - d, n) + (n // 2) * (1 - (d % (n // 2) + n // 2 - 1) // (n // 2)) * (1 - 2 * (d // (n // 2)))


def one_hot(rows, cols, test):
    r = lax.broadcasted_iota(jnp.int32, (rows, cols), 0)
    c = lax.broadcasted_iota(jnp.int32, (rows, cols), 1)
    return jnp.where(test(r, c), 1.0, 0.0).astype(BF)


def greet_pairs(d, z, n_dp):
    barrier = pltpu.get_barrier_semaphore()
    for peer in (n_dp - 1 - d, across_of(d, n_dp)):
        pl.semaphore_signal(barrier, inc=1, device_id=(peer, z), device_id_type=MESH)
    return 2


def remote(src, dst, send, recv, target):
    copy = pltpu.make_async_remote_copy(
        src_ref=src, dst_ref=dst, send_sem=send, recv_sem=recv, device_id=target, device_id_type=MESH
    )
    copy.start()
    return copy


class Pack:
    def __init__(self, rows, ch):
        self.rows, self.ch = rows, ch
        self.main = ch // 128
        self.rest = ch % 128
        self.dense = self.rest == 64 and rows % 32 == 0
        self.tail = 0 if not self.rest else rows // 2 if self.dense else rows
        self.total = self.main * rows + self.tail

    def pack(self, v):
        parts = [v[:, i * 128 : (i + 1) * 128] for i in range(self.main)]
        if self.rest:
            left = v[:, self.main * 128 :]
            if self.dense:
                parts.append(jnp.concatenate([left[: self.tail], left[self.tail :]], axis=1))
            else:
                parts.append(jnp.pad(left, ((0, 0), (0, 128 - self.rest))))
        return jnp.concatenate(parts)

    def unpack(self, v):
        parts = [v[i * self.rows : (i + 1) * self.rows] for i in range(self.main)]
        if self.rest:
            left = v[self.main * self.rows :]
            if self.dense:
                parts.append(jnp.concatenate([left[:, :64], left[:, 64:]]))
            else:
                parts.append(left[:, : self.rest])
        return jnp.concatenate(parts, axis=1)

    def pieces(self):
        out = [(i * self.rows, 0, self.rows, 0, 128, i * 128) for i in range(self.main)]
        at = self.main * self.rows
        if self.dense:
            out += [(at, 0, self.tail, 0, 64, self.main * 128), (at, self.tail, self.tail, 64, 64, self.main * 128)]
        elif self.rest:
            out += [(at, 0, self.rows, 0, self.rest, self.main * 128)]
        return out


def lanes_to(width, lane, lanes, column):
    r = lax.broadcasted_iota(jnp.int32, (128, width), 0)
    c = lax.broadcasted_iota(jnp.int32, (128, width), 1)
    inside = (r >= lane) & (r < lane + lanes)
    return jnp.where(inside & (c - r == column - lane), 1.0, 0.0).astype(BF)


def fill_places(ones, layout, width, n_tp):
    pieces = layout.pieces()
    for s in range(n_tp):
        for i, (_, _, _, lane, lanes, column) in enumerate(pieces):
            ones[s * len(pieces) + i] = lanes_to(width, lane, lanes, s * layout.ch + column)


class Line:
    def __init__(self, part, d, z, n, send, recv):
        self.part, self.d, self.z, self.n, self.send, self.recv = part, d, z, n, send, recv

    def _copy(self, way, t, block):
        target = (self.d, self.z + 1 if way == 0 else self.z - 1)
        return pltpu.make_async_remote_copy(
            src_ref=self.part(block),
            dst_ref=self.part(block),
            send_sem=self.send.at[way, t],
            recv_sem=self.recv.at[way, t],
            device_id=target,
            device_id_type=MESH,
        )

    def start(self, t):
        z, n = self.z, self.n

        @pl.when((z >= t) & (z < n - 1))
        def _():
            self._copy(0, t, z - t).start()

        @pl.when((z + t < n) & (z > 0))
        def _():
            self._copy(1, t, z + t).start()

    def wait(self, t):
        z, n = self.z, self.n

        @pl.when(z >= t + 1)
        def _():
            self._copy(0, t, z - 1 - t).wait_recv()

        @pl.when(z + t + 1 < n)
        def _():
            self._copy(1, t, z + 1 + t).wait_recv()

    def drain(self):
        z, n = self.z, self.n
        for t in range(n - 1):

            @pl.when((z >= t) & (z < n - 1))
            def _(t=t):
                self._copy(0, t, z - t).wait_send()

            @pl.when((z + t < n) & (z > 0))
            def _(t=t):
                self._copy(1, t, z + t).wait_send()


class Spread:
    def __init__(self, part, order, d, z, send, recv):
        self.part, self.z, self.send, self.recv = part, z, send, recv
        held, self.steps, used = [d], [], 0
        for step in order:
            self.steps.append((flip(d, step), [(slot, used + i) for i, slot in enumerate(held)]))
            used += len(held)
            held = held + [flip(slot, step) for slot in held]
        self.stage = 0

    def copies(self, stage):
        target, sent = self.steps[stage]
        return [
            pltpu.make_async_remote_copy(
                src_ref=self.part(slot),
                dst_ref=self.part(slot),
                send_sem=self.send.at[i],
                recv_sem=self.recv.at[i],
                device_id=(target, self.z),
                device_id_type=MESH,
            )
            for slot, i in sent
        ]

    def start(self):
        for copy in self.copies(self.stage):
            copy.start()

    def wait(self):
        for copy in self.copies(self.stage):
            copy.wait_recv()
        self.stage += 1

    def drain(self):
        for stage in range(len(self.steps)):
            for copy in self.copies(stage):
                copy.wait_send()


def chunk_of(rows):
    return next((c for c in (128, 96, 64, 48, 32, 16) if rows % c == 0), rows)


def add_rows(dst, src):
    rows = dst.shape[0]
    size = chunk_of(rows)

    @pl.loop(0, rows // size)
    def _(i):
        at = pl.ds(i * size, size)
        dst[at] = dst[at] + src[at]


def lane_place(rows, cols, offset):
    r = lax.broadcasted_iota(jnp.int32, (rows, cols), 0)
    c = lax.broadcasted_iota(jnp.int32, (rows, cols), 1)
    return jnp.where(c - r == offset, 1.0, 0.0).astype(BF)


def gather_kernel(
    n_dp, n_tp, cut, a_rows, mirror, w0, w1, w2, a_in, f_in, vec_in, x_in, ff_out, a_out, x_out, a_z, a_nat, ones, f_got, f_edge,
    la_send, la_recv, lf_send, lf_recv, x_send, x_recv, s_send, s_recv, f_send, f_recv, local,
):
    d, z = lax.axis_index("dp"), lax.axis_index("tp")
    width = a_nat.shape[1]
    ch = width // n_tp
    rows = a_nat.shape[0] - vec_in.shape[0]
    layout = Pack(a_rows, ch)
    own_ff = [pltpu.make_async_copy(w, ff_out.at[:, z, g], local.at[3 + g]) for g, w in enumerate((w0, w1, w2))]
    for copy in own_ff:
        copy.start()
    own_a = pltpu.make_async_copy(a_in, a_z.at[z, pl.ds(0, layout.total)], local.at[1])
    own_a.start()
    greet(d, z, n_dp, n_tp, mirror)
    if mirror:
        k = f_in.shape[2] // 2
        swaps = [
            remote(f_in.at[:, :, pl.ds(k, k)], f_got, f_send.at[0], f_recv.at[0], (n_dp - 1 - d, z)),
            remote(f_in.at[:, :, pl.ds(0, k)], f_edge, f_send.at[1], f_recv.at[1], (across_of(d, n_dp), z)),
        ]
        turn = one_hot(k, k, lambda r, c: r + c == k)
        corner = one_hot(k, k, lambda r, c: r + c == 0)
        upper = d > n_dp - 1 - d
        lane = lax.broadcasted_iota(jnp.int32, (1, k), 1)
        special = jnp.logical_and(lane == 0, d == 0)
        for copy in swaps:
            copy.wait()
        sums = []
        for c in range(4):
            low, high = f_in[c, :, :k], f_in[c, :, k:]
            direct = jnp.where(upper, f_got[c], low).astype(F32)
            image = mm(jnp.where(upper, low, f_got[c]), turn) + mm(jnp.where(upper, high, f_edge[c]), corner)
            if c % 2 == 0:
                nyquist = image
                folded = jnp.where(special, direct, direct + image)
            else:
                folded = jnp.where(special, nyquist, direct - image)
            a_z[z, pl.ds(layout.total + c * ch, ch)] = folded.astype(BF)
    line_a = Line(lambda s: a_z.at[s], d, z, n_tp, la_send, la_recv)
    line_f = Line(lambda s: ff_out.at[d, s], d, z, n_tp, lf_send, lf_recv)
    first, second = bit_orders(n_dp)
    vec = w0.shape[1]

    def block_spreads(block):
        out = []
        for h, order in enumerate((first, second)):
            at = 2 + 2 * block + h
            if vec % 32 == 0:
                part = lambda s, h=h: ff_out.at[s, block, :, pl.ds(h * (vec // 2), vec // 2)]
            else:
                part = lambda s, h=h: ff_out.at[s, block, pl.ds(h, 1 + h)]
            out.append(Spread(part, order + [1], d, z, s_send.at[at], s_recv.at[at]))
        return out

    own_a.wait()
    line_a.start(0)
    fill_places(ones, layout, width, n_tp)
    for t in range(n_tp - 1):
        line_a.wait(t)
        if t + 1 < n_tp - 1:
            line_a.start(t + 1)
    for copy in own_ff:
        copy.wait()
    line_f.start(0)
    half_rows = a_rows // 2
    n_pieces = len(layout.pieces())
    size = chunk_of(half_rows)
    for side in range(2):
        found = []
        for j, (packed, low, count, _, _, _) in enumerate(layout.pieces()):
            if low <= side * half_rows < low + count:
                found.append((packed + side * half_rows - low, j))

        @pl.loop(0, half_rows // size)
        def _(i, found=found, side=side):
            total = jnp.zeros((size, width), F32)
            for s in range(n_tp):
                for packed, j in found:
                    total += mm(a_z[s, pl.ds(packed + i * size, size)], ones[s * n_pieces + j])
            a_nat[pl.ds(side * half_rows + i * size, size)] = total.astype(BF)

    if mirror:
        for c in range(4):
            total = jnp.zeros((k, width), F32)
            for s in range(n_tp):
                place = one_hot(ch, width, lambda r, col, s=s: col - r == s * ch)
                total += mm_tn(a_z[s, pl.ds(layout.total + c * ch, ch)], place)
            a_nat[pl.ds(a_rows + c * k, k)] = total.astype(BF)
    a_nat[rows:] = vec_in[...]
    put = pltpu.make_async_copy(a_nat, a_out.at[d], local.at[2])
    put.start()
    put.wait()
    total_rows = a_nat.shape[0]
    sa = [
        Spread(lambda s: a_out.at[s, pl.ds(0, cut)], first + [1], d, z, s_send.at[0], s_recv.at[0]),
        Spread(lambda s: a_out.at[s, pl.ds(cut, total_rows - cut)], second + [1], d, z, s_send.at[1], s_recv.at[1]),
    ]
    for p in sa:
        p.start()
    stages = len(first) + 1

    def advance(group):
        for p in group:
            p.wait()
            if p.stage < stages:
                p.start()

    blocks = []
    for t in range(n_tp - 1):
        line_f.wait(t)
        if t + 1 < n_tp - 1:
            line_f.start(t + 1)
        for exists, block in ((z >= t + 1, z - 1 - t), (z + t + 1 < n_tp, z + 1 + t)):
            group = block_spreads(block)
            blocks.append((exists, group))

            @pl.when(exists)
            def _(group=group):
                for p in group:
                    p.start()

        if t == 0:
            advance(sa)
    size = x_in.shape[2]
    here = pl.ds(z * size, size)
    own_x = pltpu.make_async_copy(x_in.at[z], x_out.at[:, here], local.at[0])
    own_x.start()
    zx = []
    for k in range(1, n_tp):
        peer = lax.rem(z + k, n_tp)
        zx.append(remote(x_in.at[peer], x_out.at[:, here], x_send.at[k - 1], x_recv.at[k - 1], (d, peer)))
    for stage in range(stages):
        for exists, group in blocks:

            @pl.when(exists)
            def _(group=group):
                advance(group)

        if stage + 1 < stages:
            advance(sa)
    for p in sa:
        p.drain()
    for exists, group in blocks:

        @pl.when(exists)
        def _(group=group):
            for p in group:
                p.drain()

    own_x.wait()
    for copy in zx:
        copy.wait_recv()
    for copy in zx:
        copy.wait_send()
    line_a.drain()
    line_f.drain()


def gather_weights(ff, a_in, a_rows, f_in, vec_in, x_in, n_dp, n_tp):
    width = vec_in.shape[1]
    mirror = f_in.shape[2] % 256 == 0
    ch = width // n_tp
    rows = a_rows + (2 * f_in.shape[2] if mirror else 0)
    k = f_in.shape[2] // 2
    total = rows + vec_in.shape[0]
    cut = total // 2 // 16 * 16
    anyspace = pl.BlockSpec(memory_space=pl.ANY)
    vmem = pl.BlockSpec(memory_space=pltpu.VMEM)
    return pl.pallas_call(
        functools.partial(gather_kernel, n_dp, n_tp, cut, a_rows, mirror),
        out_shape=(
            jax.ShapeDtypeStruct((n_dp, n_tp, 3) + ff[0].shape[1:], BF),
            jax.ShapeDtypeStruct((n_dp, total, width), BF),
            jax.ShapeDtypeStruct((x_in.shape[1], n_tp * x_in.shape[2], width), BF),
        ),
        in_specs=[anyspace] * 4 + [vmem, vmem, anyspace],
        out_specs=(anyspace, anyspace, anyspace),
        scratch_shapes=[
            pltpu.VMEM((n_tp, a_in.shape[0] + (4 * ch if mirror else 0), 128), BF),
            pltpu.VMEM((total, width), BF),
            pltpu.VMEM((n_tp * len(Pack(a_rows, ch).pieces()), 128, width), BF),
            pltpu.VMEM((4, ch, k), BF),
            pltpu.VMEM((4, ch, k), BF),
            pltpu.SemaphoreType.DMA((2, n_tp - 1)),
            pltpu.SemaphoreType.DMA((2, n_tp - 1)),
            pltpu.SemaphoreType.DMA((2, n_tp - 1)),
            pltpu.SemaphoreType.DMA((2, n_tp - 1)),
            pltpu.SemaphoreType.DMA((n_tp - 1,)),
            pltpu.SemaphoreType.DMA((n_tp - 1,)),
            pltpu.SemaphoreType.DMA((2 + 2 * n_tp, n_dp - 1)),
            pltpu.SemaphoreType.DMA((2 + 2 * n_tp, n_dp - 1)),
            pltpu.SemaphoreType.DMA((2,)),
            pltpu.SemaphoreType.DMA((2,)),
            pltpu.SemaphoreType.DMA((6,)),
        ],
        compiler_params=pltpu.CompilerParams(
            collective_id=0, has_side_effects=True, vmem_limit_bytes=48 * 1024 * 1024
        ),
        name="gather_weights",
    )(*ff, a_in, f_in, vec_in, x_in)


class Fold:
    def __init__(self, part, mine, two, order, own, d, z, send, recv):
        self.part, self.mine, self.two, self.z, self.send, self.recv = part, mine, two, z, send, recv
        self.steps, used = [], 0

        def at(mask):
            index, step = own, 1
            while step <= mask:
                if mask & step:
                    index = flip(index, step)
                step *= 2
            return index

        for t, step in enumerate(order):
            masks = [0]
            for later in order[t + 1 :]:
                masks = masks + [m + later for m in masks]
            moves = [(at(m + step), at(m), used + j) for j, m in enumerate(masks)]
            used += len(moves)
            self.steps.append((flip(d, 2 * step), moves))
        self.stage = 0

    def copies(self, stage):
        target, moves = self.steps[stage]
        return [
            pltpu.make_async_remote_copy(
                src_ref=self.part(self.mine, away),
                dst_ref=self.part(self.two, k),
                send_sem=self.send.at[k],
                recv_sem=self.recv.at[k],
                device_id=(target, self.z),
                device_id_type=MESH,
            )
            for away, _, k in moves
        ]

    def start(self):
        for copy in self.copies(self.stage):
            copy.start()

    def finish(self, add):
        for copy, (_, keep, k) in zip(self.copies(self.stage), self.steps[self.stage][1]):
            copy.wait()
            add(self.part(self.mine, keep), self.part(self.two, k))
        self.stage += 1


class LineSum:
    def __init__(self, mine, got, d, z, n, send, recv):
        self.mine, self.got, self.d, self.z, self.n, self.send, self.recv = mine, got, d, z, n, send, recv

    def _copy(self, way, block):
        return pltpu.make_async_remote_copy(
            src_ref=self.mine(block),
            dst_ref=self.got(way, block),
            send_sem=self.send.at[way, block],
            recv_sem=self.recv.at[way, block],
            device_id=(self.d, self.z - 1 if way == 0 else self.z + 1),
            device_id_type=MESH,
        )

    def take(self, block, add):
        z, n = self.z, self.n

        @pl.when((block <= z) & (z < n - 1))
        def _():
            self._copy(0, block).wait_recv()
            add(self.mine(block), self.got(0, block))

        @pl.when((block >= z) & (z > 0))
        def _():
            self._copy(1, block).wait_recv()
            add(self.mine(block), self.got(1, block))

    def give(self, block):
        @pl.when(block < self.z)
        def _():
            self._copy(0, block).start()

        @pl.when(block > self.z)
        def _():
            self._copy(1, block).start()

    def drain(self, block):
        @pl.when(block < self.z)
        def _():
            self._copy(0, block).wait_send()

        @pl.when(block > self.z)
        def _():
            self._copy(1, block).wait_send()


def scatter_kernel(
    n_dp, n_tp, cut, mirror, g0, g1, g2, a0, a1, v_in, x_in, ff_out, a_out, f_out, v_out, x_out,
    ff_mine, a_mine, ff_core, a_core, ff_two, a_two, a_cols, ff_got, a_got, v_got, ones, f_own, f_got, f_edge,
    load, core_send, core_recv, f_send, f_recv, h_send, h_recv, lf_send, lf_recv, la_send, la_recv, lb_send, lb_recv,
    z_send, z_recv, s_send, s_recv, v_send, v_recv, f_swap_send, f_swap_recv, local,
):
    d, z = lax.axis_index("dp"), lax.axis_index("tp")
    width = a0.shape[3]
    rows = a0.shape[2] + a1.shape[2]
    ch = width // n_tp
    a_rows = a0.shape[2] if mirror else rows
    layout = Pack(a_rows, ch)
    vec = g0.shape[3]
    half = n_dp // 2
    side = d % 2
    own = d // 2
    other = (flip(d, 1), z)
    late = z // (n_tp // 2)
    order = [n_tp - 1 - j + late * (2 * j - n_tp + 1) for j in range(n_tp)]
    greet(d, z, n_dp, n_tp, mirror)
    f_core, f_load, a_swap, a_load = [], [], [], []

    def swap_a(g, src, at):
        part = pl.ds(at, src.shape[2])
        a_swap.append(remote(src.at[:, 1 - side], a_core.at[:, part], core_send.at[3, g], core_recv.at[3, g], other))
        copy = pltpu.make_async_copy(src.at[:, side], a_mine.at[:, part], load.at[3, g])
        copy.start()
        a_load.append(copy)

    swap_a(1, a1, a0.shape[2])
    for j, b in enumerate(order):
        for g, src in enumerate((g0, g1, g2)):
            f_core.append(
                remote(src.at[:, 1 - side, b], ff_core.at[b, :, g], core_send.at[g, j], core_recv.at[g, j], other)
            )
            copy = pltpu.make_async_copy(src.at[:, side, b], ff_mine.at[b, :, g], load.at[g, j])
            copy.start()
            f_load.append(copy)
    swap_a(0, a0, 0)
    slot = x_out.shape[2]
    own_x = pltpu.make_async_copy(x_in.at[:, pl.ds(z * slot, slot)], x_out.at[z], local.at[1])
    own_x.start()
    zx = []
    for k in range(1, n_tp):
        peer = lax.rem(z + k, n_tp)
        zx.append(
            remote(x_in.at[:, pl.ds(peer * slot, slot)], x_out.at[z], z_send.at[1, k - 1], z_recv.at[1, k - 1], (d, peer))
        )
    v_out[...] = v_in[...]
    first, second = bit_orders(n_dp)
    for i, step in enumerate([1] + first):
        copy = remote(v_out, v_got.at[i], v_send.at[i], v_recv.at[i], (flip(d, step), z))
        copy.wait()
        v_out[...] += v_got[i]
    v_base = len(first) + 1
    zv = []
    for k in range(1, n_tp):
        peer = lax.rem(z + k, n_tp)
        zv.append(remote(v_out, v_got.at[v_base + k - 1], z_send.at[0, k - 1], z_recv.at[0, k - 1], (d, peer)))
    fill_places(ones, layout, width, n_tp)

    def add_three(dst, src):
        for g in range(3):
            add_rows(dst.at[g], src.at[g])

    ways = ([s // 2 for s in first[::-1]], [s // 2 for s in second[::-1]])
    n_stage = len(ways[0])
    held = layout.total

    def a_ready(i):
        a_load[i].wait()
        a_swap[i].wait_recv()
        src = (a1, a0)[i]
        part = pl.ds(0 if i else a0.shape[2], src.shape[2])
        for e in range(half):
            add_rows(a_mine.at[e, part], a_core.at[e, part])

    def a_group(base, count, at):
        cut = count // 2 // 16 * 16
        return [
            Fold(
                lambda ref, e, lo=lo, size=size: ref.at[e, pl.ds(lo, size)],
                a_mine, a_two, ways[h], own, d, z, h_send.at[at + h], h_recv.at[at + h],
            )
            for h, (lo, size) in enumerate(((base, cut), (base + cut, count - cut)))
        ]

    def start(group):
        for p in group:
            p.start()

    def step(group, add):
        for fold in group:
            fold.finish(add)
            if fold.stage < n_stage:
                fold.start()

    a_ready(0)
    side_folds = a_group(a_rows, rows - a_rows, 2) if mirror else []
    start(side_folds)
    folds = []
    for j, b in enumerate(order):
        for g in range(3):
            f_load[3 * j + g].wait()
            f_core[3 * j + g].wait_recv()
        for i in range(half):
            add_three(ff_mine.at[b, i], ff_core.at[b, i])
        fold = Fold(
            lambda ref, e, b=b: ref.at[b, e], ff_mine, ff_two, ways[j % 2], own, d, z, f_send.at[j], f_recv.at[j]
        )
        fold.start()
        folds.append(fold)
    a_ready(1)
    main_folds = a_group(0, a_rows, 0)
    line_f = LineSum(lambda b: ff_mine.at[b, own], lambda w, b: ff_got.at[w, b], d, z, n_tp, lf_send, lf_recv)
    line_a = LineSum(
        lambda b: a_cols.at[b, pl.ds(0, held)], lambda w, b: a_got.at[w, b, pl.ds(0, held)], d, z, n_tp, la_send, la_recv
    )
    line_b = LineSum(
        lambda b: a_cols.at[b, pl.ds(held, 4 * ch)],
        lambda w, b: a_got.at[w, b, pl.ds(held, 4 * ch)],
        d, z, n_tp, lb_send, lb_recv,
    )

    def pass_on(line, b, add):
        @pl.when(b != z)
        def _():
            line.take(b, add)
            line.give(b)

    for t in range(n_stage - 1):
        step(side_folds, add_rows)
        step(folds, add_three)
        if t == 0:
            start(main_folds)
    if mirror:
        step(side_folds, add_rows)
        k = a1.shape[2] // 4
        for s in range(n_tp):
            place = one_hot(ch, width, lambda r, col, s=s: col - r == s * ch)
            for c in range(4):
                block = a_mine[own, pl.ds(a_rows + c * k, k)]
                a_cols[s, pl.ds(held + c * ch, ch)] = mm_nt(place, block).astype(BF)
        for b in order:
            pass_on(line_b, b, add_rows)
    for fold, b in zip(folds, order):
        fold.finish(add_three)
        pass_on(line_f, b, add_three)
    swaps = []
    if mirror:
        line_b.take(z, add_rows)
        for c in range(4):
            f_own[c] = a_cols[z, pl.ds(held + c * ch, ch)]
        swaps.append(remote(f_own, f_got, f_swap_send.at[0], f_swap_recv.at[0], (n_dp - 1 - d, z)))
        swaps.append(remote(f_own, f_edge, f_swap_send.at[1], f_swap_recv.at[1], (across_of(d, n_dp), z)))
    for t in range(1, n_stage):
        step(main_folds, add_rows)
    line_f.take(z, add_three)
    put = pltpu.make_async_copy(ff_mine.at[z, own], ff_out.at[d], local.at[0])
    put.start()
    put.wait()
    pieces = [(0, 0, vec, first), (1, 0, vec, second)]
    if vec % 32 == 0:
        pieces += [(2, 0, vec // 2, first), (2, vec // 2, vec // 2, second)]
    else:
        pieces += [(2, 0, vec, first)]
    sf = [
        Spread(lambda s, g=g, lo=lo, n=n: ff_out.at[s, g, pl.ds(lo, n)], way + [1], d, z, s_send.at[i], s_recv.at[i])
        for i, (g, lo, n, way) in enumerate(pieces)
    ]
    start(sf)
    step(main_folds, add_rows)
    n_pieces = len(layout.pieces())
    groups = {}
    for i, (packed, low, count, _, _, _) in enumerate(layout.pieces()):
        groups.setdefault((packed, count), []).append((low, i))
    for (packed, count), found in groups.items():
        size = chunk_of(count)

        @pl.loop(0, count // size)
        def _(i, packed=packed, found=found, size=size):
            for s in range(n_tp):
                total = jnp.zeros((size, 128), F32)
                for low, j in found:
                    block = a_mine[own, pl.ds(low + i * size, size)]
                    total += mm_nt(block, ones[s * n_pieces + j])
                a_cols[s, pl.ds(packed + i * size, size)] = total.astype(BF)

    for stage in range(len(first) + 1):
        for p in sf:
            p.wait()
            if stage < len(first):
                p.start()
        if stage == 0:
            for b in order:
                pass_on(line_a, b, add_rows)

    line_a.take(z, add_rows)
    if mirror:
        upper = d > n_dp - 1 - d
        turn_low = one_hot(k, 2 * k, lambda r, col: r + col == 2 * k)
        turn_high = one_hot(k, 2 * k, lambda r, col: r + k + col == 2 * k)
        corner = one_hot(k, 2 * k, lambda r, col: r + col == 0)
        stay_low = one_hot(k, 2 * k, lambda r, col: r == col)
        stay_high = one_hot(k, 2 * k, lambda r, col: r + k == col)
        lane = lax.broadcasted_iota(jnp.int32, (1, 2 * k), 1)
        zero_at = jnp.logical_and(lane == 0, d == 0)
        for copy in swaps:
            copy.wait()
        for c in range(4):
            low, high = jnp.where(upper, f_got[c], f_own[c]), jnp.where(upper, f_own[c], f_got[c])
            plain = mm(low, stay_low) + mm(high, stay_high)
            if c % 2 == 0:
                edge = jnp.where(d == n_dp // 2, f_edge[c + 1], f_edge[c])
                turned = mm(low, turn_low) + mm(high, turn_high) + mm(edge, corner)
            else:
                plain = jnp.where(zero_at, 0.0, plain)
                edge = jnp.where(d == n_dp // 2, 0.0, f_edge[c].astype(F32)).astype(BF)
                turned = -(mm(low, turn_low) + mm(high, turn_high) + mm(edge, corner))
            f_out[c] = jnp.where(upper, turned, plain)
    a_out[...] = a_cols[z, pl.ds(0, layout.total)].astype(F32)
    for copy in zv:
        copy.wait()
    for k in range(1, n_tp):
        v_out[...] += v_got[v_base + k - 1]
    own_x.wait()
    for copy in zx:
        copy.wait_recv()
    for copy in f_core + a_swap + zx:
        copy.wait_send()
    for b in range(n_tp):
        line_f.drain(b)
        line_a.drain(b)
        if mirror:
            line_b.drain(b)
    for p in sf:
        p.drain()


def scatter_grads(ff, a0, a1, vectors, x_in, n_dp, n_tp):
    width = a0.shape[2]
    rows = a0.shape[1] + a1.shape[1]
    vec, hid = ff[0].shape[2:]
    ch = width // n_tp
    k = a1.shape[1] // 4
    mirror = k % 128 == 0
    a_rows = a0.shape[1] if mirror else rows
    held = Pack(a_rows, ch).total
    packed = held + (4 * ch if mirror else 0)
    cut = rows // 2 // 16 * 16
    half = n_dp // 2
    anyspace = pl.BlockSpec(memory_space=pl.ANY)
    vmem = pl.BlockSpec(memory_space=pltpu.VMEM)
    dma = pltpu.SemaphoreType.DMA
    pairs = lambda v: v.reshape((half, 2) + v.shape[1:])
    most = max(4, n_tp, 2)
    return pl.pallas_call(
        functools.partial(scatter_kernel, n_dp, n_tp, cut, mirror),
        out_shape=(
            jax.ShapeDtypeStruct((n_dp, 3, vec, hid), BF),
            jax.ShapeDtypeStruct((held, 128), F32),
            jax.ShapeDtypeStruct((4, ch, 2 * k), F32),
            jax.ShapeDtypeStruct(vectors.shape, F32),
            jax.ShapeDtypeStruct((n_tp, x_in.shape[0], x_in.shape[1] // n_tp, width), BF),
        ),
        in_specs=[anyspace] * 5 + [vmem, anyspace],
        out_specs=(anyspace, vmem, vmem, vmem, anyspace),
        scratch_shapes=[
            pltpu.VMEM((n_tp, half, 3, vec, hid), BF),
            pltpu.VMEM((half, rows, width), BF),
            pltpu.VMEM((n_tp, half, 3, vec, hid), BF),
            pltpu.VMEM((half, rows, width), BF),
            pltpu.VMEM((n_tp, half - 1, 3, vec, hid), BF),
            pltpu.VMEM((half - 1, rows, width), BF),
            pltpu.VMEM((n_tp, packed, 128), BF),
            pltpu.VMEM((2, n_tp, 3, vec, hid), BF),
            pltpu.VMEM((2, n_tp, packed, 128), BF),
            pltpu.VMEM(((half - 1).bit_length() + n_tp,) + vectors.shape, F32),
            pltpu.VMEM((n_tp * len(Pack(a_rows, ch).pieces()), 128, width), BF),
            pltpu.VMEM((4, ch, k), BF),
            pltpu.VMEM((4, ch, k), BF),
            pltpu.VMEM((4, ch, k), BF),
            dma((4, most)),
            dma((4, most)),
            dma((4, most)),
            dma((n_tp, half - 1)),
            dma((n_tp, half - 1)),
            dma((4, half - 1)),
            dma((4, half - 1)),
            dma((2, n_tp)),
            dma((2, n_tp)),
            dma((2, n_tp)),
            dma((2, n_tp)),
            dma((2, n_tp)),
            dma((2, n_tp)),
            dma((2, n_tp - 1)),
            dma((2, n_tp - 1)),
            dma((4, n_dp - 1)),
            dma((4, n_dp - 1)),
            dma(((half - 1).bit_length() + 1,)),
            dma(((half - 1).bit_length() + 1,)),
            dma((2,)),
            dma((2,)),
            dma((2,)),
        ],
        compiler_params=pltpu.CompilerParams(
            collective_id=1, has_side_effects=True, vmem_limit_bytes=60 * 1024 * 1024
        ),
        name="scatter_grads",
    )(*[pairs(g) for g in ff], pairs(a0), pairs(a1), vectors, x_in)


def body(
    tokens,
    lengths,
    cotangent,
    norm1_gain,
    norm1_bias,
    in_weight,
    in_bias,
    filter_base,
    filter_mod,
    out_weight,
    out_bias,
    norm2_gain,
    norm2_bias,
    gate_weight,
    up_weight,
    down_weight,
    down_bias,
):
    micro, local, group, width = tokens.shape
    n_tp = lax.axis_size("tp")
    n_dp = lax.axis_size("dp")
    z = lax.axis_index("tp")
    d = lax.axis_index("dp")
    slot_len = local * n_tp
    own = micro * group // n_tp
    per_micro = min(group, own)
    ch = in_weight.shape[2]
    vec = width // n_dp
    hid = gate_weight.shape[1]
    table = jnp.asarray(packed_table(slot_len))
    scale = 0.5 / slot_len

    rows = slot_len // n_dp
    last = n_dp - 1
    upper = d > last - d
    mirror = rows % 128 == 0
    filters = jnp.stack([filter_base, filter_mod])
    across = [(i, (n_dp - i) % n_dp) for i in range(n_dp) if i % (n_dp // 2)] + [(0, n_dp // 2), (n_dp // 2, 0)]
    if not mirror:
        got = lax.ppermute(filters[:, :, rows:], "dp", [(i, last - i) for i in range(n_dp)])
        got_edge = lax.ppermute(filters[:, :, :1], "dp", across)
        direct = jnp.where(upper, got, filters[:, :, :rows]).astype(F32)
        mirror_lower = jnp.concatenate([got[:, :, 1:], got_edge], axis=2)
        mirror_upper = filters[:, :, 1 : rows + 1]
        image = jnp.flip(jnp.where(upper, mirror_upper, mirror_lower), 2).astype(F32)
        nyquist = got_edge[:, 0, 0].astype(F32)
        edge = ((jnp.arange(rows) == 0) & (d == 0))[None, :, None]
        half_real = jnp.where(edge, direct[:, 0], direct[:, 0] + image[:, 0])
        half_imag = jnp.where(edge, nyquist[:, None], direct[:, 1] - image[:, 1])
        half = jnp.stack([half_real, half_imag], 1).astype(BF).reshape(4 * rows, ch)

    slice_of = [2 * i if 2 * i < n_dp else 2 * (last - i) + 1 for i in range(n_dp)]

    a_in = [in_weight.transpose(1, 0, 2).reshape(3 * vec, ch), out_weight.T] + ([] if mirror else [half])
    a_in = jnp.concatenate(a_in)
    f_in = filters.transpose(0, 1, 3, 2).reshape(4, ch, 2 * rows)
    vectors = jnp.stack([norm1_gain, norm1_bias, norm2_gain, norm2_bias, out_bias, down_bias])
    vectors = jnp.concatenate([vectors, in_bias])
    vectors = jnp.pad(vectors, ((0, 16 - 9), (0, width - vec)))
    share = hid // n_dp
    ff = [w.reshape(n_dp, vec, hid) for w in (gate_weight, up_weight, down_weight)]
    x_in = tokens.transpose(0, 2, 1, 3).reshape(n_tp, own, local, width)
    layout = Pack(a_in.shape[0], ch)
    ffw, aw, x_own = gather_weights(ff, layout.pack(a_in), a_in.shape[0], f_in, vectors, x_in, n_dp, n_tp)
    cotangent, _ = lax.optimization_barrier((cotangent, aw))
    vectors = aw[:, 4 * vec + 4 * rows :, :vec].astype(F32).transpose(1, 0, 2).reshape(16, width)
    slots = [slice_of.index(k) for k in range(n_dp)]
    direct = vec % 16 == 0 and hid == width
    if direct:
        ws = [
            (ffw, (n_dp, n_tp, None, vec, hid), (0, 0, g, 0, 0), (n_dp, 1, None, vec, hid), lambda p, g=g: (0, p, g, 0, 0))
            for g in range(3)
        ]
        a_view = aw
    else:
        natural = [ffw[:, :, g].transpose(1, 0, 2, 3).reshape(n_tp, width, hid) for g in range(2)]
        natural.append(ffw[:, :, 2].reshape(n_dp, n_tp, share, width).transpose(1, 0, 2, 3).reshape(n_tp, hid, width))
        ws = [
            (w[None], (1,) + w.shape, (0, 0, 0, 0), (1, 1) + w.shape[1:], lambda p: (0, p, 0, 0)) for w in natural
        ]
        a_view = aw[:, : 4 * vec].reshape(n_dp, 4, vec, width).transpose(1, 0, 2, 3).reshape(1, 4 * width, width)

    def to_owner(x):
        pieces = x.transpose(0, 2, 1, 3).reshape(n_tp, own, local, width)
        return lax.all_to_all(pieces, "tp", 0, 1, tiled=False).reshape(own, slot_len, width)

    def to_slots(x):
        whole = lax.all_to_all(x.reshape(n_tp, own * local, width), "tp", 0, 0, tiled=False)
        return whole.reshape(micro, group, local, width).transpose(0, 2, 1, 3)

    c_own = to_owner(cotangent)
    flat_len = lax.dynamic_slice_in_dim(lengths.reshape(-1), z * own, own, 0)
    first = 4 * vec // rows
    gating, nsum, mixing, spec, conv, gated = mix(x_own, flat_len, a_view, vectors, table, aw, first, rows, slots, scale)
    middle, n2, act, side, hidden, out = feed(x_own, gated, flat_len, a_view, ws, n_tp, hid, vectors)
    layer_out = to_slots(out)
    e, *d_ff = feed_back(c_own, n2, act, side, hidden, flat_len, ws)
    mg, cg, gtg, d_out, sums = branch_back(e, middle, c_own, gating, conv, flat_len, a_view, vectors)
    layer_out, cg = lax.optimization_barrier((layer_out, cg))
    vg, d_filter, cgv = spectral_back(cg, spec, mixing, flat_len, table, aw, first, rows, slots, scale)
    ig, d_first, sums = input_back(vg, gtg, x_own, mg, nsum, cgv, flat_len, a_view, d_out, sums, vectors)
    if not direct:
        d_ff = [
            g[0].reshape(n_tp, n_dp, vec, hid).transpose(1, 0, 2, 3) for g in d_ff[:2]
        ] + [d_ff[2][0].reshape(n_tp, n_dp, vec, hid).transpose(1, 0, 2, 3)]
        d_first = d_first.reshape(4, n_dp, vec, width).transpose(1, 0, 2, 3).reshape(n_dp, 4 * vec, width)
    ffg, ag, full, vecs, input_grad = scatter_grads(d_ff, d_first, d_filter, sums, ig, n_dp, n_tp)
    input_grad = input_grad.reshape(micro, group, local, width).transpose(0, 2, 1, 3)
    ag = layout.unpack(ag)
    gate_grad = ffg[:, 0].reshape(width, hid).astype(F32)
    up_grad = ffg[:, 1].reshape(width, hid).astype(F32)
    down_grad = ffg[:, 2].reshape(hid, width).astype(F32)
    in_grad = ag[: 3 * vec].reshape(3, vec, ch).transpose(1, 0, 2)
    out_grad = ag[3 * vec : 4 * vec].T
    if mirror:
        full = full.reshape(2, 2, ch, 2 * rows).transpose(0, 1, 3, 2)
    else:
        fgrad = ag[4 * vec :].astype(BF).reshape(2, 2, rows, ch)
        other = lax.ppermute(fgrad, "dp", [(i, last - i) for i in range(n_dp)])
        low_slice = jnp.where(upper, other, fgrad)
        high_slice = jnp.where(upper, fgrad, other)
        both = jnp.concatenate([low_slice, high_slice], axis=2)
        follow = lax.ppermute(fgrad[:, :, :1], "dp", across)
        zero = jnp.zeros_like(follow[:, 0])
        follow = jnp.where(d == n_dp // 2, jnp.stack([follow[:, 1], zero], 1), follow)
        mirrored = jnp.flip(jnp.concatenate([both[:, :, 1:], follow], axis=2), 2)
        mirrored = jnp.stack([mirrored[:, 0], -mirrored[:, 1]], 1)
        plain = jnp.stack(
            [both[:, 0], jnp.where((d == 0) & (jnp.arange(2 * rows) == 0)[None, :, None], 0.0, both[:, 1].astype(F32)).astype(BF)], 1
        )
        full = jnp.where(upper, mirrored, plain).astype(F32)
    piece = width // (n_dp * n_tp)
    vecs = lax.dynamic_slice_in_dim(vecs, (d * n_tp + z) * piece, piece, 1)
    return (
        layer_out,
        input_grad,
        vecs[0],
        vecs[1],
        in_grad,
        vecs[6:9],
        full[0],
        full[1],
        out_grad,
        vecs[4],
        vecs[2],
        vecs[3],
        gate_grad,
        up_grad,
        down_grad,
        vecs[5],
    )


def solution(mesh):
    in_specs = (
        P(None, "tp", "dp", None),
        P(None, "dp"),
        P(None, "tp", "dp", None),
        P("dp"),
        P("dp"),
        P("dp", None, "tp"),
        P(None, "dp"),
        P(None, "dp", "tp"),
        P(None, "dp", "tp"),
        P("tp", "dp"),
        P("dp"),
        P("dp"),
        P("dp"),
        P(None, "tp"),
        P(None, "tp"),
        P("tp", None),
        P("dp"),
    )
    out_specs = (
        P(None, "tp", "dp", None),
        P(None, "tp", "dp", None),
        P(("dp", "tp")),
        P(("dp", "tp")),
        P("dp", None, "tp"),
        P(None, ("dp", "tp")),
        P(None, "dp", "tp"),
        P(None, "dp", "tp"),
        P("tp", "dp"),
        P(("dp", "tp")),
        P(("dp", "tp")),
        P(("dp", "tp")),
        P(None, "tp"),
        P(None, "tp"),
        P("tp", None),
        P(("dp", "tp")),
    )
    return jax.shard_map(body, mesh=mesh, in_specs=in_specs, out_specs=out_specs, check_vma=False)
```
